128 devices in a mesh: cin: 8 (over x_lo, y), flt: 16 (over z, x_hi, core).
Axes of the slice: x: 4 (x_hi: 2, x_lo: 2; x = x_hi * 2 + x_lo), y: 4, z: 4, core: 2. Of those that a mesh axis runs over, the one named last changes fastest.
Arguments:
- volume: bfloat16 [4, 64, 128, 256], P(None, 'cin', 'flt'), may hold values from -6 to 6
- early_w: bfloat16 [16, 4, 3, 3, 3], replicated, may hold values from -0.625 to 0.625
- deep_w: bfloat16 [256, 256, 3, 3, 3], P('flt', 'cin'), may hold values from -0.078125 to 0.078125
- d_out: bfloat16 [256, 8, 16, 128], P('flt', 'cin'), may hold values from -0.03125 to 0.03125
Outputs:
- deep_out: bfloat16 [256, 8, 16, 128], P('flt', 'cin')
- grad_deep_w: float32 [256, 256, 3, 3, 3], P('flt', 'cin')
- grad_early_w: float32 [16, 4, 3, 3, 3], replicated
The draws below stay inside these ranges and needn't reach their ends.
All inputs are finite; a program needn't handle non-finite values.
Results may differ from the reference program's by a relative error of at most 0.005.
Values may be sent and summed in bfloat16 or wider, within the bound.
A program may use at most 128 MiB of HBM per device.

```python
import jax
import jax.numpy as jnp
from jax import lax

IN_CH = 4
EARLY_CH = 16
FILT = 256
Z = 256
CH = 256
NX = 64
NY = 128
DX = 8
DY = 16
DZ = 128


def with_spikes(result, own_key, source, target, shards_of, factor):
    def block_of(position):
        return (jnp.arange(result.shape[position]) // (result.shape[position] // shards_of)).reshape((-1,) + (1,) * (result.ndim - 1 - position))

    one_side = jax.random.permutation(own_key, shards_of)[block_of(target)]
    far = (block_of(target) + shards_of // 2) % shards_of
    return jnp.where((block_of(source) == one_side) | (block_of(source) == far), factor * result, result)


def shard_levels(key, extent, cuts, low, high):
    level, own = 1.0, jax.random.fold_in(key, 6)
    for axis_at, blocks in cuts:
        heights = jnp.exp(jax.random.uniform(jax.random.fold_in(own, axis_at), (blocks,), jnp.float32, low / len(cuts), high / len(cuts)))
        level = level * jnp.repeat(heights, extent[axis_at] // blocks).reshape([-1 if axis == axis_at else 1 for axis in range(len(extent))])
    return level


def scatter_about(stream_key, dims, deviation, bound, cuts=(), dtype=jnp.bfloat16):
    values = jax.random.normal(stream_key, dims, jnp.float32) * deviation
    if len(cuts) > 0:
        values = shard_levels(stream_key, dims, cuts, -0.22, 0.18) * values
    return jnp.clip(values, min=-bound, max=bound).astype(dtype)


def bell_draw_with(key, shape, scale, limit, split, heavy, kind=jnp.bfloat16):
    entries = scale * jax.random.normal(key, shape, jnp.float32)
    if split:
        entries = entries * shard_levels(key, shape, split, -0.22, 0.18)
    return jnp.clip(with_spikes(entries, jax.random.fold_in(key, 3), *heavy), -limit, limit).astype(kind)


def setup_inputs(seed: int = 0) -> dict:
    key_of = jax.random.split(jax.random.key(seed), 5)
    return {
        "volume": scatter_about(key_of[0], (IN_CH, NX, NY, Z), 1.0, 6.0, ((1, 8), (2, 16))),
        "early_w": scatter_about(key_of[1], (EARLY_CH, IN_CH, 3, 3, 3), (IN_CH * 27) ** -0.5, 0.625),
        "deep_w": scatter_about(key_of[2], (FILT, CH, 3, 3, 3), (CH * 27) ** -0.5, 0.078125, ((0, 16), (1, 8))),
        "d_out": bell_draw_with(key_of[3], (FILT, DX, DY, DZ), (1.0 / 256), 0.03125, ((0, 16), (1, 8)), (0, 2, 16, 2.0)),
    }


slope = 0.3
all_sides = ((1, 1), (1, 1), (1, 1))

def convolve(source, kernel, padding):
    return lax.conv_general_dilated(source[None], kernel, (1, 1, 1), padding, dimension_numbers=('NCDHW', 'OIDHW', 'NCDHW'), preferred_element_type=jnp.float32)[0]

def flipped(kernel):
    return jnp.flip(kernel, (2, 3, 4)).transpose(1, 0, 2, 3, 4)

def kernel_grad(source, cotangent):
    padded = jnp.pad(source, ((0, 0), (1, 1), (1, 1), (1, 1)))
    along_x, along_y, along_z = cotangent.shape[1:]
    flat_grad = cotangent.reshape(cotangent.shape[0], -1)
    blocks = []
    for shift_x in range(3):
        for shift_y in range(3):
            for shift_z in range(3):
                window = padded[:, shift_x:shift_x + along_x, shift_y:shift_y + along_y, shift_z:shift_z + along_z]
                window = window.reshape(source.shape[0], -1)
                blocks.append(lax.dot_general(flat_grad, window, (((1,), (1,)), ((), ())), preferred_element_type=jnp.float32))
    return jnp.stack(blocks, -1).reshape(cotangent.shape[0], source.shape[0], 3, 3, 3)

def pool_cells(field):
    channels, along_x, along_y, along_z = field.shape
    return field.reshape(channels, along_x // 2, 2, along_y // 2, 2, along_z // 2, 2).mean((2, 4, 6))

def to_depth(field):
    channels, along_x, along_y, along_z = field.shape
    moved = field.reshape(channels, along_x // 4, 4, along_y // 4, 4, along_z).transpose(0, 2, 4, 1, 3, 5)
    return moved.reshape(channels * 16, along_x // 4, along_y // 4, along_z)

def from_depth(field, channels):
    wide, along_x, along_y, along_z = field.shape
    moved = field.reshape(channels, 4, 4, along_x, along_y, along_z).transpose(0, 3, 1, 4, 2, 5)
    return moved.reshape(channels, along_x * 4, along_y * 4, along_z)

def spread_back(field):
    channels, along_x, along_y, along_z = field.shape
    scaled = field / 8.0
    spread = jnp.broadcast_to(scaled[:, :, None, :, None, :, None], (channels, along_x, 2, along_y, 2, along_z, 2))
    return spread.reshape(channels, along_x * 2, along_y * 2, along_z * 2)

def reference(volume, early_w, deep_w, d_out):
    early_pre = convolve(volume, early_w, all_sides)
    early_act = jnp.where(early_pre > 0, early_pre, slope * early_pre)
    deep_in = to_depth(pool_cells(early_act)).astype(jnp.bfloat16)
    deep_out = convolve(deep_in, deep_w, all_sides).astype(jnp.bfloat16)
    grad_deep_w = kernel_grad(deep_in, d_out)
    input_grad = convolve(d_out, flipped(deep_w), all_sides).astype(jnp.bfloat16)
    upward = spread_back(from_depth(input_grad.astype(jnp.float32), early_pre.shape[0]))
    early_grad = (upward * jnp.where(early_pre > 0, 1.0, slope)).astype(jnp.bfloat16)
    grad_early_w = kernel_grad(volume, early_grad)
    return (deep_out, grad_deep_w, grad_early_w)
```

```python
import jax
import jax.numpy as jnp
import ml_dtypes
import numpy as np
from jax import lax
from jax.experimental import pallas as pl
from jax.experimental.pallas import tpu as pltpu
from jax.sharding import PartitionSpec as P

MESH = pl.DeviceIdType.MESH
F32, BF16 = jnp.float32, jnp.bfloat16
slope = 0.3
NC, NF = 8, 16

PIECES = (
    (0, 32, 1, 0), (32, 32, -1, 0), (64, 32, 0, 1), (96, 32, 0, -1),
    (128, 16, 1, 1), (144, 16, 1, -1), (160, 16, -1, 1), (176, 16, -1, -1),
)
Q0, PERM0, UP0, SWAP0, EYE0, PAIR0, END0 = 0, 192, 448, 960, 1216, 1472, 1600


def tables():
    sel = np.zeros((END0, 256), np.float32)
    for i in range(4):
        for y in range(8):
            sel[Q0 + i * 8 + y, i * 64 + 56 + y] = 1
            sel[Q0 + 32 + i * 8 + y, i * 64 + y] = 1
        for x in range(8):
            sel[Q0 + 64 + x * 4 + i, i * 64 + x * 8 + 7] = 1
            sel[Q0 + 96 + x * 4 + i, i * 64 + x * 8] = 1
        sel[Q0 + 128 + i, i * 64 + 63] = 1
        sel[Q0 + 144 + i, i * 64 + 56] = 1
        sel[Q0 + 160 + i, i * 64 + 7] = 1
        sel[Q0 + 176 + i, i * 64] = 1
    for a in range(4):
        for e in range(16):
            for b in range(4):
                sel[PERM0 + 16 * e + 4 * a + b, a * 64 + b * 16 + e] = 1
            for y in range(8):
                sel[UP0 + a * 128 + y * 16 + e, 16 * e + 4 * a + y // 2] = 1
    for v in range(16):
        for o in range(16):
            sel[SWAP0 + v * 16 + o, o * 16 + v] = 1
    sel[EYE0 : EYE0 + 256] = np.eye(256)
    for z in range(256):
        sel[PAIR0 + z // 2, z] = 1

    slab = np.zeros((480, 512), np.float32)
    for xs in range(10):
        x = xs - 1
        for i in range(4):
            for y in range(8):
                column = i * 64 + x * 8 + y if 0 <= x < 8 else 256 + (32 if x == 8 else 0) + i * 8 + y
                slab[xs * 48 + i * 8 + y, column] = 1
            low, high = (320 + x * 4, 352 + x * 4) if 0 <= x < 8 else ((384, 400) if x < 0 else (416, 432))
            slab[xs * 48 + 32 + i, low + i] = 1
            slab[xs * 48 + 36 + i, high + i] = 1

    taps = np.zeros((128, 8 * 512), np.float32)
    for y in range(8):
        for a in range(3):
            for b in range(3):
                for c in range(3):
                    for i in range(4):
                        row = y + b - 1
                        k = 32 + i if row < 0 else 36 + i if row > 7 else i * 8 + row
                        taps[(a * 9 + b * 3 + c) * 4 + i, y * 512 + a * 144 + c * 48 + k] = 1

    band = np.zeros((96, 8 * 256), np.float32)
    for u in range(8):
        for a in range(3):
            if 0 <= u + a - 1 < 8:
                for i in range(32):
                    band[a * 32 + i, u * 256 + (u + a - 1) * 32 + i] = 1
    return [t.astype(ml_dtypes.bfloat16) for t in (sel, slab, taps, band)]


def dot(a, b):
    return jnp.dot(a, b, preferred_element_type=F32)


def dot_t(a, b):
    return lax.dot_general(a, b, (((1,), (1,)), ((), ())), preferred_element_type=F32)


def moved(value, step):
    width = value.shape[1]
    lane = lax.broadcasted_iota(jnp.int32, value.shape, 1)
    edge = 0 if step > 0 else width - 1
    return jnp.where(lane == edge, 0.0, pltpu.roll(value, step % width, 1))


def kernel(
    vol, wet, wdt, dout, sel, slab, taps, band,
    deep_out, grad_deep, grad_early,
    sb, halo, vs, te, fac, pooled, dl, xx, down, g, gs, tdt, td, tw, r, rr, po, ro, igl, igr, up, ae, acc, ar1, ar2,
    halo_s, halo_r, g_s, g_r, dl_s, dl_r, xx_s, xx_r, rr_s, rr_r, ro_s, ro_r, ig_s, ig_r, a1_s, a1_r, a2_s, a2_r,
):
    c, f = lax.axis_index("cin"), lax.axis_index("flt")

    def remote(src, dst, send, recv, to_c, to_f):
        return pltpu.make_async_remote_copy(
            src_ref=src, dst_ref=dst, send_sem=send, recv_sem=recv,
            device_id=(to_c, to_f), device_id_type=MESH,
        )

    def exists(piece, sign):
        to_c, to_f = c + sign * piece[2], f + sign * piece[3]
        return (to_c >= 0) & (to_c < NC) & (to_f >= 0) & (to_f < NF)

    def halo_copy(j):
        first, rows, dc, df = PIECES[j]
        at = pl.ds(first, rows)
        return remote(sb.at[at], halo.at[at], halo_s.at[j], halo_r.at[j], c + dc, f + df)

    def g_copy(to, of):
        return remote(down, g.at[:, of], g_s.at[to], g_r.at[of], to, f)

    def dl_copy(to, of):
        return remote(dl.at[to], xx.at[1 + f, of], dl_s.at[to], dl_r.at[of], to, f)

    def xx_copy(to, of):
        return remote(xx.at[1 + of], xx.at[1 + of], xx_s.at[to], xx_r.at[of], c, to)

    def rr_copy(to, of):
        return remote(r.at[to], rr.at[of], rr_s.at[to], rr_r.at[of], c, to)

    def ro_copy(to, of):
        return remote(po.at[to], ro.at[of], ro_s.at[to], ro_r.at[of], to, f)

    def ig_copy(to, of):
        return remote(igl.at[to], igr.at[of], ig_s.at[to], ig_r.at[of], to, f)

    def a1_copy(to, of):
        return remote(ar1.at[of], ar1.at[of], a1_s.at[to], a1_r.at[of], to, f)

    def a2_copy(to, of):
        return remote(ar2.at[of], ar2.at[of], a2_s.at[to], a2_r.at[of], c, to)

    def each(count, me, act):
        @pl.loop(1, count)
        def _(k):
            act(lax.rem(me + k, count))

    def send(count, me, copy):
        each(count, me, lambda to: copy(to, me).start())

    def receive(count, me, copy):
        each(count, me, lambda of: copy(of, of).wait_recv())

    def sent(count, me, copy):
        each(count, me, lambda to: copy(to, me).wait_send())

    halo[...] = jnp.zeros_like(halo)

    barrier = pltpu.get_barrier_semaphore()

    def greet(to_c, to_f):
        pl.semaphore_signal(barrier, inc=1, device_id=(to_c, to_f), device_id_type=MESH)

    each(NC, c, lambda to: greet(to, f))
    each(NF, f, lambda to: greet(c, to))
    expected = NC + NF - 2
    for piece in PIECES[4:]:
        there = exists(piece, 1)

        @pl.when(there)
        def _(piece=piece):
            greet(c + piece[2], f + piece[3])

        expected = expected + there.astype(jnp.int32)

    sb[...] = dot(sel[Q0:PERM0], vol[...]).astype(BF16)
    swapped = dot(sel[SWAP0:EYE0], dout[...]).astype(BF16).reshape(16, 16, 128)
    down[...] = swapped
    g[:, pl.ds(c, 1)] = swapped[:, None]
    xx[0] = jnp.zeros(xx.shape[1:], BF16)
    xx[17] = jnp.zeros(xx.shape[1:], BF16)
    for k in range(3):
        gs[k, 0] = jnp.zeros(gs.shape[2:], BF16)
        gs[k, 17] = jnp.zeros(gs.shape[2:], BF16)

    pl.semaphore_wait(barrier, expected)
    for j, piece in enumerate(PIECES):

        @pl.when(exists(piece, 1))
        def _(j=j):
            halo_copy(j).start()

    send(NC, c, g_copy)

    early = dot_t(sel[EYE0 : EYE0 + 16, :16], wet[...]).astype(BF16)
    for y in range(8):
        te[y * 16 : (y + 1) * 16, :] = dot(early, taps[:, y * 512 : (y + 1) * 512]).astype(BF16)

    for j, piece in enumerate(PIECES):

        @pl.when(exists(piece, -1))
        def _(j=j):
            halo_copy(j).wait_recv()

    cells = dot(slab[:, :256], vol[...]) + dot(slab[:, 256:448], halo[...])
    for k, shifted in enumerate((moved(cells, 1), cells, moved(cells, -1))):
        shifted = shifted.astype(BF16)
        for xs in range(10):
            vs[xs * 144 + k * 48 : xs * 144 + k * 48 + 48, :] = shifted[xs * 48 : xs * 48 + 48]
    vs[1440:1584, :] = jnp.zeros((144, 256), BF16)

    @pl.loop(0, 4)
    def _(a):
        total = jnp.zeros((128, 256), F32)
        for x in range(2):
            at = pl.multiple_of((2 * a + x) * 144, 16)
            pre = dot(te[...], vs[pl.ds(at, 512), :])
            factor = jnp.where(pre > 0, 1.0, slope)
            fac[2 * a + x] = factor
            total += pre * factor
        for b in range(4):
            pooled[a, b * 16 : b * 16 + 16] = (
                total[b * 32 : b * 32 + 16] + total[b * 32 + 16 : b * 32 + 32]
            )

    pair = sel[PAIR0:END0]
    field = pooled[...].reshape(256, 256)
    high = field.astype(BF16)
    low = (field - high.astype(F32)).astype(BF16)
    means = ((dot_t(high, pair) + dot_t(low, pair)) * 0.125).astype(BF16)
    local = dot(sel[PERM0:UP0], means).astype(BF16).reshape(8, 32, 128)
    dl[...] = local
    send(NC, c, dl_copy)
    xx[1 + f, c] = dl[c]

    for u in range(8):
        columns = slice(u * 256, (u + 1) * 256)
        wide = dot(wdt[0:144], band[0:32, columns])
        wide += dot(wdt[144:288], band[32:64, columns])
        wide += dot(wdt[288:432], band[64:96, columns])
        wide = wide.astype(BF16)
        for b in range(3):
            for k in range(3):
                block = wide[(b * 3 + k) * 16 : (b * 3 + k) * 16 + 16]
                tw[k, u * 16 : u * 16 + 16, b * 256 : (b + 1) * 256] = block
                tdt[k, (2 - b) * 128 + u * 16 : (2 - b) * 128 + u * 16 + 16] = block
    for k in range(3):
        td[k] = dot_t(sel[EYE0:PAIR0], tdt[k]).astype(BF16)

    receive(NC, c, dl_copy)
    send(NF, f, xx_copy)

    receive(NC, c, g_copy)

    @pl.loop(0, 16)
    def _(v):
        plain = g[v].reshape(128, 128)
        wide = plain.astype(F32)
        gs[0, v + 1] = moved(wide, -1).astype(BF16)
        gs[1, v + 1] = plain
        gs[2, v + 1] = moved(wide, 1).astype(BF16)

    @pl.loop(0, 8)
    def _(k):
        v = 2 * lax.rem(f // 2 + 1 + k, 8)
        out = jnp.zeros((256, 256), F32)
        for t in range(3):
            both = jnp.concatenate(
                [gs[t, pl.ds(v, 3)].reshape(384, 128), gs[t, pl.ds(v + 1, 3)].reshape(384, 128)], 1
            )
            out += dot(td[t], both)
        out = out.astype(BF16)
        for h in range(2):
            r[v + h] = out[:, h * 128 : (h + 1) * 128]

            @pl.when(v + h != f)
            def _():
                rr_copy(v + h, f).start()

            @pl.when(v + h == f)
            def _():
                rr[f] = out[:, h * 128 : (h + 1) * 128]

    receive(NF, f, xx_copy)

    def pair_of_rows(v):
        return jnp.concatenate(
            [xx[pl.ds(v, 3)].reshape(768, 128), xx[pl.ds(v + 1, 3)].reshape(768, 128)], 1
        )

    @pl.loop(0, 8)
    def _(k):
        v = 2 * k
        out = dot(tw[...].reshape(384, 768), pair_of_rows(v))
        for h in range(2):
            half = out[:, h * 128 : (h + 1) * 128]
            total = moved(half[:128], 1) + half[128:256] + moved(half[256:], -1)
            po[:, v + h] = total.astype(BF16).reshape(8, 16, 128)

    send(NC, c, ro_copy)
    ro[c] = po[c]

    receive(NF, f, rr_copy)
    total = rr[0].astype(F32)
    for k in range(1, NF):
        total += rr[k].astype(F32)
    igl[...] = total.astype(BF16).reshape(8, 32, 128)
    send(NC, c, ig_copy)
    igr[c] = igl[c]

    acc[...] = jnp.zeros_like(acc)

    @pl.loop(0, 8)
    def _(k):
        v = 2 * k
        both = jnp.concatenate(
            [gs[:, v + 1].reshape(384, 128), gs[:, v + 2].reshape(384, 128)], 1
        )
        acc[...] += dot_t(both, pair_of_rows(v))

    receive(NC, c, ig_copy)
    spread = dot(sel[UP0:SWAP0], igr[...].reshape(256, 128)).astype(BF16)
    up[...] = (dot(spread, pair) * 0.125).reshape(4, 128, 256)
    ae[...] = jnp.zeros_like(ae)

    @pl.loop(0, 4)
    def _(a):
        for x in range(2):
            at = pl.multiple_of((2 * a + x) * 144, 16)
            grad = (up[a] * fac[2 * a + x]).astype(BF16)
            ae[...] += dot_t(grad, vs[pl.ds(at, 512), :])

    rest = jnp.concatenate([ae[y * 16 : (y + 1) * 16] for y in range(8)], 1)
    mine = jnp.zeros((16, 128), F32)
    for _ in range(3):
        piece = rest.astype(BF16)
        mine += dot_t(piece, taps[...])
        rest = rest - piece.astype(F32)
    ar1[c] = mine
    send(NC, c, a1_copy)

    receive(NC, c, ro_copy)
    total = ro[0].astype(F32)
    for k in range(1, NC):
        total += ro[k].astype(F32)
    rounded = total.astype(BF16).reshape(256, 128)
    deep_out[...] = dot(sel[SWAP0:EYE0], rounded).astype(BF16)

    receive(NC, c, a1_copy)
    total = ar1[0]
    for k in range(1, NC):
        total += ar1[k]
    ar2[f] = total
    send(NF, f, a2_copy)

    lane = lax.broadcasted_iota(jnp.int32, (16, 256), 1)
    for k in range(3):
        for b in range(3):
            total = jnp.zeros((16, 256), F32)
            for u in range(8):
                rows = acc[k * 128 + u * 16 : k * 128 + u * 16 + 16, b * 256 : (b + 1) * 256]
                rows = pltpu.roll(rows, (-(u - 1) * 32) % 256, 1) if u != 1 else rows
                if u == 0:
                    rows = jnp.where(lane < 32, 0.0, rows)
                if u == 7:
                    rows = jnp.where(lane >= 64, 0.0, rows)
                total += rows
            for a in range(3):
                at = ((a * 3 + b) * 3 + k) * 16
                grad_deep[at : at + 16, :] = total[:, a * 32 : (a + 1) * 32]

    receive(NF, f, a2_copy)
    total = ar2[0]
    for k in range(1, NF):
        total += ar2[k]
    square = jnp.concatenate([total, jnp.zeros((112, 128), F32)], 0)
    grad_early[...] = square.T[:, :16]

    for j, piece in enumerate(PIECES):

        @pl.when(exists(piece, 1))
        def _(j=j):
            halo_copy(j).wait_send()

    sent(NC, c, g_copy)
    sent(NC, c, dl_copy)
    sent(NF, f, xx_copy)
    sent(NF, f, rr_copy)
    sent(NC, c, ro_copy)
    sent(NC, c, ig_copy)
    sent(NC, c, a1_copy)
    sent(NF, f, a2_copy)


SCRATCH = (
    ((192, 256), BF16), ((192, 256), BF16), ((1584, 256), BF16), ((128, 512), BF16),
    ((8, 128, 256), F32), ((4, 64, 256), F32), ((8, 32, 128), BF16), ((18, 8, 32, 128), BF16),
    ((16, 16, 128), BF16), ((16, 8, 16, 128), BF16), ((3, 18, 128, 128), BF16), ((3, 384, 256), BF16),
    ((3, 256, 384), BF16), ((3, 128, 768), BF16), ((16, 256, 128), BF16), ((16, 256, 128), BF16),
    ((8, 16, 16, 128), BF16), ((8, 16, 16, 128), BF16), ((8, 32, 128), BF16), ((8, 32, 128), BF16),
    ((4, 128, 256), F32), ((128, 512), F32), ((384, 768), F32), ((8, 16, 128), F32), ((16, 16, 128), F32),
)
SEMAPHORES = (8, 8, 8, 8, 8, 8, 16, 16, 16, 16, 8, 8, 8, 8, 8, 8, 16, 16)


def local(volume, early_w, deep_w, d_out):
    early = early_w.transpose(2, 3, 4, 1, 0).reshape(108, 16)
    operands = [
        volume.reshape(256, 256),
        jnp.pad(early, ((0, 20), (0, 0))),
        deep_w.transpose(2, 3, 4, 0, 1).reshape(432, 32),
        d_out.reshape(256, 128),
        *[jnp.asarray(t) for t in tables()],
    ]
    deep_out, grad_deep, grad_early = pl.pallas_call(
        kernel,
        out_shape=(
            jax.ShapeDtypeStruct((256, 128), BF16),
            jax.ShapeDtypeStruct((432, 32), F32),
            jax.ShapeDtypeStruct((128, 16), F32),
        ),
        in_specs=[pl.BlockSpec(memory_space=pltpu.VMEM)] * len(operands),
        out_specs=[pl.BlockSpec(memory_space=pltpu.VMEM)] * 3,
        scratch_shapes=[pltpu.VMEM(shape, dtype) for shape, dtype in SCRATCH]
        + [pltpu.SemaphoreType.DMA((count,)) for count in SEMAPHORES],
        compiler_params=pltpu.CompilerParams(
            collective_id=0, has_side_effects=True, vmem_limit_bytes=44 << 20
        ),
        name="cosmo",
    )(*operands)
    return (
        deep_out.reshape(16, 1, 16, 128),
        grad_deep.reshape(3, 3, 3, 16, 32).transpose(3, 4, 0, 1, 2),
        grad_early[:108].reshape(3, 3, 3, 4, 16).transpose(4, 3, 0, 1, 2),
    )


def solution(mesh):
    in_specs = (
        P(None, "cin", "flt", None),
        P(),
        P("flt", "cin", None, None, None),
        P("flt", "cin", None, None),
    )
    out_specs = (P("flt", "cin", None, None), P("flt", "cin", None, None, None), P())
    return jax.shard_map(local, mesh=mesh, in_specs=in_specs, out_specs=out_specs, check_vma=False)
```

```python
import jax
import jax.numpy as jnp
import ml_dtypes
import numpy as np
from jax import lax
from jax.experimental import pallas as pl
from jax.experimental.pallas import tpu as pltpu
from jax.sharding import PartitionSpec as P

MESH = pl.DeviceIdType.MESH
F32, BF16 = jnp.float32, jnp.bfloat16
slope = 0.3
NC, NF = 8, 16

PIECES = (
    (0, 32, 1, 0), (32, 32, -1, 0), (64, 32, 0, 1), (96, 32, 0, -1),
    (128, 16, 1, 1), (144, 16, 1, -1), (160, 16, -1, 1), (176, 16, -1, -1),
)
Q0, PERM0, UP0, SWAP0, EYE0, PAIR0, END0 = 0, 192, 448, 960, 1216, 1472, 1600


def tables():
    sel = np.zeros((END0, 256), np.float32)
    for i in range(4):
        for y in range(8):
            sel[Q0 + i * 8 + y, i * 64 + 56 + y] = 1
            sel[Q0 + 32 + i * 8 + y, i * 64 + y] = 1
        for x in range(8):
            sel[Q0 + 64 + x * 4 + i, i * 64 + x * 8 + 7] = 1
            sel[Q0 + 96 + x * 4 + i, i * 64 + x * 8] = 1
        sel[Q0 + 128 + i, i * 64 + 63] = 1
        sel[Q0 + 144 + i, i * 64 + 56] = 1
        sel[Q0 + 160 + i, i * 64 + 7] = 1
        sel[Q0 + 176 + i, i * 64] = 1
    for a in range(4):
        for e in range(16):
            for b in range(4):
                sel[PERM0 + 16 * e + 4 * a + b, a * 64 + b * 16 + e] = 1
            for y in range(8):
                sel[UP0 + a * 128 + y * 16 + e, 16 * e + 4 * a + y // 2] = 1
    for v in range(16):
        for o in range(16):
            sel[SWAP0 + v * 16 + o, o * 16 + v] = 1
    sel[EYE0 : EYE0 + 256] = np.eye(256)
    for z in range(256):
        sel[PAIR0 + z // 2, z] = 1

    slab = np.zeros((480, 512), np.float32)
    for xs in range(10):
        x = xs - 1
        for i in range(4):
            for y in range(8):
                column = i * 64 + x * 8 + y if 0 <= x < 8 else 256 + (32 if x == 8 else 0) + i * 8 + y
                slab[xs * 48 + i * 8 + y, column] = 1
            low, high = (320 + x * 4, 352 + x * 4) if 0 <= x < 8 else ((384, 400) if x < 0 else (416, 432))
            slab[xs * 48 + 32 + i, low + i] = 1
            slab[xs * 48 + 36 + i, high + i] = 1

    taps = np.zeros((128, 8 * 512), np.float32)
    for y in range(8):
        for a in range(3):
            for b in range(3):
                for c in range(3):
                    for i in range(4):
                        row = y + b - 1
                        k = 32 + i if row < 0 else 36 + i if row > 7 else i * 8 + row
                        taps[(a * 9 + b * 3 + c) * 4 + i, y * 512 + a * 144 + c * 48 + k] = 1

    band = np.zeros((96, 8 * 256), np.float32)
    for u in range(8):
        for a in range(3):
            if 0 <= u + a - 1 < 8:
                for i in range(32):
                    band[a * 32 + i, u * 256 + (u + a - 1) * 32 + i] = 1
    return [t.astype(ml_dtypes.bfloat16) for t in (sel, slab, taps, taps.T, band)]


def dot(a, b):
    return jnp.dot(a, b, preferred_element_type=F32)


def dot_t(a, b):
    return lax.dot_general(a, b, (((1,), (1,)), ((), ())), preferred_element_type=F32)


def moved(value, step):
    width = value.shape[1]
    lane = lax.broadcasted_iota(jnp.int32, value.shape, 1)
    edge = 0 if step > 0 else width - 1
    return jnp.where(lane == edge, 0.0, pltpu.roll(value, step % width, 1))


def kernel(*refs):
    count = len(OPERANDS)
    given, refs = refs[:count], refs[count:]
    deep_out, grad_deep, grad_early = refs[:3]
    here, refs = refs[3 : 3 + count], refs[3 + count :]
    vol, wet, wdt, dout, sel, slab, taps, back, band = here
    (sb, halo, vs, te, fac, pooled, dl, xx, down, g, gs, tdt, td, tw, own, r, pr, q, rr, po, ro, igl, igr, up, ae, acc,
     ar1, ar2) = refs[: len(SCRATCH)]
    (got, halo_s, halo_r, g_s, g_r, dl_s, dl_r, xx_s, xx_r, fw_s, pr_s, pr_r, rr_s, rr_r, ro_s, ro_r, ig_s, ig_r,
     a1_s, a1_r, a2_s, a2_r) = refs[len(SCRATCH) :]

    fetches = [pltpu.make_async_copy(given[k], here[k], got.at[k]) for k in range(count)]
    for k in (0, 3, 4, 1, 6, 5, 2, 8, 7):
        fetches[k].start()

    def fetched(*which):
        for k in which:
            fetches[k].wait()

    c, f = lax.axis_index("cin"), lax.axis_index("flt")
    chip, core = f // 2, lax.rem(f, 2)
    mate = f + 1 - 2 * core

    def remote(src, dst, send, recv, to_c, to_f):
        return pltpu.make_async_remote_copy(
            src_ref=src, dst_ref=dst, send_sem=send, recv_sem=recv,
            device_id=(to_c, to_f), device_id_type=MESH,
        )

    def exists(piece, sign):
        to_c, to_f = c + sign * piece[2], f + sign * piece[3]
        return (to_c >= 0) & (to_c < NC) & (to_f >= 0) & (to_f < NF)

    def halo_copy(j):
        first, rows, dc, df = PIECES[j]
        at = pl.ds(first, rows)
        return remote(sb.at[at], halo.at[at], halo_s.at[j], halo_r.at[j], c + dc, f + df)

    def g_copy(to, of):
        return remote(down, g.at[:, of], g_s.at[to], g_r.at[of], to, f)

    def dl_copy(to, of):
        return remote(dl.at[to], xx.at[1 + f, of], dl_s.at[to], dl_r.at[of], to, f)

    def xx_copy(to, of):
        block = 2 * of + core
        return remote(xx.at[1 + block], xx.at[1 + block], xx_s.at[to], xx_r.at[block], c, 2 * to + core)

    def mate_copy(block):
        return remote(xx.at[1 + block], xx.at[1 + block], fw_s.at[block], xx_r.at[block], c, mate)

    def pr_copy(k):
        return remote(r.at[k], pr.at[k], pr_s.at[k], pr_r.at[k], c, mate)

    def rr_copy(to, of):
        return remote(q.at[to], rr.at[of], rr_s.at[to], rr_r.at[of], c, 2 * to + core)

    def ro_copy(to, of):
        return remote(po.at[to], ro.at[of], ro_s.at[to], ro_r.at[of], to, f)

    def ig_copy(to, of):
        return remote(igl.at[to], igr.at[of], ig_s.at[to], ig_r.at[of], to, f)

    def a1_copy(to, of):
        return remote(ar1.at[of], ar1.at[of], a1_s.at[to], a1_r.at[of], to, f)

    def a2_copy(to, of):
        return remote(ar2.at[of], ar2.at[of], a2_s.at[to], a2_r.at[of], c, to)

    def each(count, me, act):
        @pl.loop(1, count)
        def _(k):
            act(lax.rem(me + k, count))

    def send(count, me, copy):
        each(count, me, lambda to: copy(to, me).start())

    def receive(count, me, copy):
        each(count, me, lambda of: copy(of, of).wait_recv())

    def sent(count, me, copy):
        each(count, me, lambda to: copy(to, me).wait_send())

    halo[...] = jnp.zeros_like(halo)

    barrier = pltpu.get_barrier_semaphore()

    def greet(to_c, to_f):
        pl.semaphore_signal(barrier, inc=1, device_id=(to_c, to_f), device_id_type=MESH)

    each(NC, c, lambda to: greet(to, f))
    each(NF, f, lambda to: greet(c, to))
    expected = NC + NF - 2
    for piece in PIECES[4:]:
        there = exists(piece, 1)

        @pl.when(there)
        def _(piece=piece):
            greet(c + piece[2], f + piece[3])

        expected = expected + there.astype(jnp.int32)

    fetched(0, 3, 4)
    sb[...] = dot(sel[Q0:PERM0], vol[...]).astype(BF16)
    swapped = dot(sel[SWAP0:EYE0], dout[...]).astype(BF16).reshape(16, 16, 128)
    down[...] = swapped
    g[:, pl.ds(c, 1)] = swapped[:, None]
    xx[0] = jnp.zeros(xx.shape[1:], BF16)
    xx[17] = jnp.zeros(xx.shape[1:], BF16)
    for k in range(3):
        gs[k, 0] = jnp.zeros(gs.shape[2:], BF16)
        gs[k, 17] = jnp.zeros(gs.shape[2:], BF16)

    pl.semaphore_wait(barrier, expected)
    for j, piece in enumerate(PIECES):

        @pl.when(exists(piece, 1))
        def _(j=j):
            halo_copy(j).start()

    send(NC, c, g_copy)

    fetched(1, 6)
    early = dot_t(sel[EYE0 : EYE0 + 16, :16], wet[...]).astype(BF16)
    for y in range(8):
        te[y * 16 : (y + 1) * 16, :] = dot(early, taps[:, y * 512 : (y + 1) * 512]).astype(BF16)

    for j, piece in enumerate(PIECES):

        @pl.when(exists(piece, -1))
        def _(j=j):
            halo_copy(j).wait_recv()

    fetched(5)
    cells = dot(slab[:, :256], vol[...]) + dot(slab[:, 256:448], halo[...])
    for k, shifted in enumerate((moved(cells, 1), cells, moved(cells, -1))):
        shifted = shifted.astype(BF16)
        for xs in range(10):
            vs[xs * 144 + k * 48 : xs * 144 + k * 48 + 48, :] = shifted[xs * 48 : xs * 48 + 48]
    vs[1440:1584, :] = jnp.zeros((144, 256), BF16)

    @pl.loop(0, 4)
    def _(a):
        total = jnp.zeros((128, 256), F32)
        for x in range(2):
            at = pl.multiple_of((2 * a + x) * 144, 16)
            pre = dot(te[...], vs[pl.ds(at, 512), :])
            factor = jnp.where(pre > 0, 1.0, slope)
            fac[2 * a + x] = factor
            total += pre * factor
        for b in range(4):
            pooled[a, b * 16 : b * 16 + 16] = (
                total[b * 32 : b * 32 + 16] + total[b * 32 + 16 : b * 32 + 32]
            )

    pair = sel[PAIR0:END0]
    field = pooled[...].reshape(256, 256)
    high = field.astype(BF16)
    low = (field - high.astype(F32)).astype(BF16)
    means = ((dot_t(high, pair) + dot_t(low, pair)) * 0.125).astype(BF16)
    local = dot(sel[PERM0:UP0], means).astype(BF16).reshape(8, 32, 128)
    dl[...] = local
    send(NC, c, dl_copy)
    xx[1 + f, c] = dl[c]

    fetched(2, 8)
    for u in range(8):
        columns = slice(u * 256, (u + 1) * 256)
        wide = dot(wdt[0:144], band[0:32, columns])
        wide += dot(wdt[144:288], band[32:64, columns])
        wide += dot(wdt[288:432], band[64:96, columns])
        wide = wide.astype(BF16)
        for b in range(3):
            for k in range(3):
                block = wide[(b * 3 + k) * 16 : (b * 3 + k) * 16 + 16]
                tw[k, u * 16 : u * 16 + 16, b * 256 : (b + 1) * 256] = block
                tdt[k, (2 - b) * 128 + u * 16 : (2 - b) * 128 + u * 16 + 16] = block
    for k in range(3):
        td[k] = dot_t(sel[EYE0:PAIR0], tdt[k]).astype(BF16)

    receive(NC, c, dl_copy)
    send(NF // 2, chip, xx_copy)
    mate_copy(f).start()

    receive(NC, c, g_copy)

    @pl.loop(0, 16)
    def _(v):
        plain = g[v].reshape(128, 128)
        wide = plain.astype(F32)
        gs[0, v + 1] = moved(wide, -1).astype(BF16)
        gs[1, v + 1] = plain
        gs[2, v + 1] = moved(wide, 1).astype(BF16)

    def chip_at(k):
        return lax.rem(chip + 1 + k, 8)

    def combine(k):
        to = chip_at(k)
        pr_copy(to).wait_recv()
        total = (own[to] + pr[to].astype(F32)).astype(BF16)

        @pl.when(to != chip)
        def _():
            q[to] = total
            rr_copy(to, chip).start()

        @pl.when(to == chip)
        def _():
            rr[chip] = total

    @pl.loop(0, 8)
    def _(k):
        to = chip_at(k)
        v = 2 * to
        out = jnp.zeros((256, 256), F32)
        for t in range(3):
            both = jnp.concatenate(
                [gs[t, pl.ds(v, 3)].reshape(384, 128), gs[t, pl.ds(v + 1, 3)].reshape(384, 128)], 1
            )
            out += dot(td[t], both)
        first, second = out[:, :128], out[:, 128:]
        r[to] = jnp.where(core == 0, second, first).astype(BF16)
        pr_copy(to).start()
        own[to] = jnp.where(core == 0, first, second)

        @pl.when(k >= 2)
        def _():
            combine(k - 2)

    combine(6)
    combine(7)

    @pl.loop(1, 8)
    def _(k):
        of = lax.rem(chip + k, 8)
        xx_copy(of, of).wait_recv()
        mate_copy(2 * of + core).start()

    @pl.loop(0, 8)
    def _(k):
        mate_copy(2 * k + 1 - core).wait_recv()

    def pair_of_rows(v):
        return jnp.concatenate(
            [xx[pl.ds(v, 3)].reshape(768, 128), xx[pl.ds(v + 1, 3)].reshape(768, 128)], 1
        )

    @pl.loop(0, 8)
    def _(k):
        v = 2 * k
        out = dot(tw[...].reshape(384, 768), pair_of_rows(v))
        for h in range(2):
            half = out[:, h * 128 : (h + 1) * 128]
            total = moved(half[:128], 1) + half[128:256] + moved(half[256:], -1)
            po[:, v + h] = total.astype(BF16).reshape(8, 16, 128)

    send(NC, c, ro_copy)
    ro[c] = po[c]

    receive(NF // 2, chip, rr_copy)
    total = rr[0].astype(F32)
    for k in range(1, NF // 2):
        total += rr[k].astype(F32)
    igl[...] = total.astype(BF16).reshape(8, 32, 128)
    send(NC, c, ig_copy)
    igr[c] = igl[c]

    acc[...] = jnp.zeros_like(acc)

    @pl.loop(0, 8)
    def _(k):
        v = 2 * k
        both = jnp.concatenate(
            [gs[:, v + 1].reshape(384, 128), gs[:, v + 2].reshape(384, 128)], 1
        )
        acc[...] += dot_t(both, pair_of_rows(v))

    receive(NC, c, ig_copy)
    spread = dot(sel[UP0:SWAP0], igr[...].reshape(256, 128)).astype(BF16)
    up[...] = (dot(spread, pair) * 0.125).reshape(4, 128, 256)
    ae[...] = jnp.zeros_like(ae)

    @pl.loop(0, 4)
    def _(a):
        for x in range(2):
            at = pl.multiple_of((2 * a + x) * 144, 16)
            grad = (up[a] * fac[2 * a + x]).astype(BF16)
            ae[...] += dot_t(grad, vs[pl.ds(at, 512), :])

    rest = jnp.concatenate([ae[y * 16 : (y + 1) * 16] for y in range(8)], 1)
    pieces = []
    for _ in range(3):
        pieces.append(rest.astype(BF16))
        rest = rest - pieces[-1].astype(F32)
    fetched(7)
    mine = dot(jnp.concatenate(pieces, 0), back[...])
    mine = mine[:16] + mine[16:32] + mine[32:]
    ar1[c] = mine
    send(NC, c, a1_copy)

    receive(NC, c, ro_copy)
    total = ro[0].astype(F32)
    for k in range(1, NC):
        total += ro[k].astype(F32)
    rounded = total.astype(BF16).reshape(256, 128)
    deep_out[...] = dot(sel[SWAP0:EYE0], rounded).astype(BF16)

    receive(NC, c, a1_copy)
    total = ar1[0]
    for k in range(1, NC):
        total += ar1[k]
    ar2[f] = total
    send(NF, f, a2_copy)

    lane = lax.broadcasted_iota(jnp.int32, (16, 256), 1)
    for k in range(3):
        for b in range(3):
            total = jnp.zeros((16, 256), F32)
            for u in range(8):
                rows = acc[k * 128 + u * 16 : k * 128 + u * 16 + 16, b * 256 : (b + 1) * 256]
                rows = pltpu.roll(rows, (-(u - 1) * 32) % 256, 1) if u != 1 else rows
                if u == 0:
                    rows = jnp.where(lane < 32, 0.0, rows)
                if u == 7:
                    rows = jnp.where(lane >= 64, 0.0, rows)
                total += rows
            for a in range(3):
                at = ((a * 3 + b) * 3 + k) * 16
                grad_deep[at : at + 16, :] = total[:, a * 32 : (a + 1) * 32]

    receive(NF, f, a2_copy)
    total = ar2[0]
    for k in range(1, NF):
        total += ar2[k]
    square = jnp.concatenate([total, jnp.zeros((112, 128), F32)], 0)
    grad_early[...] = square.T[:, :16]

    for j, piece in enumerate(PIECES):

        @pl.when(exists(piece, 1))
        def _(j=j):
            halo_copy(j).wait_send()

    sent(NC, c, g_copy)
    sent(NC, c, dl_copy)
    sent(NF // 2, chip, xx_copy)
    sent(NF // 2, chip, rr_copy)

    @pl.loop(0, 8)
    def _(k):
        mate_copy(2 * k + core).wait_send()
        pr_copy(k).wait_send()

    sent(NC, c, ro_copy)
    sent(NC, c, ig_copy)
    sent(NC, c, a1_copy)
    sent(NF, f, a2_copy)


SCRATCH = (
    ((192, 256), BF16), ((192, 256), BF16), ((1584, 256), BF16), ((128, 512), BF16),
    ((8, 128, 256), F32), ((4, 64, 256), F32), ((8, 32, 128), BF16), ((18, 8, 32, 128), BF16),
    ((16, 16, 128), BF16), ((16, 8, 16, 128), BF16), ((3, 18, 128, 128), BF16), ((3, 384, 256), BF16),
    ((3, 256, 384), BF16), ((3, 128, 768), BF16), ((8, 256, 128), F32), ((8, 256, 128), BF16),
    ((8, 256, 128), BF16), ((8, 256, 128), BF16), ((8, 256, 128), BF16),
    ((8, 16, 16, 128), BF16), ((8, 16, 16, 128), BF16), ((8, 32, 128), BF16), ((8, 32, 128), BF16),
    ((4, 128, 256), F32), ((128, 512), F32), ((384, 768), F32), ((8, 16, 128), F32), ((16, 16, 128), F32),
)
SEMAPHORES = (9, 8, 8, 8, 8, 8, 8, 8, 16, 16, 8, 8, 8, 8, 8, 8, 8, 8, 8, 8, 16, 16)
OPERANDS = (
    (256, 256), (128, 16), (432, 32), (256, 128), (END0, 256), (480, 512), (128, 4096), (4096, 128), (96, 2048),
)


def local(volume, early_w, deep_w, d_out):
    early = early_w.transpose(2, 3, 4, 1, 0).reshape(108, 16)
    operands = [
        volume.reshape(256, 256),
        jnp.pad(early, ((0, 20), (0, 0))),
        deep_w.transpose(2, 3, 4, 0, 1).reshape(432, 32),
        d_out.reshape(256, 128),
        *[jnp.asarray(t) for t in tables()],
    ]
    deep_out, grad_deep, grad_early = pl.pallas_call(
        kernel,
        out_shape=(
            jax.ShapeDtypeStruct((256, 128), BF16),
            jax.ShapeDtypeStruct((432, 32), F32),
            jax.ShapeDtypeStruct((128, 16), F32),
        ),
        in_specs=[pl.BlockSpec(memory_space=pltpu.HBM)] * len(operands),
        out_specs=[pl.BlockSpec(memory_space=pltpu.VMEM)] * 3,
        scratch_shapes=[pltpu.VMEM(shape, BF16) for shape in OPERANDS]
        + [pltpu.VMEM(shape, dtype) for shape, dtype in SCRATCH]
        + [pltpu.SemaphoreType.DMA((count,)) for count in SEMAPHORES],
        compiler_params=pltpu.CompilerParams(
            collective_id=0, has_side_effects=True, vmem_limit_bytes=60 << 20
        ),
        name="cosmo",
    )(*operands)
    return (
        deep_out.reshape(16, 1, 16, 128),
        grad_deep.reshape(3, 3, 3, 16, 32).transpose(3, 4, 0, 1, 2),
        grad_early[:108].reshape(3, 3, 3, 4, 16).transpose(4, 3, 0, 1, 2),
    )


def solution(mesh):
    in_specs = (
        P(None, "cin", "flt", None),
        P(),
        P("flt", "cin", None, None, None),
        P("flt", "cin", None, None),
    )
    out_specs = (P("flt", "cin", None, None), P("flt", "cin", None, None, None), P())
    return jax.shard_map(local, mesh=mesh, in_specs=in_specs, out_specs=out_specs, check_vma=False)
```

```python
import jax
import jax.numpy as jnp
import ml_dtypes
import numpy as np
from jax import lax
from jax.experimental import pallas as pl
from jax.experimental.pallas import tpu as pltpu
from jax.sharding import PartitionSpec as P

MESH = pl.DeviceIdType.MESH
F32, BF16 = jnp.float32, jnp.bfloat16
slope = 0.3
NC, NF = 8, 16

PIECES = (
    (0, 32, 1, 0), (32, 32, -1, 0), (64, 32, 0, 1), (96, 32, 0, -1),
    (128, 16, 1, 1), (144, 16, 1, -1), (160, 16, -1, 1), (176, 16, -1, -1),
)
Q0, PERM0, UP0, SWAP0, EYE0, PAIR0, END0 = 0, 192, 448, 960, 1216, 1472, 1600


def tables():
    sel = np.zeros((END0, 256), np.float32)
    for i in range(4):
        for y in range(8):
            sel[Q0 + i * 8 + y, i * 64 + 56 + y] = 1
            sel[Q0 + 32 + i * 8 + y, i * 64 + y] = 1
        for x in range(8):
            sel[Q0 + 64 + x * 4 + i, i * 64 + x * 8 + 7] = 1
            sel[Q0 + 96 + x * 4 + i, i * 64 + x * 8] = 1
        sel[Q0 + 128 + i, i * 64 + 63] = 1
        sel[Q0 + 144 + i, i * 64 + 56] = 1
        sel[Q0 + 160 + i, i * 64 + 7] = 1
        sel[Q0 + 176 + i, i * 64] = 1
    for a in range(4):
        for e in range(16):
            for b in range(4):
                sel[PERM0 + 16 * e + 4 * a + b, a * 64 + b * 16 + e] = 1
            for y in range(8):
                sel[UP0 + a * 128 + y * 16 + e, 16 * e + 4 * a + y // 2] = 1
    for v in range(16):
        for o in range(16):
            sel[SWAP0 + v * 16 + o, o * 16 + v] = 1
    sel[EYE0 : EYE0 + 256] = np.eye(256)
    for z in range(256):
        sel[PAIR0 + z // 2, z] = 1

    slab = np.zeros((480, 512), np.float32)
    for xs in range(10):
        x = xs - 1
        for i in range(4):
            for y in range(8):
                column = i * 64 + x * 8 + y if 0 <= x < 8 else 256 + (32 if x == 8 else 0) + i * 8 + y
                slab[xs * 48 + i * 8 + y, column] = 1
            low, high = (320 + x * 4, 352 + x * 4) if 0 <= x < 8 else ((384, 400) if x < 0 else (416, 432))
            slab[xs * 48 + 32 + i, low + i] = 1
            slab[xs * 48 + 36 + i, high + i] = 1

    taps = np.zeros((128, 8 * 512), np.float32)
    for y in range(8):
        for a in range(3):
            for b in range(3):
                for c in range(3):
                    for i in range(4):
                        row = y + b - 1
                        k = 32 + i if row < 0 else 36 + i if row > 7 else i * 8 + row
                        taps[(a * 9 + b * 3 + c) * 4 + i, y * 512 + a * 144 + c * 48 + k] = 1

    band = np.zeros((96, 8 * 256), np.float32)
    for u in range(8):
        for a in range(3):
            if 0 <= u + a - 1 < 8:
                for i in range(32):
                    band[a * 32 + i, u * 256 + (u + a - 1) * 32 + i] = 1
    return [t.astype(ml_dtypes.bfloat16) for t in (sel, slab, taps, taps.T, band)]


def dot(a, b):
    return jnp.dot(a, b, preferred_element_type=F32)


def dot_t(a, b):
    return lax.dot_general(a, b, (((1,), (1,)), ((), ())), preferred_element_type=F32)


def moved(value, step):
    width = value.shape[1]
    lane = lax.broadcasted_iota(jnp.int32, value.shape, 1)
    edge = 0 if step > 0 else width - 1
    return jnp.where(lane == edge, 0.0, pltpu.roll(value, step % width, 1))


def kernel(*refs):
    count = len(OPERANDS)
    given, refs = refs[:count], refs[count:]
    deep_out, grad_deep, grad_early = refs[:3]
    here, refs = refs[3 : 3 + count], refs[3 + count :]
    vol, wet, wdt, dout, sel, slab, taps, back, band = here
    (sb, halo, vs, te, fac, pooled, dl, xx, down, g, gs, gh, wl, wall, tw, own, r, pr, q, rr, po, ro, up, ae, acc,
     ar1, ar2) = refs[: len(SCRATCH)]
    (got, halo_s, halo_r, g_s, g_r, dl_s, dl_r, xx_s, xx_r, fw_s, pr_s, pr_r, rr_s, rr_r, ro_s, ro_r, w_s, w_r,
     a1_s, a1_r, a2_s, a2_r) = refs[len(SCRATCH) :]

    fetches = [pltpu.make_async_copy(given[k], here[k], got.at[k]) for k in range(count)]
    for k in (0, 3, 4, 2, 1, 6, 5, 8, 7):
        fetches[k].start()

    def fetched(*which):
        for k in which:
            fetches[k].wait()

    c, f = lax.axis_index("cin"), lax.axis_index("flt")
    chip, core = f // 2, lax.rem(f, 2)
    mate = f + 1 - 2 * core

    def remote(src, dst, send, recv, to_c, to_f):
        return pltpu.make_async_remote_copy(
            src_ref=src, dst_ref=dst, send_sem=send, recv_sem=recv,
            device_id=(to_c, to_f), device_id_type=MESH,
        )

    def exists(piece, sign):
        to_c, to_f = c + sign * piece[2], f + sign * piece[3]
        return (to_c >= 0) & (to_c < NC) & (to_f >= 0) & (to_f < NF)

    def is_cin(k):
        return (k >= 0) & (k < NC)

    def halo_copy(j):
        first, rows, dc, df = PIECES[j]
        at = pl.ds(first, rows)
        return remote(sb.at[at], halo.at[at], halo_s.at[j], halo_r.at[j], c + dc, f + df)

    def g_copy(to, of):
        return remote(down, g.at[:, of], g_s.at[to], g_r.at[of], to, f)

    def dl_copy(to, of):
        return remote(dl.at[to], xx.at[1 + f, of], dl_s.at[to], dl_r.at[of], to, f)

    def xx_copy(to, of):
        block = 2 * of + core
        return remote(xx.at[1 + block], xx.at[1 + block], xx_s.at[to], xx_r.at[block], c, 2 * to + core)

    def mate_copy(block):
        return remote(xx.at[1 + block], xx.at[1 + block], fw_s.at[block], xx_r.at[block], c, mate)

    def pr_copy(k):
        return remote(r.at[k], pr.at[k], pr_s.at[k], pr_r.at[k], c, mate)

    def rr_copy(to, of):
        return remote(q.at[to], rr.at[of], rr_s.at[to], rr_r.at[of], c, 2 * to + core)

    def ro_copy(to, of):
        return remote(po.at[to], ro.at[of], ro_s.at[to], ro_r.at[of], to, f)

    def w_copy(to, of):
        return remote(wl, wall.at[of], w_s.at[to], w_r.at[of], to, f)

    def a1_copy(to, of):
        return remote(ar1.at[of], ar1.at[of], a1_s.at[to], a1_r.at[of], to, f)

    def a2_copy(to, of):
        return remote(ar2.at[of], ar2.at[of], a2_s.at[to], a2_r.at[of], c, to)

    def each(count, me, act):
        @pl.loop(1, count)
        def _(k):
            act(lax.rem(me + k, count))

    def send(count, me, copy):
        each(count, me, lambda to: copy(to, me).start())

    def receive(count, me, copy):
        each(count, me, lambda of: copy(of, of).wait_recv())

    def sent(count, me, copy):
        each(count, me, lambda to: copy(to, me).wait_send())

    halo[...] = jnp.zeros_like(halo)

    barrier = pltpu.get_barrier_semaphore()

    def greet(to_c, to_f):
        pl.semaphore_signal(barrier, inc=1, device_id=(to_c, to_f), device_id_type=MESH)

    each(NC, c, lambda to: greet(to, f))
    each(NF, f, lambda to: greet(c, to))
    expected = NC + NF - 2
    for piece in PIECES[4:]:
        there = exists(piece, 1)

        @pl.when(there)
        def _(piece=piece):
            greet(c + piece[2], f + piece[3])

        expected = expected + there.astype(jnp.int32)

    fetched(0, 3, 4)
    sb[...] = dot(sel[Q0:PERM0], vol[...]).astype(BF16)
    swapped = dot(sel[SWAP0:EYE0], dout[...]).astype(BF16).reshape(16, 16, 128)
    down[...] = swapped
    g[:, pl.ds(c, 1)] = swapped[:, None]
    xx[0] = jnp.zeros(xx.shape[1:], BF16)
    xx[17] = jnp.zeros(xx.shape[1:], BF16)
    for k in range(3):
        gs[k, 0] = jnp.zeros(gs.shape[2:], BF16)
        gs[k, 17] = jnp.zeros(gs.shape[2:], BF16)

    fetched(2)
    turned = dot_t(sel[EYE0 : EYE0 + 32, :32], wdt[...]).astype(BF16)
    wl[:, :432] = turned
    wl[:, 432:] = jnp.zeros((32, 80), BF16)

    pl.semaphore_wait(barrier, expected)
    for j, piece in enumerate(PIECES):

        @pl.when(exists(piece, 1))
        def _(j=j):
            halo_copy(j).start()

    for step in (1, -1):

        @pl.when(is_cin(c + step))
        def _(step=step):
            g_copy(c + step, c).start()

    send(NC, c, w_copy)
    wall[c] = wl[...]

    fetched(1, 6)
    rows = jnp.concatenate([wet[...].astype(F32).reshape(108, 16), jnp.zeros((20, 16), F32)], 0)
    early = dot_t(sel[EYE0 : EYE0 + 16, :16], rows.astype(BF16)).astype(BF16)
    for y in range(8):
        te[y * 16 : (y + 1) * 16, :] = dot(early, taps[:, y * 512 : (y + 1) * 512]).astype(BF16)

    for j, piece in enumerate(PIECES):

        @pl.when(exists(piece, -1))
        def _(j=j):
            halo_copy(j).wait_recv()

    fetched(5)
    cells = dot(slab[:, :256], vol[...]) + dot(slab[:, 256:448], halo[...])
    for k, shifted in enumerate((moved(cells, 1), cells, moved(cells, -1))):
        shifted = shifted.astype(BF16)
        for xs in range(10):
            vs[xs * 144 + k * 48 : xs * 144 + k * 48 + 48, :] = shifted[xs * 48 : xs * 48 + 48]
    vs[1440:1584, :] = jnp.zeros((144, 256), BF16)

    @pl.loop(0, 4)
    def _(a):
        total = jnp.zeros((128, 256), F32)
        for x in range(2):
            at = pl.multiple_of((2 * a + x) * 144, 16)
            pre = dot(te[...], vs[pl.ds(at, 512), :])
            factor = jnp.where(pre > 0, 1.0, slope)
            fac[2 * a + x] = factor
            total += pre * factor
        for b in range(4):
            pooled[a, b * 16 : b * 16 + 16] = (
                total[b * 32 : b * 32 + 16] + total[b * 32 + 16 : b * 32 + 32]
            )

    pair = sel[PAIR0:END0]
    field = pooled[...].reshape(256, 256)
    high = field.astype(BF16)
    low = (field - high.astype(F32)).astype(BF16)
    means = ((dot_t(high, pair) + dot_t(low, pair)) * 0.125).astype(BF16)
    local = dot(sel[PERM0:UP0], means).astype(BF16).reshape(8, 32, 128)
    dl[...] = local
    send(NC, c, dl_copy)
    xx[1 + f, c] = dl[c]

    def far(k):
        return (k < c - 1) | (k > c + 1)

    @pl.loop(0, NC)
    def _(to):
        @pl.when(far(to))
        def _():
            g_copy(to, c).start()

    receive(NC, c, w_copy)
    for a in range(3):
        of = c + 1 - a
        if a != 1:

            @pl.when(is_cin(of))
            def _(of=of):
                g_copy(of, of).wait_recv()

            @pl.when(jnp.logical_not(is_cin(of)))
            def _(a=a):
                gh[a] = jnp.zeros(gh.shape[1:], BF16)

        @pl.when(is_cin(of))
        def _(a=a, of=of):
            @pl.loop(0, 16)
            def _(v):
                plain = g[v, of]
                wide = plain.astype(F32)
                gh[a, 16 - v, 0:16] = moved(wide, -1).astype(BF16)
                gh[a, 16 - v, 16:32] = plain
                gh[a, 16 - v, 32:48] = moved(wide, 1).astype(BF16)

            for edge in (0, 17):
                gh[a, edge] = jnp.zeros((48, 128), BF16)

    def chip_at(k):
        return lax.rem(chip + 1 + k, 8)

    def combine(k):
        to = chip_at(k)
        pr_copy(to).wait_recv()
        total = (own[to] + pr[to].astype(F32)).astype(BF16)

        @pl.when(to != chip)
        def _():
            q[to] = total
            rr_copy(to, chip).start()

        @pl.when(to == chip)
        def _():
            rr[chip] = total

    def dgrad(k):
        to = chip_at(k)
        v = 2 * to
        low = [gh[a, pl.ds(15 - v, 3)].reshape(144, 128) for a in range(3)]
        high = [gh[a, pl.ds(14 - v, 3)].reshape(144, 128) for a in range(3)]
        both = jnp.concatenate([jnp.concatenate(low, 0), jnp.concatenate(high, 0)], 1)
        out = dot(wall[...].reshape(256, 512)[:, :432], both)
        first, second = out[:, :128], out[:, 128:]
        r[to] = jnp.where(core == 0, second, first).astype(BF16)
        pr_copy(to).start()
        own[to] = jnp.where(core == 0, first, second)

        @pl.when(k >= 2)
        def _():
            combine(k - 2)

    pl.loop(0, 3)(dgrad)
    receive(NC, c, dl_copy)
    send(NF // 2, chip, xx_copy)
    mate_copy(f).start()
    pl.loop(3, 8)(dgrad)
    combine(6)
    combine(7)

    fetched(8)
    for u in range(8):
        columns = slice(u * 256, (u + 1) * 256)
        wide = dot(wdt[0:144], band[0:32, columns])
        wide += dot(wdt[144:288], band[32:64, columns])
        wide += dot(wdt[288:432], band[64:96, columns])
        wide = wide.astype(BF16)
        for b in range(3):
            for k in range(3):
                block = wide[(b * 3 + k) * 16 : (b * 3 + k) * 16 + 16]
                tw[k, u * 16 : u * 16 + 16, b * 256 : (b + 1) * 256] = block

    @pl.loop(0, NC)
    def _(of):
        @pl.when(far(of))
        def _():
            g_copy(of, of).wait_recv()

    @pl.loop(0, 16)
    def _(v):
        plain = g[v].reshape(128, 128)
        wide = plain.astype(F32)
        gs[0, v + 1] = moved(wide, -1).astype(BF16)
        gs[1, v + 1] = plain
        gs[2, v + 1] = moved(wide, 1).astype(BF16)

    @pl.loop(1, 8)
    def _(k):
        of = lax.rem(chip + k, 8)
        xx_copy(of, of).wait_recv()
        mate_copy(2 * of + core).start()

    @pl.loop(0, 8)
    def _(k):
        mate_copy(2 * k + 1 - core).wait_recv()

    def pair_of_rows(v):
        return jnp.concatenate(
            [xx[pl.ds(v, 3)].reshape(768, 128), xx[pl.ds(v + 1, 3)].reshape(768, 128)], 1
        )

    @pl.loop(0, 8)
    def _(k):
        v = 2 * k
        out = dot(tw[...].reshape(384, 768), pair_of_rows(v))
        for h in range(2):
            half = out[:, h * 128 : (h + 1) * 128]
            total = moved(half[:128], 1) + half[128:256] + moved(half[256:], -1)
            po[:, v + h] = total.astype(BF16).reshape(8, 16, 128)

    send(NC, c, ro_copy)
    ro[c] = po[c]

    receive(NF // 2, chip, rr_copy)
    total = rr[0].astype(F32)
    for k in range(1, NF // 2):
        total += rr[k].astype(F32)
    spread = dot(sel[UP0:SWAP0], total.astype(BF16)).astype(BF16)
    up[...] = (dot(spread, pair) * 0.125).reshape(4, 128, 256)
    ae[...] = jnp.zeros_like(ae)

    @pl.loop(0, 4)
    def _(a):
        for x in range(2):
            at = pl.multiple_of((2 * a + x) * 144, 16)
            grad = (up[a] * fac[2 * a + x]).astype(BF16)
            ae[...] += dot_t(grad, vs[pl.ds(at, 512), :])

    rest = jnp.concatenate([ae[y * 16 : (y + 1) * 16] for y in range(8)], 1)
    pieces = []
    for _ in range(3):
        pieces.append(rest.astype(BF16))
        rest = rest - pieces[-1].astype(F32)
    fetched(7)
    mine = dot(jnp.concatenate(pieces, 0), back[...])
    mine = mine[:16] + mine[16:32] + mine[32:]
    ar1[c] = mine
    send(NC, c, a1_copy)

    acc[...] = jnp.zeros_like(acc)

    @pl.loop(0, 8)
    def _(k):
        v = 2 * k
        both = jnp.concatenate(
            [gs[:, v + 1].reshape(384, 128), gs[:, v + 2].reshape(384, 128)], 1
        )
        acc[...] += dot_t(both, pair_of_rows(v))

    receive(NC, c, a1_copy)
    total = ar1[0]
    for k in range(1, NC):
        total += ar1[k]
    ar2[f] = total
    send(NF, f, a2_copy)

    receive(NC, c, ro_copy)
    total = ro[0].astype(F32)
    for k in range(1, NC):
        total += ro[k].astype(F32)
    rounded = total.astype(BF16).reshape(256, 128)
    deep_out[...] = dot(sel[SWAP0:EYE0], rounded).astype(BF16)

    lane = lax.broadcasted_iota(jnp.int32, (16, 256), 1)
    for k in range(3):
        for b in range(3):
            total = jnp.zeros((16, 256), F32)
            for u in range(8):
                rows = acc[k * 128 + u * 16 : k * 128 + u * 16 + 16, b * 256 : (b + 1) * 256]
                rows = pltpu.roll(rows, (-(u - 1) * 32) % 256, 1) if u != 1 else rows
                if u == 0:
                    rows = jnp.where(lane < 32, 0.0, rows)
                if u == 7:
                    rows = jnp.where(lane >= 64, 0.0, rows)
                total += rows
            for a in range(3):
                at = ((a * 3 + b) * 3 + k) * 16
                grad_deep[at : at + 16, :] = total[:, a * 32 : (a + 1) * 32]

    receive(NF, f, a2_copy)
    total = ar2[0]
    for k in range(1, NF):
        total += ar2[k]
    square = jnp.concatenate([total, jnp.zeros((112, 128), F32)], 0)
    grad_early[...] = square.T[:108, :16].reshape(27, 4, 16)

    for j, piece in enumerate(PIECES):

        @pl.when(exists(piece, 1))
        def _(j=j):
            halo_copy(j).wait_send()

    sent(NC, c, g_copy)
    sent(NC, c, dl_copy)
    sent(NF // 2, chip, xx_copy)
    sent(NF // 2, chip, rr_copy)

    @pl.loop(0, 8)
    def _(k):
        mate_copy(2 * k + core).wait_send()
        pr_copy(k).wait_send()

    sent(NC, c, ro_copy)
    sent(NC, c, w_copy)
    sent(NC, c, a1_copy)
    sent(NF, f, a2_copy)


SCRATCH = (
    ((192, 256), BF16), ((192, 256), BF16), ((1584, 256), BF16), ((128, 512), BF16),
    ((8, 128, 256), F32), ((4, 64, 256), F32), ((8, 32, 128), BF16), ((18, 8, 32, 128), BF16),
    ((16, 16, 128), BF16), ((16, 8, 16, 128), BF16), ((3, 18, 128, 128), BF16), ((3, 18, 48, 128), BF16),
    ((32, 512), BF16), ((8, 32, 512), BF16), ((3, 128, 768), BF16), ((8, 256, 128), F32), ((8, 256, 128), BF16),
    ((8, 256, 128), BF16), ((8, 256, 128), BF16), ((8, 256, 128), BF16),
    ((8, 16, 16, 128), BF16), ((8, 16, 16, 128), BF16),
    ((4, 128, 256), F32), ((128, 512), F32), ((384, 768), F32), ((8, 16, 128), F32), ((16, 16, 128), F32),
)
SEMAPHORES = (9, 8, 8, 8, 8, 8, 8, 8, 16, 16, 8, 8, 8, 8, 8, 8, 8, 8, 8, 8, 16, 16)
OPERANDS = (
    (256, 256), (27, 4, 16), (432, 32), (256, 128), (END0, 256), (480, 512), (128, 4096), (4096, 128), (96, 2048),
)


def hand_on(*refs):
    given, results, held, sems = refs[:3], refs[3:6], refs[6:9], refs[9]
    into = [pltpu.make_async_copy(given[k], held[k], sems.at[k]) for k in range(3)]
    out = [pltpu.make_async_copy(held[k], results[k], sems.at[3 + k]) for k in range(3)]
    for copy in into:
        copy.start()
    for k in range(3):
        into[k].wait()
        out[k].start()
    for copy in out:
        copy.wait()


def local(volume, early_w, deep_w, d_out):
    operands = [
        volume.reshape(256, 256),
        early_w.transpose(2, 3, 4, 1, 0).reshape(27, 4, 16),
        deep_w.transpose(2, 3, 4, 0, 1).reshape(432, 32),
        d_out.reshape(256, 128),
        *[jnp.asarray(t) for t in tables()],
    ]
    results = pl.pallas_call(
        kernel,
        out_shape=(
            jax.ShapeDtypeStruct((256, 128), BF16),
            jax.ShapeDtypeStruct((432, 32), F32),
            jax.ShapeDtypeStruct((27, 4, 16), F32),
        ),
        in_specs=[pl.BlockSpec(memory_space=pltpu.HBM)] * len(operands),
        out_specs=[pl.BlockSpec(memory_space=pltpu.VMEM)] * 3,
        scratch_shapes=[pltpu.VMEM(shape, BF16) for shape in OPERANDS]
        + [pltpu.VMEM(shape, dtype) for shape, dtype in SCRATCH]
        + [pltpu.SemaphoreType.DMA((count,)) for count in SEMAPHORES],
        compiler_params=pltpu.CompilerParams(
            collective_id=0, has_side_effects=True, vmem_limit_bytes=60 << 20
        ),
        name="cosmo",
    )(*operands)
    deep_out, grad_deep, grad_early = pl.pallas_call(
        hand_on,
        out_shape=[jax.ShapeDtypeStruct(x.shape, x.dtype) for x in results],
        in_specs=[pl.BlockSpec(memory_space=pl.ANY)] * 3,
        out_specs=[pl.BlockSpec(memory_space=pl.ANY)] * 3,
        scratch_shapes=[pltpu.VMEM(x.shape, x.dtype) for x in results]
        + [pltpu.SemaphoreType.DMA((6,))],
        name="results",
    )(*results)
    return (
        deep_out.reshape(16, 1, 16, 128),
        grad_deep.reshape(3, 3, 3, 16, 32).transpose(3, 4, 0, 1, 2),
        grad_early.reshape(3, 3, 3, 4, 16).transpose(4, 3, 0, 1, 2),
    )


def solution(mesh):
    in_specs = (
        P(None, "cin", "flt", None),
        P(),
        P("flt", "cin", None, None, None),
        P("flt", "cin", None, None),
    )
    out_specs = (P("flt", "cin", None, None), P("flt", "cin", None, None, None), P())
    return jax.shard_map(local, mesh=mesh, in_specs=in_specs, out_specs=out_specs, check_vma=False)
```

```python
import jax
import jax.numpy as jnp
import ml_dtypes
import numpy as np
from jax import lax
from jax.experimental import pallas as pl
from jax.experimental.pallas import tpu as pltpu
from jax.sharding import PartitionSpec as P

MESH = pl.DeviceIdType.MESH
F32, BF16 = jnp.float32, jnp.bfloat16
slope = 0.3
NC, NF = 8, 16

PIECES = (
    (0, 32, 1, 0), (32, 32, -1, 0), (64, 32, 0, 1), (96, 32, 0, -1),
    (128, 16, 1, 1), (144, 16, 1, -1), (160, 16, -1, 1), (176, 16, -1, -1),
)
Q0, PERM0, UP0, SWAP0, EYE0, PAIR0, END0 = 0, 192, 448, 960, 1216, 1472, 1600


def tables():
    sel = np.zeros((END0, 256), np.float32)
    for i in range(4):
        for y in range(8):
            sel[Q0 + i * 8 + y, i * 64 + 56 + y] = 1
            sel[Q0 + 32 + i * 8 + y, i * 64 + y] = 1
        for x in range(8):
            sel[Q0 + 64 + x * 4 + i, i * 64 + x * 8 + 7] = 1
            sel[Q0 + 96 + x * 4 + i, i * 64 + x * 8] = 1
        sel[Q0 + 128 + i, i * 64 + 63] = 1
        sel[Q0 + 144 + i, i * 64 + 56] = 1
        sel[Q0 + 160 + i, i * 64 + 7] = 1
        sel[Q0 + 176 + i, i * 64] = 1
    for a in range(4):
        for e in range(16):
            for b in range(4):
                sel[PERM0 + 16 * e + 4 * a + b, a * 64 + b * 16 + e] = 1
            for y in range(8):
                sel[UP0 + a * 128 + y * 16 + e, 16 * e + 4 * a + y // 2] = 1
    for v in range(16):
        for o in range(16):
            sel[SWAP0 + v * 16 + o, o * 16 + v] = 1
    sel[EYE0 : EYE0 + 256] = np.eye(256)
    for z in range(256):
        sel[PAIR0 + z // 2, z] = 1

    slab = np.zeros((480, 512), np.float32)
    for xs in range(10):
        x = xs - 1
        for i in range(4):
            for y in range(8):
                column = i * 64 + x * 8 + y if 0 <= x < 8 else 256 + (32 if x == 8 else 0) + i * 8 + y
                slab[xs * 48 + i * 8 + y, column] = 1
            low, high = (320 + x * 4, 352 + x * 4) if 0 <= x < 8 else ((384, 400) if x < 0 else (416, 432))
            slab[xs * 48 + 32 + i, low + i] = 1
            slab[xs * 48 + 36 + i, high + i] = 1

    taps = np.zeros((128, 8 * 512), np.float32)
    for y in range(8):
        for a in range(3):
            for b in range(3):
                for c in range(3):
                    for i in range(4):
                        row = y + b - 1
                        k = 32 + i if row < 0 else 36 + i if row > 7 else i * 8 + row
                        taps[(a * 9 + b * 3 + c) * 4 + i, y * 512 + a * 144 + c * 48 + k] = 1

    band = np.zeros((96, 8 * 256), np.float32)
    for u in range(8):
        for a in range(3):
            if 0 <= u + a - 1 < 8:
                for i in range(32):
                    band[a * 32 + i, u * 256 + (u + a - 1) * 32 + i] = 1
    return [t.astype(ml_dtypes.bfloat16) for t in (sel, slab, taps, taps.T, band)]


def dot(a, b):
    return jnp.dot(a, b, preferred_element_type=F32)


def dot_t(a, b):
    return lax.dot_general(a, b, (((1,), (1,)), ((), ())), preferred_element_type=F32)


def moved(value, step):
    width = value.shape[1]
    lane = lax.broadcasted_iota(jnp.int32, value.shape, 1)
    edge = 0 if step > 0 else width - 1
    return jnp.where(lane == edge, 0.0, pltpu.roll(value, step % width, 1))


def kernel(*refs):
    count = len(OPERANDS)
    given, refs = refs[:count], refs[count:]
    deep_out, grad_deep, grad_early = refs[:3]
    here, refs = refs[3 : 3 + count], refs[3 + count :]
    vol, wet, wdt, dout, sel, slab, taps, back, band = here
    (sb, halo, vs, te, fac, pooled, dl, xx, down, g, gs, gh, wl, wall, tw, own, r, pr, q, rr, po, ro, up, ae, acc,
     ar1, ar2, xsum, xgot) = refs[: len(SCRATCH)]
    (got, halo_s, halo_r, g_s, g_r, dl_s, dl_r, xx_s, xx_r, far_s, far_r, fw_s, pr_s, pr_r, rr_s, rr_r, ro_s, ro_r, w_s, w_r,
     a1_s, a1_r, a2_s, a2_r) = refs[len(SCRATCH) :]

    fetches = [pltpu.make_async_copy(given[k], here[k], got.at[k]) for k in range(count)]
    for k in (0, 3, 4, 2, 1, 6, 5, 8, 7):
        fetches[k].start()

    def fetched(*which):
        for k in which:
            fetches[k].wait()

    c, f = lax.axis_index("cin"), lax.axis_index("flt")
    chip, core = f // 2, lax.rem(f, 2)
    mate = f + 1 - 2 * core
    z, xh = chip // 2, lax.rem(chip, 2)
    across = f + 2 - 4 * xh

    def remote(src, dst, send, recv, to_c, to_f):
        return pltpu.make_async_remote_copy(
            src_ref=src, dst_ref=dst, send_sem=send, recv_sem=recv,
            device_id=(to_c, to_f), device_id_type=MESH,
        )

    def exists(piece, sign):
        to_c, to_f = c + sign * piece[2], f + sign * piece[3]
        return (to_c >= 0) & (to_c < NC) & (to_f >= 0) & (to_f < NF)

    def is_cin(k):
        return (k >= 0) & (k < NC)

    def halo_copy(j):
        first, rows, dc, df = PIECES[j]
        at = pl.ds(first, rows)
        return remote(sb.at[at], halo.at[at], halo_s.at[j], halo_r.at[j], c + dc, f + df)

    def g_copy(to, of):
        return remote(down, g.at[:, of], g_s.at[to], g_r.at[of], to, f)

    def dl_copy(to, of):
        return remote(dl.at[to], xx.at[1 + f, of], dl_s.at[to], dl_r.at[of], to, f)

    def at_z(to):
        return 4 * to + 2 * xh + core

    def across_copy(block):
        return remote(xx.at[1 + block], xx.at[1 + block], far_s.at[0], xx_r.at[block], c, across)

    def z_copy(to, block, k):
        return remote(xx.at[1 + block], xx.at[1 + block], xx_s.at[4 * k + to], xx_r.at[block], c, at_z(to))

    def mate_copy(block):
        return remote(xx.at[1 + block], xx.at[1 + block], fw_s.at[block], xx_r.at[block], c, mate)

    def pr_copy(k):
        return remote(r.at[k], pr.at[k], pr_s.at[k], pr_r.at[k], c, mate)

    def rr_copy(to):
        to_z, to_x = to // 2, lax.rem(to, 2)
        return remote(q.at[to], rr.at[to_x, z], rr_s.at[to], rr_r.at[4 * to_x + z], c, at_z(to_z))

    def rr_wait(x, of):
        remote(q.at[0], rr.at[x, of], rr_s.at[0], rr_r.at[4 * x + of], c, mate).wait_recv()

    def sum_copy():
        return remote(xsum, xgot, far_s.at[1], far_r.at[0], c, across)

    def ro_copy(to, of):
        return remote(po.at[to], ro.at[of], ro_s.at[to], ro_r.at[of], to, f)

    def w_copy(to, of):
        return remote(wl, wall.at[of], w_s.at[to], w_r.at[of], to, f)

    def a1_copy(to, of):
        return remote(ar1.at[of], ar1.at[of], a1_s.at[to], a1_r.at[of], c, to)

    def a2_copy(to, of):
        return remote(ar2.at[of], ar2.at[of], a2_s.at[to], a2_r.at[of], to, f)

    def each(count, me, act):
        @pl.loop(1, count)
        def _(k):
            act(lax.rem(me + k, count))

    def send(count, me, copy):
        each(count, me, lambda to: copy(to, me).start())

    def receive(count, me, copy):
        each(count, me, lambda of: copy(of, of).wait_recv())

    def sent(count, me, copy):
        each(count, me, lambda to: copy(to, me).wait_send())

    halo[...] = jnp.zeros_like(halo)

    barrier = pltpu.get_barrier_semaphore()

    def greet(to_c, to_f):
        pl.semaphore_signal(barrier, inc=1, device_id=(to_c, to_f), device_id_type=MESH)

    each(NC, c, lambda to: greet(to, f))
    each(NF, f, lambda to: greet(c, to))
    expected = NC + NF - 2
    for piece in PIECES[4:]:
        there = exists(piece, 1)

        @pl.when(there)
        def _(piece=piece):
            greet(c + piece[2], f + piece[3])

        expected = expected + there.astype(jnp.int32)

    fetched(0, 3, 4)
    sb[...] = dot(sel[Q0:PERM0], vol[...]).astype(BF16)
    swapped = dot(sel[SWAP0:EYE0], dout[...]).astype(BF16).reshape(16, 16, 128)
    down[...] = swapped
    g[:, pl.ds(c, 1)] = swapped[:, None]
    xx[0] = jnp.zeros(xx.shape[1:], BF16)
    xx[17] = jnp.zeros(xx.shape[1:], BF16)
    for k in range(3):
        gs[k, 0] = jnp.zeros(gs.shape[2:], BF16)
        gs[k, 17] = jnp.zeros(gs.shape[2:], BF16)

    fetched(2)
    turned = dot_t(sel[EYE0 : EYE0 + 32, :32], wdt[...]).astype(BF16)
    wl[:, :432] = turned
    wl[:, 432:] = jnp.zeros((32, 80), BF16)

    pl.semaphore_wait(barrier, expected)
    for j, piece in enumerate(PIECES):

        @pl.when(exists(piece, 1))
        def _(j=j):
            halo_copy(j).start()

    for step in (1, -1):

        @pl.when(is_cin(c + step))
        def _(step=step):
            g_copy(c + step, c).start()

    send(NC, c, w_copy)
    wall[c] = wl[...]

    fetched(1, 6)
    rows = jnp.concatenate([wet[...].astype(F32).reshape(108, 16), jnp.zeros((20, 16), F32)], 0)
    early = dot_t(sel[EYE0 : EYE0 + 16, :16], rows.astype(BF16)).astype(BF16)
    for y in range(8):
        te[y * 16 : (y + 1) * 16, :] = dot(early, taps[:, y * 512 : (y + 1) * 512]).astype(BF16)

    for j, piece in enumerate(PIECES):

        @pl.when(exists(piece, -1))
        def _(j=j):
            halo_copy(j).wait_recv()

    fetched(5)
    cells = dot(slab[:, :256], vol[...]) + dot(slab[:, 256:448], halo[...])
    for k, shifted in enumerate((moved(cells, 1), cells, moved(cells, -1))):
        shifted = shifted.astype(BF16)
        for xs in range(10):
            vs[xs * 144 + k * 48 : xs * 144 + k * 48 + 48, :] = shifted[xs * 48 : xs * 48 + 48]
    vs[1440:1584, :] = jnp.zeros((144, 256), BF16)

    @pl.loop(0, 4)
    def _(a):
        total = jnp.zeros((128, 256), F32)
        for x in range(2):
            at = pl.multiple_of((2 * a + x) * 144, 16)
            pre = dot(te[...], vs[pl.ds(at, 512), :])
            factor = jnp.where(pre > 0, 1.0, slope)
            fac[2 * a + x] = factor
            total += pre * factor
        for b in range(4):
            pooled[a, b * 16 : b * 16 + 16] = (
                total[b * 32 : b * 32 + 16] + total[b * 32 + 16 : b * 32 + 32]
            )

    pair = sel[PAIR0:END0]
    field = pooled[...].reshape(256, 256)
    high = field.astype(BF16)
    low = (field - high.astype(F32)).astype(BF16)
    means = ((dot_t(high, pair) + dot_t(low, pair)) * 0.125).astype(BF16)
    local = dot(sel[PERM0:UP0], means).astype(BF16).reshape(8, 32, 128)
    dl[...] = local
    send(NC, c, dl_copy)
    xx[1 + f, c] = dl[c]

    def far(k):
        return (k < c - 1) | (k > c + 1)

    @pl.loop(0, NC)
    def _(to):
        @pl.when(far(to))
        def _():
            g_copy(to, c).start()

    receive(NC, c, w_copy)
    for a in range(3):
        of = c + 1 - a
        if a != 1:

            @pl.when(is_cin(of))
            def _(of=of):
                g_copy(of, of).wait_recv()

            @pl.when(jnp.logical_not(is_cin(of)))
            def _(a=a):
                gh[a] = jnp.zeros(gh.shape[1:], BF16)

        @pl.when(is_cin(of))
        def _(a=a, of=of):
            plain = g[:, pl.ds(of, 1)].reshape(256, 128)
            wide = plain.astype(F32)
            parts = (moved(wide, -1).astype(BF16), plain, moved(wide, 1).astype(BF16))
            for v in range(16):
                for k in range(3):
                    gh[a, 16 - v, k * 16 : k * 16 + 16] = parts[k][v * 16 : v * 16 + 16]

            for edge in (0, 17):
                gh[a, edge] = jnp.zeros((48, 128), BF16)

    def chip_at(k):
        return 2 * lax.rem(z + 1 + k, 4) + lax.rem(xh + 1 + k // 4, 2)

    def combine(k):
        to = chip_at(k)
        pr_copy(to).wait_recv()
        total = (own[to] + pr[to].astype(F32)).astype(BF16)

        @pl.when(to // 2 != z)
        def _():
            q[to] = total
            rr_copy(to).start()

        @pl.when(to // 2 == z)
        def _():
            rr[lax.rem(to, 2), z] = total

    def dgrad(k):
        to = chip_at(k)
        v = 2 * to
        low = [gh[a, pl.ds(15 - v, 3)].reshape(144, 128) for a in range(3)]
        high = [gh[a, pl.ds(14 - v, 3)].reshape(144, 128) for a in range(3)]
        both = jnp.concatenate([jnp.concatenate(low, 0), jnp.concatenate(high, 0)], 1)
        out = dot(wall[...].reshape(256, 512)[:, :432], both)
        first, second = out[:, :128], out[:, 128:]
        r[to] = jnp.where(core == 0, second, first).astype(BF16)
        pr_copy(to).start()
        own[to] = jnp.where(core == 0, first, second)

        @pl.when(k >= 2)
        def _():
            combine(k - 2)

    pl.loop(0, 3)(dgrad)
    receive(NC, c, dl_copy)
    across_copy(f).start()
    each(4, z, lambda to: z_copy(to, f, 0).start())
    mate_copy(f).start()
    pl.loop(3, 6)(dgrad)
    across_copy(across).wait_recv()
    each(4, z, lambda to: z_copy(to, across, 1).start())
    mate_copy(across).start()
    pl.loop(6, 8)(dgrad)
    combine(6)
    combine(7)

    fetched(8)
    for u in range(8):
        columns = slice(u * 256, (u + 1) * 256)
        wide = dot(wdt[0:144], band[0:32, columns])
        wide += dot(wdt[144:288], band[32:64, columns])
        wide += dot(wdt[288:432], band[64:96, columns])
        wide = wide.astype(BF16)
        for b in range(3):
            for k in range(3):
                block = wide[(b * 3 + k) * 16 : (b * 3 + k) * 16 + 16]
                tw[k, u * 16 : u * 16 + 16, b * 256 : (b + 1) * 256] = block

    def summed(x):
        each(4, z, lambda of: rr_wait(x, of))
        total = rr[x, 0].astype(F32)
        for k in range(1, 4):
            total += rr[x, k].astype(F32)
        return total

    xsum[...] = summed(1 - xh).astype(BF16)
    sum_copy().start()
    for x in range(2):
        side = f if x else across

        def pass_on(of, side=side):
            block = 4 * of + lax.rem(side, 4)
            z_copy(of, block, 0).wait_recv()
            mate_copy(block).start()

        each(4, z, pass_on)

    total = summed(xh)
    sum_copy().wait_recv()
    total += xgot[...].astype(F32)
    spread = dot(sel[UP0:SWAP0], total.astype(BF16)).astype(BF16)
    up[...] = (dot(spread, pair) * 0.125).reshape(4, 128, 256)
    ae[...] = jnp.zeros_like(ae)

    @pl.loop(0, 4)
    def _(a):
        for x in range(2):
            at = pl.multiple_of((2 * a + x) * 144, 16)
            grad = (up[a] * fac[2 * a + x]).astype(BF16)
            ae[...] += dot_t(grad, vs[pl.ds(at, 512), :])

    rest = jnp.concatenate([ae[y * 16 : (y + 1) * 16] for y in range(8)], 1)
    pieces = []
    for _ in range(3):
        pieces.append(rest.astype(BF16))
        rest = rest - pieces[-1].astype(F32)
    fetched(7)
    mine = dot(jnp.concatenate(pieces, 0), back[...])
    mine = mine[:16] + mine[16:32] + mine[32:]
    ar1[f] = mine
    send(NF, f, a1_copy)

    @pl.loop(0, 8)
    def _(k):
        mate_copy(2 * k + 1 - core).wait_recv()

    def pair_of_rows(v):
        return jnp.concatenate(
            [xx[pl.ds(v, 3)].reshape(768, 128), xx[pl.ds(v + 1, 3)].reshape(768, 128)], 1
        )

    @pl.loop(0, 8)
    def _(k):
        v = 2 * k
        out = dot(tw[...].reshape(384, 768), pair_of_rows(v))
        for h in range(2):
            half = out[:, h * 128 : (h + 1) * 128]
            total = moved(half[:128], 1) + half[128:256] + moved(half[256:], -1)
            po[:, v + h] = total.astype(BF16).reshape(8, 16, 128)

    send(NC, c, ro_copy)
    ro[c] = po[c]

    receive(NF, f, a1_copy)
    total = ar1[0]
    for k in range(1, NF):
        total += ar1[k]
    ar2[c] = total
    send(NC, c, a2_copy)

    @pl.loop(0, NC)
    def _(of):
        @pl.when(far(of))
        def _():
            g_copy(of, of).wait_recv()

    @pl.loop(0, 16)
    def _(v):
        plain = g[v].reshape(128, 128)
        wide = plain.astype(F32)
        gs[0, v + 1] = moved(wide, -1).astype(BF16)
        gs[1, v + 1] = plain
        gs[2, v + 1] = moved(wide, 1).astype(BF16)

    acc[...] = jnp.zeros_like(acc)

    @pl.loop(0, 8)
    def _(k):
        v = 2 * k
        both = jnp.concatenate(
            [gs[:, v + 1].reshape(384, 128), gs[:, v + 2].reshape(384, 128)], 1
        )
        acc[...] += dot_t(both, pair_of_rows(v))

    receive(NC, c, ro_copy)
    total = ro[0].astype(F32)
    for k in range(1, NC):
        total += ro[k].astype(F32)
    rounded = total.astype(BF16).reshape(256, 128)
    deep_out[...] = dot(sel[SWAP0:EYE0], rounded).astype(BF16)

    lane = lax.broadcasted_iota(jnp.int32, (16, 256), 1)
    for k in range(3):
        for b in range(3):
            total = jnp.zeros((16, 256), F32)
            for u in range(8):
                rows = acc[k * 128 + u * 16 : k * 128 + u * 16 + 16, b * 256 : (b + 1) * 256]
                rows = pltpu.roll(rows, (-(u - 1) * 32) % 256, 1) if u != 1 else rows
                if u == 0:
                    rows = jnp.where(lane < 32, 0.0, rows)
                if u == 7:
                    rows = jnp.where(lane >= 64, 0.0, rows)
                total += rows
            for a in range(3):
                at = ((a * 3 + b) * 3 + k) * 16
                grad_deep[at : at + 16, :] = total[:, a * 32 : (a + 1) * 32]

    receive(NC, c, a2_copy)
    total = ar2[0]
    for k in range(1, NC):
        total += ar2[k]
    square = jnp.concatenate([total, jnp.zeros((112, 128), F32)], 0)
    grad_early[...] = square.T[:108, :16].reshape(27, 4, 16)

    for j, piece in enumerate(PIECES):

        @pl.when(exists(piece, 1))
        def _(j=j):
            halo_copy(j).wait_send()

    sent(NC, c, g_copy)
    sent(NC, c, dl_copy)
    across_copy(f).wait_send()
    sum_copy().wait_send()
    for k in range(2):
        each(4, z, lambda to, k=k: z_copy(to, f, k).wait_send())
        each(4, z, lambda to, k=k: rr_copy(2 * to + k).wait_send())

    @pl.loop(0, 8)
    def _(k):
        mate_copy(2 * k + core).wait_send()
        pr_copy(k).wait_send()

    sent(NC, c, ro_copy)
    sent(NC, c, w_copy)
    sent(NF, f, a1_copy)
    sent(NC, c, a2_copy)


SCRATCH = (
    ((192, 256), BF16), ((192, 256), BF16), ((1584, 256), BF16), ((128, 512), BF16),
    ((8, 128, 256), F32), ((4, 64, 256), F32), ((8, 32, 128), BF16), ((18, 8, 32, 128), BF16),
    ((16, 16, 128), BF16), ((16, 8, 16, 128), BF16), ((3, 18, 128, 128), BF16), ((3, 18, 48, 128), BF16),
    ((32, 512), BF16), ((8, 32, 512), BF16), ((3, 128, 768), BF16), ((8, 256, 128), F32), ((8, 256, 128), BF16),
    ((8, 256, 128), BF16), ((8, 256, 128), BF16), ((2, 4, 256, 128), BF16),
    ((8, 16, 16, 128), BF16), ((8, 16, 16, 128), BF16),
    ((4, 128, 256), F32), ((128, 512), F32), ((384, 768), F32), ((16, 16, 128), F32), ((8, 16, 128), F32),
    ((256, 128), BF16), ((256, 128), BF16),
)
SEMAPHORES = (9, 8, 8, 8, 8, 8, 8, 8, 16, 2, 1, 16, 8, 8, 8, 8, 8, 8, 8, 8, 16, 16, 8, 8)
OPERANDS = (
    (256, 256), (27, 4, 16), (432, 32), (256, 128), (END0, 256), (480, 512), (128, 4096), (4096, 128), (96, 2048),
)


def hand_on(*refs):
    given, results, held, sems = refs[:3], refs[3:6], refs[6:9], refs[9]
    into = [pltpu.make_async_copy(given[k], held[k], sems.at[k]) for k in range(3)]
    out = [pltpu.make_async_copy(held[k], results[k], sems.at[3 + k]) for k in range(3)]
    for copy in into:
        copy.start()
    for k in range(3):
        into[k].wait()
        out[k].start()
    for copy in out:
        copy.wait()


def local(volume, early_w, deep_w, d_out):
    operands = [
        volume.reshape(256, 256),
        early_w.transpose(2, 3, 4, 1, 0).reshape(27, 4, 16),
        deep_w.transpose(2, 3, 4, 0, 1).reshape(432, 32),
        d_out.reshape(256, 128),
        *[jnp.asarray(t) for t in tables()],
    ]
    results = pl.pallas_call(
        kernel,
        out_shape=(
            jax.ShapeDtypeStruct((256, 128), BF16),
            jax.ShapeDtypeStruct((432, 32), F32),
            jax.ShapeDtypeStruct((27, 4, 16), F32),
        ),
        in_specs=[pl.BlockSpec(memory_space=pltpu.HBM)] * len(operands),
        out_specs=[pl.BlockSpec(memory_space=pltpu.VMEM)] * 3,
        scratch_shapes=[pltpu.VMEM(shape, BF16) for shape in OPERANDS]
        + [pltpu.VMEM(shape, dtype) for shape, dtype in SCRATCH]
        + [pltpu.SemaphoreType.DMA((count,)) for count in SEMAPHORES],
        compiler_params=pltpu.CompilerParams(
            collective_id=0, has_side_effects=True, vmem_limit_bytes=60 << 20
        ),
        name="cosmo",
    )(*operands)
    deep_out, grad_deep, grad_early = pl.pallas_call(
        hand_on,
        out_shape=[jax.ShapeDtypeStruct(x.shape, x.dtype) for x in results],
        in_specs=[pl.BlockSpec(memory_space=pl.ANY)] * 3,
        out_specs=[pl.BlockSpec(memory_space=pl.ANY)] * 3,
        scratch_shapes=[pltpu.VMEM(x.shape, x.dtype) for x in results]
        + [pltpu.SemaphoreType.DMA((6,))],
        name="results",
    )(*results)
    return (
        deep_out.reshape(16, 1, 16, 128),
        grad_deep.reshape(3, 3, 3, 16, 32).transpose(3, 4, 0, 1, 2),
        grad_early.reshape(3, 3, 3, 4, 16).transpose(4, 3, 0, 1, 2),
    )


def solution(mesh):
    in_specs = (
        P(None, "cin", "flt", None),
        P(),
        P("flt", "cin", None, None, None),
        P("flt", "cin", None, None),
    )
    out_specs = (P("flt", "cin", None, None), P("flt", "cin", None, None, None), P())
    return jax.shard_map(local, mesh=mesh, in_specs=in_specs, out_specs=out_specs, check_vma=False)
```

```python
import jax
import jax.numpy as jnp
import ml_dtypes
import numpy as np
from jax import lax
from jax.experimental import pallas as pl
from jax.experimental.pallas import tpu as pltpu
from jax.sharding import PartitionSpec as P

MESH = pl.DeviceIdType.MESH
F32, BF16 = jnp.float32, jnp.bfloat16
slope = 0.3
NC, NF = 8, 16

PIECES = (
    (0, 32, 1, 0), (32, 32, -1, 0), (64, 32, 0, 1), (96, 32, 0, -1),
    (128, 16, 1, 1), (144, 16, 1, -1), (160, 16, -1, 1), (176, 16, -1, -1),
)
Q0, PERM0, UP0, SWAP0, EYE0, PAIR0, END0 = 0, 192, 448, 960, 1216, 1472, 1600


def tables():
    sel = np.zeros((END0, 256), np.float32)
    for i in range(4):
        for y in range(8):
            sel[Q0 + i * 8 + y, i * 64 + 56 + y] = 1
            sel[Q0 + 32 + i * 8 + y, i * 64 + y] = 1
        for x in range(8):
            sel[Q0 + 64 + x * 4 + i, i * 64 + x * 8 + 7] = 1
            sel[Q0 + 96 + x * 4 + i, i * 64 + x * 8] = 1
        sel[Q0 + 128 + i, i * 64 + 63] = 1
        sel[Q0 + 144 + i, i * 64 + 56] = 1
        sel[Q0 + 160 + i, i * 64 + 7] = 1
        sel[Q0 + 176 + i, i * 64] = 1
    for a in range(4):
        for e in range(16):
            for b in range(4):
                sel[PERM0 + 16 * e + 4 * a + b, a * 64 + b * 16 + e] = 1
            for y in range(8):
                sel[UP0 + a * 128 + y * 16 + e, 16 * e + 4 * a + y // 2] = 1
    for v in range(16):
        for o in range(16):
            sel[SWAP0 + v * 16 + o, o * 16 + v] = 1
    sel[EYE0 : EYE0 + 256] = np.eye(256)
    for z in range(256):
        sel[PAIR0 + z // 2, z] = 1

    slab = np.zeros((480, 512), np.float32)
    for xs in range(10):
        x = xs - 1
        for i in range(4):
            for y in range(8):
                column = i * 64 + x * 8 + y if 0 <= x < 8 else 256 + (32 if x == 8 else 0) + i * 8 + y
                slab[xs * 48 + i * 8 + y, column] = 1
            low, high = (320 + x * 4, 352 + x * 4) if 0 <= x < 8 else ((384, 400) if x < 0 else (416, 432))
            slab[xs * 48 + 32 + i, low + i] = 1
            slab[xs * 48 + 36 + i, high + i] = 1

    taps = np.zeros((128, 8 * 512), np.float32)
    for y in range(8):
        for a in range(3):
            for b in range(3):
                for c in range(3):
                    for i in range(4):
                        row = y + b - 1
                        k = 32 + i if row < 0 else 36 + i if row > 7 else i * 8 + row
                        taps[(a * 9 + b * 3 + c) * 4 + i, y * 512 + a * 144 + c * 48 + k] = 1

    band = np.zeros((96, 8 * 256), np.float32)
    for u in range(8):
        for a in range(3):
            if 0 <= u + a - 1 < 8:
                for i in range(32):
                    band[a * 32 + i, u * 256 + (u + a - 1) * 32 + i] = 1
    return [t.astype(ml_dtypes.bfloat16) for t in (sel, slab, taps, taps.T, band)]


def dot(a, b):
    return jnp.dot(a, b, preferred_element_type=F32)


def dot_t(a, b):
    return lax.dot_general(a, b, (((1,), (1,)), ((), ())), preferred_element_type=F32)


def moved(value, step):
    width = value.shape[1]
    lane = lax.broadcasted_iota(jnp.int32, value.shape, 1)
    edge = 0 if step > 0 else width - 1
    return jnp.where(lane == edge, 0.0, pltpu.roll(value, step % width, 1))


def kernel(*refs):
    count = len(OPERANDS)
    given, refs = refs[:count], refs[count:]
    deep_out, grad_deep, grad_early = refs[:3]
    here, refs = refs[3 : 3 + count], refs[3 + count :]
    vol, wet, wdt, dout, sel, slab, taps, back, band = here
    (sb, halo, vs, te, fac, pooled, dl, xx, down, g, gs, gh, wl, wall, tw, own, r, pr, q, rr, po, ro, up, ae, acc,
     ar1, ar2, xsum, xgot) = refs[: len(SCRATCH)]
    (got, halo_s, halo_r, g_s, g_r, dl_s, dl_r, xx_s, xx_r, far_s, far_r, fw_s, pr_s, pr_r, rr_s, rr_r, ro_s, ro_r, w_s, w_r,
     a1_s, a1_r, a2_s, a2_r) = refs[len(SCRATCH) :]

    fetches = [pltpu.make_async_copy(given[k], here[k], got.at[k]) for k in range(count)]
    for k in (0, 3, 4, 2, 1, 6, 5, 8, 7):
        fetches[k].start()

    def fetched(*which):
        for k in which:
            fetches[k].wait()

    c, f = lax.axis_index("cin"), lax.axis_index("flt")
    chip, core = f // 2, lax.rem(f, 2)
    mate = f + 1 - 2 * core
    z, xh = chip // 2, lax.rem(chip, 2)
    across = f + 2 - 4 * xh

    def remote(src, dst, send, recv, to_c, to_f):
        return pltpu.make_async_remote_copy(
            src_ref=src, dst_ref=dst, send_sem=send, recv_sem=recv,
            device_id=(to_c, to_f), device_id_type=MESH,
        )

    def exists(piece, sign):
        to_c, to_f = c + sign * piece[2], f + sign * piece[3]
        return (to_c >= 0) & (to_c < NC) & (to_f >= 0) & (to_f < NF)

    def is_cin(k):
        return (k >= 0) & (k < NC)

    def halo_copy(j):
        first, rows, dc, df = PIECES[j]
        at = pl.ds(first, rows)
        return remote(sb.at[at], halo.at[at], halo_s.at[j], halo_r.at[j], c + dc, f + df)

    def g_copy(to, of):
        return remote(down, g.at[:, of], g_s.at[to], g_r.at[of], to, f)

    def dl_copy(to, of):
        return remote(dl.at[to], xx.at[1 + f, of], dl_s.at[to], dl_r.at[of], to, f)

    def at_z(to):
        return 4 * to + 2 * xh + core

    def across_copy(block):
        return remote(xx.at[1 + block], xx.at[1 + block], far_s.at[0], xx_r.at[block], c, across)

    def z_copy(to, block, k):
        return remote(xx.at[1 + block], xx.at[1 + block], xx_s.at[4 * k + to], xx_r.at[block], c, at_z(to))

    def mate_copy(block):
        return remote(xx.at[1 + block], xx.at[1 + block], fw_s.at[block], xx_r.at[block], c, mate)

    def pr_copy(k):
        return remote(r.at[k], pr.at[k], pr_s.at[k], pr_r.at[k], c, mate)

    def rr_copy(to):
        to_z, to_x = to // 2, lax.rem(to, 2)
        return remote(q.at[to], rr.at[to_x, z], rr_s.at[to], rr_r.at[4 * to_x + z], c, at_z(to_z))

    def rr_wait(x, of):
        remote(q.at[0], rr.at[x, of], rr_s.at[0], rr_r.at[4 * x + of], c, mate).wait_recv()

    def sum_copy():
        return remote(xsum, xgot, far_s.at[1], far_r.at[0], c, across)

    def ro_half(h):
        at = pl.ds(8 * h, 8)

        def ro_copy(to, of):
            return remote(po.at[to, at], ro.at[of, at], ro_s.at[8 * h + to], ro_r.at[8 * h + of], to, f)

        return ro_copy

    def w_copy(to, of):
        return remote(wl, wall.at[of], w_s.at[to], w_r.at[of], to, f)

    def a1_copy(to, of):
        return remote(ar1.at[of], ar1.at[of], a1_s.at[to], a1_r.at[of], c, to)

    def a2_copy(to, of):
        return remote(ar2.at[of], ar2.at[of], a2_s.at[to], a2_r.at[of], to, f)

    def each(count, me, act):
        @pl.loop(1, count)
        def _(k):
            act(lax.rem(me + k, count))

    def send(count, me, copy):
        each(count, me, lambda to: copy(to, me).start())

    def receive(count, me, copy):
        each(count, me, lambda of: copy(of, of).wait_recv())

    def sent(count, me, copy):
        each(count, me, lambda to: copy(to, me).wait_send())

    halo[...] = jnp.zeros_like(halo)

    barrier = pltpu.get_barrier_semaphore()

    def greet(to_c, to_f):
        pl.semaphore_signal(barrier, inc=1, device_id=(to_c, to_f), device_id_type=MESH)

    each(NC, c, lambda to: greet(to, f))
    each(NF, f, lambda to: greet(c, to))
    expected = NC + NF - 2
    for piece in PIECES[4:]:
        there = exists(piece, 1)

        @pl.when(there)
        def _(piece=piece):
            greet(c + piece[2], f + piece[3])

        expected = expected + there.astype(jnp.int32)

    fetched(0, 3, 4)
    sb[...] = dot(sel[Q0:PERM0], vol[...]).astype(BF16)
    swapped = dot(sel[SWAP0:EYE0], dout[...]).astype(BF16).reshape(16, 16, 128)
    down[...] = swapped
    g[:, pl.ds(c, 1)] = swapped[:, None]
    xx[0] = jnp.zeros(xx.shape[1:], BF16)
    xx[17] = jnp.zeros(xx.shape[1:], BF16)
    for k in range(3):
        gs[k, 0] = jnp.zeros(gs.shape[2:], BF16)
        gs[k, 17] = jnp.zeros(gs.shape[2:], BF16)

    fetched(2)
    turned = dot_t(sel[EYE0 : EYE0 + 32, :32], wdt[...]).astype(BF16)
    wl[:, :432] = turned
    wl[:, 432:] = jnp.zeros((32, 80), BF16)

    pl.semaphore_wait(barrier, expected)
    for j, piece in enumerate(PIECES):

        @pl.when(exists(piece, 1))
        def _(j=j):
            halo_copy(j).start()

    for step in (1, -1):

        @pl.when(is_cin(c + step))
        def _(step=step):
            g_copy(c + step, c).start()

    send(NC, c, w_copy)
    wall[c] = wl[...]

    fetched(1, 6)
    rows = jnp.concatenate([wet[...].astype(F32).reshape(108, 16), jnp.zeros((20, 16), F32)], 0)
    early = dot_t(sel[EYE0 : EYE0 + 16, :16], rows.astype(BF16)).astype(BF16)
    for y in range(8):
        te[y * 16 : (y + 1) * 16, :] = dot(early, taps[:, y * 512 : (y + 1) * 512]).astype(BF16)

    for j, piece in enumerate(PIECES):

        @pl.when(exists(piece, -1))
        def _(j=j):
            halo_copy(j).wait_recv()

    fetched(5)
    cells = dot(slab[:, :256], vol[...]) + dot(slab[:, 256:448], halo[...])
    for k, shifted in enumerate((moved(cells, 1), cells, moved(cells, -1))):
        shifted = shifted.astype(BF16)
        for xs in range(10):
            vs[xs * 144 + k * 48 : xs * 144 + k * 48 + 48, :] = shifted[xs * 48 : xs * 48 + 48]
    vs[1440:1584, :] = jnp.zeros((144, 256), BF16)

    @pl.loop(0, 4)
    def _(a):
        total = jnp.zeros((128, 256), F32)
        for x in range(2):
            at = pl.multiple_of((2 * a + x) * 144, 16)
            pre = dot(te[...], vs[pl.ds(at, 512), :])
            factor = jnp.where(pre > 0, 1.0, slope)
            fac[2 * a + x] = factor
            total += pre * factor
        for b in range(4):
            pooled[a, b * 16 : b * 16 + 16] = (
                total[b * 32 : b * 32 + 16] + total[b * 32 + 16 : b * 32 + 32]
            )

    pair = sel[PAIR0:END0]
    field = pooled[...].reshape(256, 256)
    high = field.astype(BF16)
    low = (field - high.astype(F32)).astype(BF16)
    means = ((dot_t(high, pair) + dot_t(low, pair)) * 0.125).astype(BF16)
    local = dot(sel[PERM0:UP0], means).astype(BF16).reshape(8, 32, 128)
    dl[...] = local
    send(NC, c, dl_copy)
    xx[1 + f, c] = dl[c]

    def far(k):
        return (k < c - 1) | (k > c + 1)

    @pl.loop(0, NC)
    def _(to):
        @pl.when(far(to))
        def _():
            g_copy(to, c).start()

    receive(NC, c, w_copy)
    for a in range(3):
        of = c + 1 - a
        if a != 1:

            @pl.when(is_cin(of))
            def _(of=of):
                g_copy(of, of).wait_recv()

            @pl.when(jnp.logical_not(is_cin(of)))
            def _(a=a):
                gh[a] = jnp.zeros(gh.shape[1:], BF16)

        @pl.when(is_cin(of))
        def _(a=a, of=of):
            plain = g[:, pl.ds(of, 1)].reshape(256, 128)
            wide = plain.astype(F32)
            parts = (moved(wide, -1).astype(BF16), plain, moved(wide, 1).astype(BF16))
            for v in range(16):
                for k in range(3):
                    gh[a, 16 - v, k * 16 : k * 16 + 16] = parts[k][v * 16 : v * 16 + 16]

            for edge in (0, 17):
                gh[a, edge] = jnp.zeros((48, 128), BF16)

    def chip_at(k):
        return 2 * lax.rem(z + 1 + k, 4) + lax.rem(xh + 1 + k // 4, 2)

    def combine(k):
        to = chip_at(k)
        pr_copy(to).wait_recv()
        total = (own[to] + pr[to].astype(F32)).astype(BF16)

        @pl.when(to // 2 != z)
        def _():
            q[to] = total
            rr_copy(to).start()

        @pl.when(to // 2 == z)
        def _():
            rr[lax.rem(to, 2), z] = total

    def dgrad(k):
        to = chip_at(k)
        v = 2 * to
        low = [gh[a, pl.ds(15 - v, 3)].reshape(144, 128) for a in range(3)]
        high = [gh[a, pl.ds(14 - v, 3)].reshape(144, 128) for a in range(3)]
        both = jnp.concatenate([jnp.concatenate(low, 0), jnp.concatenate(high, 0)], 1)
        out = dot(wall[...].reshape(256, 512)[:, :432], both)
        first, second = out[:, :128], out[:, 128:]
        r[to] = jnp.where(core == 0, second, first).astype(BF16)
        pr_copy(to).start()
        own[to] = jnp.where(core == 0, first, second)

        @pl.when(k >= 2)
        def _():
            combine(k - 2)

    pl.loop(0, 3)(dgrad)
    receive(NC, c, dl_copy)
    across_copy(f).start()
    each(4, z, lambda to: z_copy(to, f, 0).start())
    mate_copy(f).start()
    pl.loop(3, 8)(dgrad)
    combine(6)
    combine(7)
    across_copy(across).wait_recv()
    each(4, z, lambda to: z_copy(to, across, 1).start())
    mate_copy(across).start()

    fetched(8)
    for u in range(8):
        columns = slice(u * 256, (u + 1) * 256)
        wide = dot(wdt[0:144], band[0:32, columns])
        wide += dot(wdt[144:288], band[32:64, columns])
        wide += dot(wdt[288:432], band[64:96, columns])
        wide = wide.astype(BF16)
        for b in range(3):
            for k in range(3):
                block = wide[(b * 3 + k) * 16 : (b * 3 + k) * 16 + 16]
                tw[k, u * 16 : u * 16 + 16, b * 256 : (b + 1) * 256] = block

    @pl.loop(0, NC)
    def _(of):
        @pl.when(far(of))
        def _():
            g_copy(of, of).wait_recv()

    @pl.loop(0, 16)
    def _(v):
        plain = g[v].reshape(128, 128)
        wide = plain.astype(F32)
        gs[0, v + 1] = moved(wide, -1).astype(BF16)
        gs[1, v + 1] = plain
        gs[2, v + 1] = moved(wide, 1).astype(BF16)

    def summed(x):
        each(4, z, lambda of: rr_wait(x, of))
        total = rr[x, 0].astype(F32)
        for k in range(1, 4):
            total += rr[x, k].astype(F32)
        return total

    xsum[...] = summed(1 - xh).astype(BF16)
    sum_copy().start()
    for x in range(2):
        side = f if x else across

        def pass_on(of, side=side):
            block = 4 * of + lax.rem(side, 4)
            z_copy(of, block, 0).wait_recv()
            mate_copy(block).start()

        each(4, z, pass_on)

    total = summed(xh)
    sum_copy().wait_recv()
    total += xgot[...].astype(F32)
    spread = dot(sel[UP0:SWAP0], total.astype(BF16)).astype(BF16)
    up[...] = (dot(spread, pair) * 0.125).reshape(4, 128, 256)
    ae[...] = jnp.zeros_like(ae)

    @pl.loop(0, 4)
    def _(a):
        for x in range(2):
            at = pl.multiple_of((2 * a + x) * 144, 16)
            grad = (up[a] * fac[2 * a + x]).astype(BF16)
            ae[...] += dot_t(grad, vs[pl.ds(at, 512), :])

    rest = jnp.concatenate([ae[y * 16 : (y + 1) * 16] for y in range(8)], 1)
    pieces = []
    for _ in range(3):
        pieces.append(rest.astype(BF16))
        rest = rest - pieces[-1].astype(F32)
    fetched(7)
    mine = dot(jnp.concatenate(pieces, 0), back[...])
    mine = mine[:16] + mine[16:32] + mine[32:]
    ar1[f] = mine
    send(NF, f, a1_copy)

    @pl.loop(0, 8)
    def _(k):
        mate_copy(2 * k + 1 - core).wait_recv()

    def pair_of_rows(v):
        return jnp.concatenate(
            [xx[pl.ds(v, 3)].reshape(768, 128), xx[pl.ds(v + 1, 3)].reshape(768, 128)], 1
        )

    def forward(k):
        v = 2 * k
        out = dot(tw[...].reshape(384, 768), pair_of_rows(v))
        for h in range(2):
            half = out[:, h * 128 : (h + 1) * 128]
            total = moved(half[:128], 1) + half[128:256] + moved(half[256:], -1)
            po[:, v + h] = total.astype(BF16).reshape(8, 16, 128)

    pl.loop(0, 4)(forward)
    send(NC, c, ro_half(0))
    pl.loop(4, 8)(forward)
    send(NC, c, ro_half(1))
    ro[c] = po[c]

    receive(NF, f, a1_copy)
    total = ar1[0]
    for k in range(1, NF):
        total += ar1[k]
    ar2[c] = total
    send(NC, c, a2_copy)

    acc[...] = jnp.zeros_like(acc)

    @pl.loop(0, 8)
    def _(k):
        v = 2 * k
        both = jnp.concatenate(
            [gs[:, v + 1].reshape(384, 128), gs[:, v + 2].reshape(384, 128)], 1
        )
        acc[...] += dot_t(both, pair_of_rows(v))

    receive(NC, c, ro_half(0))
    receive(NC, c, ro_half(1))
    total = ro[0].astype(F32)
    for k in range(1, NC):
        total += ro[k].astype(F32)
    rounded = total.astype(BF16).reshape(256, 128)
    deep_out[...] = dot(sel[SWAP0:EYE0], rounded).astype(BF16)

    lane = lax.broadcasted_iota(jnp.int32, (16, 256), 1)
    for k in range(3):
        for b in range(3):
            total = jnp.zeros((16, 256), F32)
            for u in range(8):
                rows = acc[k * 128 + u * 16 : k * 128 + u * 16 + 16, b * 256 : (b + 1) * 256]
                rows = pltpu.roll(rows, (-(u - 1) * 32) % 256, 1) if u != 1 else rows
                if u == 0:
                    rows = jnp.where(lane < 32, 0.0, rows)
                if u == 7:
                    rows = jnp.where(lane >= 64, 0.0, rows)
                total += rows
            for a in range(3):
                at = ((a * 3 + b) * 3 + k) * 16
                grad_deep[at : at + 16, :] = total[:, a * 32 : (a + 1) * 32]

    receive(NC, c, a2_copy)
    total = ar2[0]
    for k in range(1, NC):
        total += ar2[k]
    square = jnp.concatenate([total, jnp.zeros((112, 128), F32)], 0)
    grad_early[...] = square.T[:108, :16].reshape(27, 4, 16)

    for j, piece in enumerate(PIECES):

        @pl.when(exists(piece, 1))
        def _(j=j):
            halo_copy(j).wait_send()

    sent(NC, c, g_copy)
    sent(NC, c, dl_copy)
    across_copy(f).wait_send()
    sum_copy().wait_send()
    for k in range(2):
        each(4, z, lambda to, k=k: z_copy(to, f, k).wait_send())
        each(4, z, lambda to, k=k: rr_copy(2 * to + k).wait_send())

    @pl.loop(0, 8)
    def _(k):
        mate_copy(2 * k + core).wait_send()
        pr_copy(k).wait_send()

    sent(NC, c, ro_half(0))
    sent(NC, c, ro_half(1))
    sent(NC, c, w_copy)
    sent(NF, f, a1_copy)
    sent(NC, c, a2_copy)


SCRATCH = (
    ((192, 256), BF16), ((192, 256), BF16), ((1584, 256), BF16), ((128, 512), BF16),
    ((8, 128, 256), F32), ((4, 64, 256), F32), ((8, 32, 128), BF16), ((18, 8, 32, 128), BF16),
    ((16, 16, 128), BF16), ((16, 8, 16, 128), BF16), ((3, 18, 128, 128), BF16), ((3, 18, 48, 128), BF16),
    ((32, 512), BF16), ((8, 32, 512), BF16), ((3, 128, 768), BF16), ((8, 256, 128), F32), ((8, 256, 128), BF16),
    ((8, 256, 128), BF16), ((8, 256, 128), BF16), ((2, 4, 256, 128), BF16),
    ((8, 16, 16, 128), BF16), ((8, 16, 16, 128), BF16),
    ((4, 128, 256), F32), ((128, 512), F32), ((384, 768), F32), ((16, 16, 128), F32), ((8, 16, 128), F32),
    ((256, 128), BF16), ((256, 128), BF16),
)
SEMAPHORES = (9, 8, 8, 8, 8, 8, 8, 8, 16, 2, 1, 16, 8, 8, 8, 8, 16, 16, 8, 8, 16, 16, 8, 8)
OPERANDS = (
    (256, 256), (27, 4, 16), (432, 32), (256, 128), (END0, 256), (480, 512), (128, 4096), (4096, 128), (96, 2048),
)


def hand_on(*refs):
    given, results, held, sems = refs[:3], refs[3:6], refs[6:9], refs[9]
    into = [pltpu.make_async_copy(given[k], held[k], sems.at[k]) for k in range(3)]
    out = [pltpu.make_async_copy(held[k], results[k], sems.at[3 + k]) for k in range(3)]
    for copy in into:
        copy.start()
    for k in range(3):
        into[k].wait()
        out[k].start()
    for copy in out:
        copy.wait()


def local(volume, early_w, deep_w, d_out):
    operands = [
        volume.reshape(256, 256),
        early_w.transpose(2, 3, 4, 1, 0).reshape(27, 4, 16),
        deep_w.transpose(2, 3, 4, 0, 1).reshape(432, 32),
        d_out.reshape(256, 128),
        *[jnp.asarray(t) for t in tables()],
    ]
    results = pl.pallas_call(
        kernel,
        out_shape=(
            jax.ShapeDtypeStruct((256, 128), BF16),
            jax.ShapeDtypeStruct((432, 32), F32),
            jax.ShapeDtypeStruct((27, 4, 16), F32),
        ),
        in_specs=[pl.BlockSpec(memory_space=pltpu.HBM)] * len(operands),
        out_specs=[pl.BlockSpec(memory_space=pltpu.VMEM)] * 3,
        scratch_shapes=[pltpu.VMEM(shape, BF16) for shape in OPERANDS]
        + [pltpu.VMEM(shape, dtype) for shape, dtype in SCRATCH]
        + [pltpu.SemaphoreType.DMA((count,)) for count in SEMAPHORES],
        compiler_params=pltpu.CompilerParams(
            collective_id=0, has_side_effects=True, vmem_limit_bytes=60 << 20
        ),
        name="cosmo",
    )(*operands)
    deep_out, grad_deep, grad_early = pl.pallas_call(
        hand_on,
        out_shape=[jax.ShapeDtypeStruct(x.shape, x.dtype) for x in results],
        in_specs=[pl.BlockSpec(memory_space=pl.ANY)] * 3,
        out_specs=[pl.BlockSpec(memory_space=pl.ANY)] * 3,
        scratch_shapes=[pltpu.VMEM(x.shape, x.dtype) for x in results]
        + [pltpu.SemaphoreType.DMA((6,))],
        name="results",
    )(*results)
    return (
        deep_out.reshape(16, 1, 16, 128),
        grad_deep.reshape(3, 3, 3, 16, 32).transpose(3, 4, 0, 1, 2),
        grad_early.reshape(3, 3, 3, 4, 16).transpose(4, 3, 0, 1, 2),
    )


def solution(mesh):
    in_specs = (
        P(None, "cin", "flt", None),
        P(),
        P("flt", "cin", None, None, None),
        P("flt", "cin", None, None),
    )
    out_specs = (P("flt", "cin", None, None), P("flt", "cin", None, None, None), P())
    return jax.shard_map(local, mesh=mesh, in_specs=in_specs, out_specs=out_specs, check_vma=False)
```

```python
import jax
import jax.numpy as jnp
import ml_dtypes
import numpy as np
from jax import lax
from jax.experimental import pallas as pl
from jax.experimental.pallas import tpu as pltpu
from jax.sharding import PartitionSpec as P

MESH = pl.DeviceIdType.MESH
F32, BF16 = jnp.float32, jnp.bfloat16
slope = 0.3
NC, NF = 8, 16

PIECES = (
    (0, 32, 1, 0), (32, 32, -1, 0), (64, 32, 0, 1), (96, 32, 0, -1),
    (128, 16, 1, 1), (144, 16, 1, -1), (160, 16, -1, 1), (176, 16, -1, -1),
)
Q0, PERM0, UP0, SWAP0, EYE0, PAIR0, END0 = 0, 192, 448, 960, 1216, 1472, 1600


def tables():
    sel = np.zeros((END0, 256), np.float32)
    for i in range(4):
        for y in range(8):
            sel[Q0 + i * 8 + y, i * 64 + 56 + y] = 1
            sel[Q0 + 32 + i * 8 + y, i * 64 + y] = 1
        for x in range(8):
            sel[Q0 + 64 + x * 4 + i, i * 64 + x * 8 + 7] = 1
            sel[Q0 + 96 + x * 4 + i, i * 64 + x * 8] = 1
        sel[Q0 + 128 + i, i * 64 + 63] = 1
        sel[Q0 + 144 + i, i * 64 + 56] = 1
        sel[Q0 + 160 + i, i * 64 + 7] = 1
        sel[Q0 + 176 + i, i * 64] = 1
    for a in range(4):
        for e in range(16):
            for b in range(4):
                sel[PERM0 + 16 * e + 4 * a + b, a * 64 + b * 16 + e] = 1
            for y in range(8):
                sel[UP0 + a * 128 + y * 16 + e, 16 * e + 4 * a + y // 2] = 1
    for v in range(16):
        for o in range(16):
            sel[SWAP0 + v * 16 + o, o * 16 + v] = 1
    sel[EYE0 : EYE0 + 256] = np.eye(256)
    for z in range(256):
        sel[PAIR0 + z // 2, z] = 1

    slab = np.zeros((480, 512), np.float32)
    for xs in range(10):
        x = xs - 1
        for i in range(4):
            for y in range(8):
                column = i * 64 + x * 8 + y if 0 <= x < 8 else 256 + (32 if x == 8 else 0) + i * 8 + y
                slab[xs * 48 + i * 8 + y, column] = 1
            low, high = (320 + x * 4, 352 + x * 4) if 0 <= x < 8 else ((384, 400) if x < 0 else (416, 432))
            slab[xs * 48 + 32 + i, low + i] = 1
            slab[xs * 48 + 36 + i, high + i] = 1

    taps = np.zeros((128, 8 * 512), np.float32)
    for y in range(8):
        for a in range(3):
            for b in range(3):
                for c in range(3):
                    for i in range(4):
                        row = y + b - 1
                        k = 32 + i if row < 0 else 36 + i if row > 7 else i * 8 + row
                        taps[(a * 9 + b * 3 + c) * 4 + i, y * 512 + a * 144 + c * 48 + k] = 1

    band = np.zeros((96, 8 * 256), np.float32)
    for u in range(8):
        for a in range(3):
            if 0 <= u + a - 1 < 8:
                for i in range(32):
                    band[a * 32 + i, u * 256 + (u + a - 1) * 32 + i] = 1
    return [t.astype(ml_dtypes.bfloat16) for t in (sel, slab, taps, taps.T, band)]


def dot(a, b):
    return jnp.dot(a, b, preferred_element_type=F32)


def dot_t(a, b):
    return lax.dot_general(a, b, (((1,), (1,)), ((), ())), preferred_element_type=F32)


def moved(value, step):
    width = value.shape[1]
    lane = lax.broadcasted_iota(jnp.int32, value.shape, 1)
    edge = 0 if step > 0 else width - 1
    return jnp.where(lane == edge, 0.0, pltpu.roll(value, step % width, 1))


def kernel(*refs):
    count = len(OPERANDS)
    given, refs = refs[:count], refs[count:]
    deep_out, grad_deep, grad_early = refs[:3]
    here, refs = refs[3 : 3 + count], refs[3 + count :]
    vol, wet, wdt, dout, sel, slab, taps, back, band = here
    (sb, halo, vs, te, fac, pooled, dl, xx, down, g, gs, gh, wl, wall, tw, own, r, pr, q, rr, po, ro, up, ae, acc,
     ar1, ar2, xsum, xgot) = refs[: len(SCRATCH)]
    (got, halo_s, halo_r, g_s, g_r, dl_s, dl_r, xx_s, xx_r, far_s, far_r, fw_s, pr_s, pr_r, rr_s, rr_r, ro_s, ro_r, w_s, w_r,
     a1_s, a1_r, a2_s, a2_r) = refs[len(SCRATCH) :]

    fetches = [pltpu.make_async_copy(given[k], here[k], got.at[k]) for k in range(count)]
    for k in (0, 3, 4, 2, 1, 6, 5, 8, 7):
        fetches[k].start()

    def fetched(*which):
        for k in which:
            fetches[k].wait()

    c, f = lax.axis_index("cin"), lax.axis_index("flt")
    chip, core = f // 2, lax.rem(f, 2)
    mate = f + 1 - 2 * core
    z, xh = chip // 2, lax.rem(chip, 2)
    across = f + 2 - 4 * xh

    def remote(src, dst, send, recv, to_c, to_f):
        return pltpu.make_async_remote_copy(
            src_ref=src, dst_ref=dst, send_sem=send, recv_sem=recv,
            device_id=(to_c, to_f), device_id_type=MESH,
        )

    def exists(piece, sign):
        to_c, to_f = c + sign * piece[2], f + sign * piece[3]
        return (to_c >= 0) & (to_c < NC) & (to_f >= 0) & (to_f < NF)

    def is_cin(k):
        return (k >= 0) & (k < NC)

    def halo_copy(j):
        first, rows, dc, df = PIECES[j]
        at = pl.ds(first, rows)
        return remote(sb.at[at], halo.at[at], halo_s.at[j], halo_r.at[j], c + dc, f + df)

    def g_copy(to, of):
        return remote(down, g.at[:, of], g_s.at[to], g_r.at[of], to, f)

    def dl_copy(to, of):
        return remote(dl.at[to], xx.at[1 + f, of], dl_s.at[to], dl_r.at[of], to, f)

    def at_z(to):
        return 4 * to + 2 * xh + core

    def across_copy(block):
        return remote(xx.at[1 + block], xx.at[1 + block], far_s.at[0], xx_r.at[block], c, across)

    def z_copy(to, block, k):
        return remote(xx.at[1 + block], xx.at[1 + block], xx_s.at[4 * k + to], xx_r.at[block], c, at_z(to))

    def mate_copy(block):
        return remote(xx.at[1 + block], xx.at[1 + block], fw_s.at[block], xx_r.at[block], c, mate)

    def pr_copy(k):
        return remote(r.at[k], pr.at[k], pr_s.at[k], pr_r.at[k], c, mate)

    def rr_copy(to):
        to_z, to_x = to // 2, lax.rem(to, 2)
        return remote(q.at[to], rr.at[to_x, z], rr_s.at[to], rr_r.at[4 * to_x + z], c, at_z(to_z))

    def rr_wait(x, of):
        remote(q.at[0], rr.at[x, of], rr_s.at[0], rr_r.at[4 * x + of], c, mate).wait_recv()

    def sum_copy():
        return remote(xsum, xgot, far_s.at[1], far_r.at[0], c, across)

    def ro_half(h):
        at = pl.ds(8 * h, 8)

        def ro_copy(to, of):
            return remote(po.at[to, at], ro.at[of, at], ro_s.at[8 * h + to], ro_r.at[8 * h + of], to, f)

        return ro_copy

    def w_copy(to, of):
        return remote(wl, wall.at[of], w_s.at[to], w_r.at[of], to, f)

    def a1_copy(to, of):
        return remote(ar1.at[of], ar1.at[of], a1_s.at[to], a1_r.at[of], to, f)

    def a2_copy(to, of):
        return remote(ar2.at[of], ar2.at[of], a2_s.at[to], a2_r.at[of], c, to)

    def each(count, me, act):
        @pl.loop(1, count)
        def _(k):
            act(lax.rem(me + k, count))

    def send(count, me, copy):
        each(count, me, lambda to: copy(to, me).start())

    def receive(count, me, copy):
        each(count, me, lambda of: copy(of, of).wait_recv())

    def sent(count, me, copy):
        each(count, me, lambda to: copy(to, me).wait_send())

    halo[...] = jnp.zeros_like(halo)

    barrier = pltpu.get_barrier_semaphore()

    def greet(to_c, to_f):
        pl.semaphore_signal(barrier, inc=1, device_id=(to_c, to_f), device_id_type=MESH)

    each(NC, c, lambda to: greet(to, f))
    each(NF, f, lambda to: greet(c, to))
    expected = NC + NF - 2
    for piece in PIECES[4:]:
        there = exists(piece, 1)

        @pl.when(there)
        def _(piece=piece):
            greet(c + piece[2], f + piece[3])

        expected = expected + there.astype(jnp.int32)

    fetched(0, 3, 4)
    sb[...] = dot(sel[Q0:PERM0], vol[...]).astype(BF16)
    swapped = dot(sel[SWAP0:EYE0], dout[...]).astype(BF16).reshape(16, 16, 128)
    down[...] = swapped
    g[:, pl.ds(c, 1)] = swapped[:, None]
    xx[0] = jnp.zeros(xx.shape[1:], BF16)
    xx[17] = jnp.zeros(xx.shape[1:], BF16)
    for k in range(3):
        gs[k, 0] = jnp.zeros(gs.shape[2:], BF16)
        gs[k, 17] = jnp.zeros(gs.shape[2:], BF16)

    fetched(2)
    turned = dot_t(sel[EYE0 : EYE0 + 32, :32], wdt[...]).astype(BF16)
    wl[:, :432] = turned
    wl[:, 432:] = jnp.zeros((32, 80), BF16)

    pl.semaphore_wait(barrier, expected)
    for j, piece in enumerate(PIECES):

        @pl.when(exists(piece, 1))
        def _(j=j):
            halo_copy(j).start()

    for step in (1, -1):

        @pl.when(is_cin(c + step))
        def _(step=step):
            g_copy(c + step, c).start()

    send(NC, c, w_copy)
    wall[c] = wl[...]

    fetched(1, 6)
    rows = jnp.concatenate([wet[...].astype(F32).reshape(108, 16), jnp.zeros((20, 16), F32)], 0)
    early = dot_t(sel[EYE0 : EYE0 + 16, :16], rows.astype(BF16)).astype(BF16)
    for y in range(8):
        te[y * 16 : (y + 1) * 16, :] = dot(early, taps[:, y * 512 : (y + 1) * 512]).astype(BF16)

    for j, piece in enumerate(PIECES):

        @pl.when(exists(piece, -1))
        def _(j=j):
            halo_copy(j).wait_recv()

    fetched(5)
    cells = dot(slab[:, :256], vol[...]) + dot(slab[:, 256:448], halo[...])
    for k, shifted in enumerate((moved(cells, 1), cells, moved(cells, -1))):
        shifted = shifted.astype(BF16)
        for xs in range(10):
            vs[xs * 144 + k * 48 : xs * 144 + k * 48 + 48, :] = shifted[xs * 48 : xs * 48 + 48]
    vs[1440:1584, :] = jnp.zeros((144, 256), BF16)

    @pl.loop(0, 4)
    def _(a):
        total = jnp.zeros((128, 256), F32)
        for x in range(2):
            at = pl.multiple_of((2 * a + x) * 144, 16)
            pre = dot(te[...], vs[pl.ds(at, 512), :])
            factor = jnp.where(pre > 0, 1.0, slope)
            fac[2 * a + x] = factor
            total += pre * factor
        for b in range(4):
            pooled[a, b * 16 : b * 16 + 16] = (
                total[b * 32 : b * 32 + 16] + total[b * 32 + 16 : b * 32 + 32]
            )

    pair = sel[PAIR0:END0]
    field = pooled[...].reshape(256, 256)
    high = field.astype(BF16)
    low = (field - high.astype(F32)).astype(BF16)
    means = ((dot_t(high, pair) + dot_t(low, pair)) * 0.125).astype(BF16)
    local = dot(sel[PERM0:UP0], means).astype(BF16).reshape(8, 32, 128)
    dl[...] = local
    send(NC, c, dl_copy)
    xx[1 + f, c] = dl[c]

    def far(k):
        return (k < c - 1) | (k > c + 1)

    @pl.loop(0, NC)
    def _(to):
        @pl.when(far(to))
        def _():
            g_copy(to, c).start()

    receive(NC, c, w_copy)
    for a in range(3):
        of = c + 1 - a
        if a != 1:

            @pl.when(is_cin(of))
            def _(of=of):
                g_copy(of, of).wait_recv()

            @pl.when(jnp.logical_not(is_cin(of)))
            def _(a=a):
                gh[a] = jnp.zeros(gh.shape[1:], BF16)

        @pl.when(is_cin(of))
        def _(a=a, of=of):
            plain = g[:, pl.ds(of, 1)].reshape(256, 128)
            wide = plain.astype(F32)
            parts = (moved(wide, -1).astype(BF16), plain, moved(wide, 1).astype(BF16))
            for v in range(16):
                for k in range(3):
                    gh[a, 16 - v, k * 16 : k * 16 + 16] = parts[k][v * 16 : v * 16 + 16]

            for edge in (0, 17):
                gh[a, edge] = jnp.zeros((48, 128), BF16)

    def chip_at(k):
        return 2 * lax.rem(z + 1 + k, 4) + lax.rem(xh + 1 + k // 4, 2)

    def combine(k):
        to = chip_at(k)
        pr_copy(to).wait_recv()
        total = (own[to] + pr[to].astype(F32)).astype(BF16)

        @pl.when(to // 2 != z)
        def _():
            q[to] = total
            rr_copy(to).start()

        @pl.when(to // 2 == z)
        def _():
            rr[lax.rem(to, 2), z] = total

    def dgrad(k):
        to = chip_at(k)
        v = 2 * to
        low = [gh[a, pl.ds(15 - v, 3)].reshape(144, 128) for a in range(3)]
        high = [gh[a, pl.ds(14 - v, 3)].reshape(144, 128) for a in range(3)]
        both = jnp.concatenate([jnp.concatenate(low, 0), jnp.concatenate(high, 0)], 1)
        out = dot(wall[...].reshape(256, 512)[:, :432], both)
        first, second = out[:, :128], out[:, 128:]
        r[to] = jnp.where(core == 0, second, first).astype(BF16)
        pr_copy(to).start()
        own[to] = jnp.where(core == 0, first, second)

        @pl.when(k >= 2)
        def _():
            combine(k - 2)

    pl.loop(0, 6)(dgrad)
    receive(NC, c, dl_copy)
    across_copy(f).start()
    each(4, z, lambda to: z_copy(to, f, 0).start())
    mate_copy(f).start()
    pl.loop(6, 8)(dgrad)
    combine(6)
    combine(7)
    across_copy(across).wait_recv()
    each(4, z, lambda to: z_copy(to, across, 1).start())
    mate_copy(across).start()

    fetched(8)
    for u in range(8):
        columns = slice(u * 256, (u + 1) * 256)
        wide = dot(wdt[0:144], band[0:32, columns])
        wide += dot(wdt[144:288], band[32:64, columns])
        wide += dot(wdt[288:432], band[64:96, columns])
        wide = wide.astype(BF16)
        for b in range(3):
            for k in range(3):
                block = wide[(b * 3 + k) * 16 : (b * 3 + k) * 16 + 16]
                tw[k, u * 16 : u * 16 + 16, b * 256 : (b + 1) * 256] = block

    @pl.loop(0, NC)
    def _(of):
        @pl.when(far(of))
        def _():
            g_copy(of, of).wait_recv()

    @pl.loop(0, 16)
    def _(v):
        plain = g[v].reshape(128, 128)
        wide = plain.astype(F32)
        gs[0, v + 1] = moved(wide, -1).astype(BF16)
        gs[1, v + 1] = plain
        gs[2, v + 1] = moved(wide, 1).astype(BF16)

    def summed(x):
        each(4, z, lambda of: rr_wait(x, of))
        total = rr[x, 0].astype(F32)
        for k in range(1, 4):
            total += rr[x, k].astype(F32)
        return total

    xsum[...] = summed(1 - xh).astype(BF16)
    sum_copy().start()
    for x in range(2):
        side = f if x else across

        def pass_on(of, side=side):
            block = 4 * of + lax.rem(side, 4)
            z_copy(of, block, 0).wait_recv()
            mate_copy(block).start()

        each(4, z, pass_on)

    total = summed(xh)
    sum_copy().wait_recv()
    total += xgot[...].astype(F32)
    spread = dot(sel[UP0:SWAP0], total.astype(BF16)).astype(BF16)
    up[...] = (dot(spread, pair) * 0.125).reshape(4, 128, 256)
    ae[...] = jnp.zeros_like(ae)

    @pl.loop(0, 4)
    def _(a):
        for x in range(2):
            at = pl.multiple_of((2 * a + x) * 144, 16)
            grad = (up[a] * fac[2 * a + x]).astype(BF16)
            ae[...] += dot_t(grad, vs[pl.ds(at, 512), :])

    rest = jnp.concatenate([ae[y * 16 : (y + 1) * 16] for y in range(8)], 1)
    pieces = []
    for _ in range(3):
        pieces.append(rest.astype(BF16))
        rest = rest - pieces[-1].astype(F32)
    fetched(7)
    mine = dot(jnp.concatenate(pieces, 0), back[...])
    mine = mine[:16] + mine[16:32] + mine[32:]
    ar1[c] = mine
    send(NC, c, a1_copy)

    @pl.loop(0, 8)
    def _(k):
        mate_copy(2 * k + 1 - core).wait_recv()

    def pair_of_rows(v):
        return jnp.concatenate(
            [xx[pl.ds(v, 3)].reshape(768, 128), xx[pl.ds(v + 1, 3)].reshape(768, 128)], 1
        )

    def forward(k):
        v = 2 * k
        out = dot(tw[...].reshape(384, 768), pair_of_rows(v))
        for h in range(2):
            half = out[:, h * 128 : (h + 1) * 128]
            total = moved(half[:128], 1) + half[128:256] + moved(half[256:], -1)
            po[:, v + h] = total.astype(BF16).reshape(8, 16, 128)

    pl.loop(0, 4)(forward)
    send(NC, c, ro_half(0))
    pl.loop(4, 8)(forward)
    send(NC, c, ro_half(1))
    ro[c] = po[c]

    receive(NC, c, a1_copy)
    total = ar1[0]
    for k in range(1, NC):
        total += ar1[k]
    ar2[f] = total
    send(NF, f, a2_copy)

    acc[...] = jnp.zeros_like(acc)

    @pl.loop(0, 8)
    def _(k):
        v = 2 * k
        both = jnp.concatenate(
            [gs[:, v + 1].reshape(384, 128), gs[:, v + 2].reshape(384, 128)], 1
        )
        acc[...] += dot_t(both, pair_of_rows(v))

    receive(NC, c, ro_half(0))
    receive(NC, c, ro_half(1))
    total = ro[0].astype(F32)
    for k in range(1, NC):
        total += ro[k].astype(F32)
    rounded = total.astype(BF16).reshape(256, 128)
    deep_out[...] = dot(sel[SWAP0:EYE0], rounded).astype(BF16)

    lane = lax.broadcasted_iota(jnp.int32, (16, 256), 1)
    for k in range(3):
        for b in range(3):
            total = jnp.zeros((16, 256), F32)
            for u in range(8):
                rows = acc[k * 128 + u * 16 : k * 128 + u * 16 + 16, b * 256 : (b + 1) * 256]
                rows = pltpu.roll(rows, (-(u - 1) * 32) % 256, 1) if u != 1 else rows
                if u == 0:
                    rows = jnp.where(lane < 32, 0.0, rows)
                if u == 7:
                    rows = jnp.where(lane >= 64, 0.0, rows)
                total += rows
            for a in range(3):
                at = ((a * 3 + b) * 3 + k) * 16
                grad_deep[at : at + 16, :] = total[:, a * 32 : (a + 1) * 32]

    receive(NF, f, a2_copy)
    total = ar2[0]
    for k in range(1, NF):
        total += ar2[k]
    square = jnp.concatenate([total, jnp.zeros((112, 128), F32)], 0)
    grad_early[...] = square.T[:108, :16].reshape(27, 4, 16)

    for j, piece in enumerate(PIECES):

        @pl.when(exists(piece, 1))
        def _(j=j):
            halo_copy(j).wait_send()

    sent(NC, c, g_copy)
    sent(NC, c, dl_copy)
    across_copy(f).wait_send()
    sum_copy().wait_send()
    for k in range(2):
        each(4, z, lambda to, k=k: z_copy(to, f, k).wait_send())
        each(4, z, lambda to, k=k: rr_copy(2 * to + k).wait_send())

    @pl.loop(0, 8)
    def _(k):
        mate_copy(2 * k + core).wait_send()
        pr_copy(k).wait_send()

    sent(NC, c, ro_half(0))
    sent(NC, c, ro_half(1))
    sent(NC, c, w_copy)
    sent(NC, c, a1_copy)
    sent(NF, f, a2_copy)


SCRATCH = (
    ((192, 256), BF16), ((192, 256), BF16), ((1584, 256), BF16), ((128, 512), BF16),
    ((8, 128, 256), F32), ((4, 64, 256), F32), ((8, 32, 128), BF16), ((18, 8, 32, 128), BF16),
    ((16, 16, 128), BF16), ((16, 8, 16, 128), BF16), ((3, 18, 128, 128), BF16), ((3, 18, 48, 128), BF16),
    ((32, 512), BF16), ((8, 32, 512), BF16), ((3, 128, 768), BF16), ((8, 256, 128), F32), ((8, 256, 128), BF16),
    ((8, 256, 128), BF16), ((8, 256, 128), BF16), ((2, 4, 256, 128), BF16),
    ((8, 16, 16, 128), BF16), ((8, 16, 16, 128), BF16),
    ((4, 128, 256), F32), ((128, 512), F32), ((384, 768), F32), ((8, 16, 128), F32), ((16, 16, 128), F32),
    ((256, 128), BF16), ((256, 128), BF16),
)
SEMAPHORES = (9, 8, 8, 8, 8, 8, 8, 8, 16, 2, 1, 16, 8, 8, 8, 8, 16, 16, 8, 8, 8, 8, 16, 16)
OPERANDS = (
    (256, 256), (27, 4, 16), (432, 32), (256, 128), (END0, 256), (480, 512), (128, 4096), (4096, 128), (96, 2048),
)


def hand_on(*refs):
    given, results, held, sems = refs[:3], refs[3:6], refs[6:9], refs[9]
    into = [pltpu.make_async_copy(given[k], held[k], sems.at[k]) for k in range(3)]
    out = [pltpu.make_async_copy(held[k], results[k], sems.at[3 + k]) for k in range(3)]
    for copy in into:
        copy.start()
    for k in range(3):
        into[k].wait()
        out[k].start()
    for copy in out:
        copy.wait()


def local(volume, early_w, deep_w, d_out):
    operands = [
        volume.reshape(256, 256),
        early_w.transpose(2, 3, 4, 1, 0).reshape(27, 4, 16),
        deep_w.transpose(2, 3, 4, 0, 1).reshape(432, 32),
        d_out.reshape(256, 128),
        *[jnp.asarray(t) for t in tables()],
    ]
    results = pl.pallas_call(
        kernel,
        out_shape=(
            jax.ShapeDtypeStruct((256, 128), BF16),
            jax.ShapeDtypeStruct((432, 32), F32),
            jax.ShapeDtypeStruct((27, 4, 16), F32),
        ),
        in_specs=[pl.BlockSpec(memory_space=pltpu.HBM)] * len(operands),
        out_specs=[pl.BlockSpec(memory_space=pltpu.VMEM)] * 3,
        scratch_shapes=[pltpu.VMEM(shape, BF16) for shape in OPERANDS]
        + [pltpu.VMEM(shape, dtype) for shape, dtype in SCRATCH]
        + [pltpu.SemaphoreType.DMA((count,)) for count in SEMAPHORES],
        compiler_params=pltpu.CompilerParams(
            collective_id=0, has_side_effects=True, vmem_limit_bytes=60 << 20
        ),
        name="cosmo",
    )(*operands)
    deep_out, grad_deep, grad_early = pl.pallas_call(
        hand_on,
        out_shape=[jax.ShapeDtypeStruct(x.shape, x.dtype) for x in results],
        in_specs=[pl.BlockSpec(memory_space=pl.ANY)] * 3,
        out_specs=[pl.BlockSpec(memory_space=pl.ANY)] * 3,
        scratch_shapes=[pltpu.VMEM(x.shape, x.dtype) for x in results]
        + [pltpu.SemaphoreType.DMA((6,))],
        name="results",
    )(*results)
    return (
        deep_out.reshape(16, 1, 16, 128),
        grad_deep.reshape(3, 3, 3, 16, 32).transpose(3, 4, 0, 1, 2),
        grad_early.reshape(3, 3, 3, 4, 16).transpose(4, 3, 0, 1, 2),
    )


def solution(mesh):
    in_specs = (
        P(None, "cin", "flt", None),
        P(),
        P("flt", "cin", None, None, None),
        P("flt", "cin", None, None),
    )
    out_specs = (P("flt", "cin", None, None), P("flt", "cin", None, None, None), P())
    return jax.shard_map(local, mesh=mesh, in_specs=in_specs, out_specs=out_specs, check_vma=False)
```

```python
import jax
import jax.numpy as jnp
import ml_dtypes
import numpy as np
from jax import lax
from jax.experimental import pallas as pl
from jax.experimental.pallas import tpu as pltpu
from jax.sharding import PartitionSpec as P

MESH = pl.DeviceIdType.MESH
F32, BF16 = jnp.float32, jnp.bfloat16
slope = 0.3
NC, NF = 8, 16

PIECES = (
    (0, 32, 1, 0), (32, 32, -1, 0), (64, 32, 0, 1), (96, 32, 0, -1),
    (128, 16, 1, 1), (144, 16, 1, -1), (160, 16, -1, 1), (176, 16, -1, -1),
)
Q0, PERM0, UP0, SWAP0, EYE0, PAIR0, END0 = 0, 192, 448, 960, 1216, 1472, 1600


def tables():
    sel = np.zeros((END0, 256), np.float32)
    for i in range(4):
        for y in range(8):
            sel[Q0 + i * 8 + y, i * 64 + 56 + y] = 1
            sel[Q0 + 32 + i * 8 + y, i * 64 + y] = 1
        for x in range(8):
            sel[Q0 + 64 + x * 4 + i, i * 64 + x * 8 + 7] = 1
            sel[Q0 + 96 + x * 4 + i, i * 64 + x * 8] = 1
        sel[Q0 + 128 + i, i * 64 + 63] = 1
        sel[Q0 + 144 + i, i * 64 + 56] = 1
        sel[Q0 + 160 + i, i * 64 + 7] = 1
        sel[Q0 + 176 + i, i * 64] = 1
    for a in range(4):
        for e in range(16):
            for b in range(4):
                sel[PERM0 + 16 * e + 4 * a + b, a * 64 + b * 16 + e] = 1
            for y in range(8):
                sel[UP0 + a * 128 + y * 16 + e, 16 * e + 4 * a + y // 2] = 1
    for v in range(16):
        for o in range(16):
            sel[SWAP0 + v * 16 + o, o * 16 + v] = 1
    sel[EYE0 : EYE0 + 256] = np.eye(256)
    for z in range(256):
        sel[PAIR0 + z // 2, z] = 1

    slab = np.zeros((480, 512), np.float32)
    for xs in range(10):
        x = xs - 1
        for i in range(4):
            for y in range(8):
                column = i * 64 + x * 8 + y if 0 <= x < 8 else 256 + (32 if x == 8 else 0) + i * 8 + y
                slab[xs * 48 + i * 8 + y, column] = 1
            low, high = (320 + x * 4, 352 + x * 4) if 0 <= x < 8 else ((384, 400) if x < 0 else (416, 432))
            slab[xs * 48 + 32 + i, low + i] = 1
            slab[xs * 48 + 36 + i, high + i] = 1

    taps = np.zeros((128, 8 * 512), np.float32)
    for y in range(8):
        for a in range(3):
            for b in range(3):
                for c in range(3):
                    for i in range(4):
                        row = y + b - 1
                        k = 32 + i if row < 0 else 36 + i if row > 7 else i * 8 + row
                        taps[(a * 9 + b * 3 + c) * 4 + i, y * 512 + a * 144 + c * 48 + k] = 1

    band = np.zeros((96, 8 * 256), np.float32)
    for u in range(8):
        for a in range(3):
            if 0 <= u + a - 1 < 8:
                for i in range(32):
                    band[a * 32 + i, u * 256 + (u + a - 1) * 32 + i] = 1
    return [t.astype(ml_dtypes.bfloat16) for t in (sel, slab, taps, taps.T, band)]


def dot(a, b):
    return jnp.dot(a, b, preferred_element_type=F32)


def dot_t(a, b):
    return lax.dot_general(a, b, (((1,), (1,)), ((), ())), preferred_element_type=F32)


def moved(value, step):
    width = value.shape[1]
    lane = lax.broadcasted_iota(jnp.int32, value.shape, 1)
    edge = 0 if step > 0 else width - 1
    return jnp.where(lane == edge, 0.0, pltpu.roll(value, step % width, 1))


def kernel(*refs):
    count = len(OPERANDS)
    given, refs = refs[:count], refs[count:]
    deep_out, grad_deep, grad_early = refs[:3]
    here, refs = refs[3 : 3 + count], refs[3 + count :]
    vol, wet, wdt, dout, sel, slab, taps, back, band = here
    (sb, halo, vs, te, fac, pooled, dl, xx, down, g, gs, gh, wl, wall, tw, own, r, pr, q, rr, po, ro, up, ae, acc,
     ar1, ar2, xsum, xgot) = refs[: len(SCRATCH)]
    (got, halo_s, halo_r, g_s, g_r, dl_s, dl_r, xx_s, xx_r, far_s, far_r, fw_s, pr_s, pr_r, rr_s, rr_r, ro_s, ro_r, w_s, w_r,
     a1_s, a1_r, a2_s, a2_r) = refs[len(SCRATCH) :]

    fetches = [pltpu.make_async_copy(given[k], here[k], got.at[k]) for k in range(count)]
    for k in (0, 3, 4, 2, 1, 6, 5, 8, 7):
        fetches[k].start()

    def fetched(*which):
        for k in which:
            fetches[k].wait()

    c, f = lax.axis_index("cin"), lax.axis_index("flt")
    chip, core = f // 2, lax.rem(f, 2)
    mate = f + 1 - 2 * core
    z, xh = chip // 2, lax.rem(chip, 2)
    across = f + 2 - 4 * xh

    def remote(src, dst, send, recv, to_c, to_f):
        return pltpu.make_async_remote_copy(
            src_ref=src, dst_ref=dst, send_sem=send, recv_sem=recv,
            device_id=(to_c, to_f), device_id_type=MESH,
        )

    def exists(piece, sign):
        to_c, to_f = c + sign * piece[2], f + sign * piece[3]
        return (to_c >= 0) & (to_c < NC) & (to_f >= 0) & (to_f < NF)

    def is_cin(k):
        return (k >= 0) & (k < NC)

    def halo_copy(j):
        first, rows, dc, df = PIECES[j]
        at = pl.ds(first, rows)
        return remote(sb.at[at], halo.at[at], halo_s.at[j], halo_r.at[j], c + dc, f + df)

    def g_copy(to, of):
        return remote(down, g.at[:, of], g_s.at[to], g_r.at[of], to, f)

    def dl_copy(to, of):
        return remote(dl.at[to], xx.at[1 + f, of], dl_s.at[to], dl_r.at[of], to, f)

    def at_z(to):
        return 4 * to + 2 * xh + core

    def across_copy(block):
        return remote(xx.at[1 + block], xx.at[1 + block], far_s.at[0], xx_r.at[block], c, across)

    def z_copy(to, block, k):
        return remote(xx.at[1 + block], xx.at[1 + block], xx_s.at[4 * k + to], xx_r.at[block], c, at_z(to))

    def mate_copy(block):
        return remote(xx.at[1 + block], xx.at[1 + block], fw_s.at[block], xx_r.at[block], c, mate)

    def pr_copy(k):
        return remote(r.at[k], pr.at[k], pr_s.at[k], pr_r.at[k], c, mate)

    def rr_copy(to):
        to_z, to_x = to // 2, lax.rem(to, 2)
        return remote(q.at[to], rr.at[to_x, z], rr_s.at[to], rr_r.at[4 * to_x + z], c, at_z(to_z))

    def rr_wait(x, of):
        remote(q.at[0], rr.at[x, of], rr_s.at[0], rr_r.at[4 * x + of], c, mate).wait_recv()

    def sum_copy():
        return remote(xsum, xgot, far_s.at[1], far_r.at[0], c, across)

    def ro_half(h):
        at = pl.ds(8 * h, 8)

        def ro_copy(to, of):
            return remote(po.at[to, at], ro.at[of, at], ro_s.at[8 * h + to], ro_r.at[8 * h + of], to, f)

        return ro_copy

    def w_copy(to, of):
        return remote(wl, wall.at[of], w_s.at[to], w_r.at[of], to, f)

    def a1_copy(to, of):
        return remote(ar1.at[of], ar1.at[of], a1_s.at[to], a1_r.at[of], c, to)

    def a2_copy(to, of):
        return remote(ar2.at[of], ar2.at[of], a2_s.at[to], a2_r.at[of], to, f)

    def each(count, me, act):
        @pl.loop(1, count)
        def _(k):
            act(lax.rem(me + k, count))

    def send(count, me, copy):
        each(count, me, lambda to: copy(to, me).start())

    def receive(count, me, copy):
        each(count, me, lambda of: copy(of, of).wait_recv())

    def sent(count, me, copy):
        each(count, me, lambda to: copy(to, me).wait_send())

    halo[...] = jnp.zeros_like(halo)

    barrier = pltpu.get_barrier_semaphore()

    def greet(to_c, to_f):
        pl.semaphore_signal(barrier, inc=1, device_id=(to_c, to_f), device_id_type=MESH)

    each(NC, c, lambda to: greet(to, f))
    each(NF, f, lambda to: greet(c, to))
    expected = NC + NF - 2
    for piece in PIECES[4:]:
        there = exists(piece, 1)

        @pl.when(there)
        def _(piece=piece):
            greet(c + piece[2], f + piece[3])

        expected = expected + there.astype(jnp.int32)

    fetched(0, 3, 4)
    sb[...] = dot(sel[Q0:PERM0], vol[...]).astype(BF16)
    swapped = dot(sel[SWAP0:EYE0], dout[...]).astype(BF16).reshape(16, 16, 128)
    down[...] = swapped
    g[:, pl.ds(c, 1)] = swapped[:, None]
    xx[0] = jnp.zeros(xx.shape[1:], BF16)
    xx[17] = jnp.zeros(xx.shape[1:], BF16)
    for k in range(3):
        gs[k, 0] = jnp.zeros(gs.shape[2:], BF16)
        gs[k, 17] = jnp.zeros(gs.shape[2:], BF16)

    fetched(2)
    turned = dot_t(sel[EYE0 : EYE0 + 32, :32], wdt[...]).astype(BF16)
    wl[:, :432] = turned
    wl[:, 432:] = jnp.zeros((32, 80), BF16)

    pl.semaphore_wait(barrier, expected)
    for j, piece in enumerate(PIECES):

        @pl.when(exists(piece, 1))
        def _(j=j):
            halo_copy(j).start()

    for step in (1, -1):

        @pl.when(is_cin(c + step))
        def _(step=step):
            g_copy(c + step, c).start()

    send(NC, c, w_copy)
    wall[c] = wl[...]

    fetched(1, 6)
    rows = jnp.concatenate([wet[...].astype(F32).reshape(108, 16), jnp.zeros((20, 16), F32)], 0)
    early = dot_t(sel[EYE0 : EYE0 + 16, :16], rows.astype(BF16)).astype(BF16)
    for y in range(8):
        te[y * 16 : (y + 1) * 16, :] = dot(early, taps[:, y * 512 : (y + 1) * 512]).astype(BF16)

    for j, piece in enumerate(PIECES):

        @pl.when(exists(piece, -1))
        def _(j=j):
            halo_copy(j).wait_recv()

    fetched(5)
    cells = dot(slab[:, :256], vol[...]) + dot(slab[:, 256:448], halo[...])
    for k, shifted in enumerate((moved(cells, 1), cells, moved(cells, -1))):
        shifted = shifted.astype(BF16)
        for xs in range(10):
            vs[xs * 144 + k * 48 : xs * 144 + k * 48 + 48, :] = shifted[xs * 48 : xs * 48 + 48]
    vs[1440:1584, :] = jnp.zeros((144, 256), BF16)

    @pl.loop(0, 4)
    def _(a):
        total = jnp.zeros((128, 256), F32)
        for x in range(2):
            at = pl.multiple_of((2 * a + x) * 144, 16)
            pre = dot(te[...], vs[pl.ds(at, 512), :])
            factor = jnp.where(pre > 0, 1.0, slope)
            fac[2 * a + x] = factor
            total += pre * factor
        for b in range(4):
            pooled[a, b * 16 : b * 16 + 16] = (
                total[b * 32 : b * 32 + 16] + total[b * 32 + 16 : b * 32 + 32]
            )

    pair = sel[PAIR0:END0]
    field = pooled[...].reshape(256, 256)
    high = field.astype(BF16)
    low = (field - high.astype(F32)).astype(BF16)
    means = ((dot_t(high, pair) + dot_t(low, pair)) * 0.125).astype(BF16)
    local = dot(sel[PERM0:UP0], means).astype(BF16).reshape(8, 32, 128)
    dl[...] = local
    send(NC, c, dl_copy)
    xx[1 + f, c] = dl[c]

    def far(k):
        return (k < c - 1) | (k > c + 1)

    @pl.loop(0, NC)
    def _(to):
        @pl.when(far(to))
        def _():
            g_copy(to, c).start()

    receive(NC, c, w_copy)
    for a in range(3):
        of = c + 1 - a
        if a != 1:

            @pl.when(is_cin(of))
            def _(of=of):
                g_copy(of, of).wait_recv()

            @pl.when(jnp.logical_not(is_cin(of)))
            def _(a=a):
                gh[a] = jnp.zeros(gh.shape[1:], BF16)

        @pl.when(is_cin(of))
        def _(a=a, of=of):
            plain = g[:, pl.ds(of, 1)].reshape(256, 128)
            wide = plain.astype(F32)
            parts = (moved(wide, -1).astype(BF16), plain, moved(wide, 1).astype(BF16))
            for v in range(16):
                for k in range(3):
                    gh[a, 16 - v, k * 16 : k * 16 + 16] = parts[k][v * 16 : v * 16 + 16]

            for edge in (0, 17):
                gh[a, edge] = jnp.zeros((48, 128), BF16)

    def chip_at(k):
        return 2 * lax.rem(z + 1 + k, 4) + lax.rem(xh + 1 + k // 4, 2)

    def combine(k):
        to = chip_at(k)
        pr_copy(to).wait_recv()
        total = (own[to] + pr[to].astype(F32)).astype(BF16)

        @pl.when(to // 2 != z)
        def _():
            q[to] = total
            rr_copy(to).start()

        @pl.when(to // 2 == z)
        def _():
            rr[lax.rem(to, 2), z] = total

    def dgrad(k):
        to = chip_at(k)
        v = 2 * to
        low = [gh[a, pl.ds(15 - v, 3)].reshape(144, 128) for a in range(3)]
        high = [gh[a, pl.ds(14 - v, 3)].reshape(144, 128) for a in range(3)]
        both = jnp.concatenate([jnp.concatenate(low, 0), jnp.concatenate(high, 0)], 1)
        out = dot(wall[...].reshape(256, 512)[:, :432], both)
        first, second = out[:, :128], out[:, 128:]
        r[to] = jnp.where(core == 0, second, first).astype(BF16)
        pr_copy(to).start()
        own[to] = jnp.where(core == 0, first, second)

        @pl.when(k >= 2)
        def _():
            combine(k - 2)

    pl.loop(0, 3)(dgrad)
    receive(NC, c, dl_copy)
    across_copy(f).start()
    each(4, z, lambda to: z_copy(to, f, 0).start())
    mate_copy(f).start()
    pl.loop(3, 8)(dgrad)
    combine(6)
    combine(7)
    across_copy(across).wait_recv()
    each(4, z, lambda to: z_copy(to, across, 1).start())
    mate_copy(across).start()

    fetched(8)
    for u in range(8):
        columns = slice(u * 256, (u + 1) * 256)
        wide = dot(wdt[0:144], band[0:32, columns])
        wide += dot(wdt[144:288], band[32:64, columns])
        wide += dot(wdt[288:432], band[64:96, columns])
        wide = wide.astype(BF16)
        for b in range(3):
            for k in range(3):
                block = wide[(b * 3 + k) * 16 : (b * 3 + k) * 16 + 16]
                tw[k, u * 16 : u * 16 + 16, b * 256 : (b + 1) * 256] = block

    @pl.loop(0, NC)
    def _(of):
        @pl.when(far(of))
        def _():
            g_copy(of, of).wait_recv()

    @pl.loop(0, 16)
    def _(v):
        plain = g[v].reshape(128, 128)
        wide = plain.astype(F32)
        gs[0, v + 1] = moved(wide, -1).astype(BF16)
        gs[1, v + 1] = plain
        gs[2, v + 1] = moved(wide, 1).astype(BF16)

    def summed(x):
        each(4, z, lambda of: rr_wait(x, of))
        total = rr[x, 0].astype(F32)
        for k in range(1, 4):
            total += rr[x, k].astype(F32)
        return total

    xsum[...] = summed(1 - xh).astype(BF16)
    sum_copy().start()
    for x in range(2):
        side = f if x else across

        def pass_on(of, side=side):
            block = 4 * of + lax.rem(side, 4)
            z_copy(of, block, 0).wait_recv()
            mate_copy(block).start()

        each(4, z, pass_on)

    @pl.loop(0, 8)
    def _(k):
        mate_copy(2 * k + 1 - core).wait_recv()

    def pair_of_rows(v):
        return jnp.concatenate(
            [xx[pl.ds(v, 3)].reshape(768, 128), xx[pl.ds(v + 1, 3)].reshape(768, 128)], 1
        )

    def forward(k):
        v = 2 * k
        out = dot(tw[...].reshape(384, 768), pair_of_rows(v))
        for h in range(2):
            half = out[:, h * 128 : (h + 1) * 128]
            total = moved(half[:128], 1) + half[128:256] + moved(half[256:], -1)
            po[:, v + h] = total.astype(BF16).reshape(8, 16, 128)

    pl.loop(0, 4)(forward)
    send(NC, c, ro_half(0))
    pl.loop(4, 8)(forward)
    send(NC, c, ro_half(1))
    ro[c] = po[c]

    total = summed(xh)
    sum_copy().wait_recv()
    total += xgot[...].astype(F32)
    spread = dot(sel[UP0:SWAP0], total.astype(BF16)).astype(BF16)
    up[...] = (dot(spread, pair) * 0.125).reshape(4, 128, 256)
    ae[...] = jnp.zeros_like(ae)

    @pl.loop(0, 4)
    def _(a):
        for x in range(2):
            at = pl.multiple_of((2 * a + x) * 144, 16)
            grad = (up[a] * fac[2 * a + x]).astype(BF16)
            ae[...] += dot_t(grad, vs[pl.ds(at, 512), :])

    rest = jnp.concatenate([ae[y * 16 : (y + 1) * 16] for y in range(8)], 1)
    pieces = []
    for _ in range(3):
        pieces.append(rest.astype(BF16))
        rest = rest - pieces[-1].astype(F32)
    fetched(7)
    mine = dot(jnp.concatenate(pieces, 0), back[...])
    mine = mine[:16] + mine[16:32] + mine[32:]
    ar1[f] = mine
    send(NF, f, a1_copy)

    receive(NF, f, a1_copy)
    total = ar1[0]
    for k in range(1, NF):
        total += ar1[k]
    ar2[c] = total
    send(NC, c, a2_copy)

    acc[...] = jnp.zeros_like(acc)

    @pl.loop(0, 8)
    def _(k):
        v = 2 * k
        both = jnp.concatenate(
            [gs[:, v + 1].reshape(384, 128), gs[:, v + 2].reshape(384, 128)], 1
        )
        acc[...] += dot_t(both, pair_of_rows(v))

    receive(NC, c, ro_half(0))
    receive(NC, c, ro_half(1))
    total = ro[0].astype(F32)
    for k in range(1, NC):
        total += ro[k].astype(F32)
    rounded = total.astype(BF16).reshape(256, 128)
    deep_out[...] = dot(sel[SWAP0:EYE0], rounded).astype(BF16)

    lane = lax.broadcasted_iota(jnp.int32, (16, 256), 1)
    for k in range(3):
        for b in range(3):
            total = jnp.zeros((16, 256), F32)
            for u in range(8):
                rows = acc[k * 128 + u * 16 : k * 128 + u * 16 + 16, b * 256 : (b + 1) * 256]
                rows = pltpu.roll(rows, (-(u - 1) * 32) % 256, 1) if u != 1 else rows
                if u == 0:
                    rows = jnp.where(lane < 32, 0.0, rows)
                if u == 7:
                    rows = jnp.where(lane >= 64, 0.0, rows)
                total += rows
            for a in range(3):
                at = ((a * 3 + b) * 3 + k) * 16
                grad_deep[at : at + 16, :] = total[:, a * 32 : (a + 1) * 32]

    receive(NC, c, a2_copy)
    total = ar2[0]
    for k in range(1, NC):
        total += ar2[k]
    square = jnp.concatenate([total, jnp.zeros((112, 128), F32)], 0)
    grad_early[...] = square.T[:108, :16].reshape(27, 4, 16)

    for j, piece in enumerate(PIECES):

        @pl.when(exists(piece, 1))
        def _(j=j):
            halo_copy(j).wait_send()

    sent(NC, c, g_copy)
    sent(NC, c, dl_copy)
    across_copy(f).wait_send()
    sum_copy().wait_send()
    for k in range(2):
        each(4, z, lambda to, k=k: z_copy(to, f, k).wait_send())
        each(4, z, lambda to, k=k: rr_copy(2 * to + k).wait_send())

    @pl.loop(0, 8)
    def _(k):
        mate_copy(2 * k + core).wait_send()
        pr_copy(k).wait_send()

    sent(NC, c, ro_half(0))
    sent(NC, c, ro_half(1))
    sent(NC, c, w_copy)
    sent(NF, f, a1_copy)
    sent(NC, c, a2_copy)


SCRATCH = (
    ((192, 256), BF16), ((192, 256), BF16), ((1584, 256), BF16), ((128, 512), BF16),
    ((8, 128, 256), F32), ((4, 64, 256), F32), ((8, 32, 128), BF16), ((18, 8, 32, 128), BF16),
    ((16, 16, 128), BF16), ((16, 8, 16, 128), BF16), ((3, 18, 128, 128), BF16), ((3, 18, 48, 128), BF16),
    ((32, 512), BF16), ((8, 32, 512), BF16), ((3, 128, 768), BF16), ((8, 256, 128), F32), ((8, 256, 128), BF16),
    ((8, 256, 128), BF16), ((8, 256, 128), BF16), ((2, 4, 256, 128), BF16),
    ((8, 16, 16, 128), BF16), ((8, 16, 16, 128), BF16),
    ((4, 128, 256), F32), ((128, 512), F32), ((384, 768), F32), ((16, 16, 128), F32), ((8, 16, 128), F32),
    ((256, 128), BF16), ((256, 128), BF16),
)
SEMAPHORES = (9, 8, 8, 8, 8, 8, 8, 8, 16, 2, 1, 16, 8, 8, 8, 8, 16, 16, 8, 8, 16, 16, 8, 8)
OPERANDS = (
    (256, 256), (27, 4, 16), (432, 32), (256, 128), (END0, 256), (480, 512), (128, 4096), (4096, 128), (96, 2048),
)


def hand_on(*refs):
    given, results, held, sems = refs[:3], refs[3:6], refs[6:9], refs[9]
    into = [pltpu.make_async_copy(given[k], held[k], sems.at[k]) for k in range(3)]
    out = [pltpu.make_async_copy(held[k], results[k], sems.at[3 + k]) for k in range(3)]
    for copy in into:
        copy.start()
    for k in range(3):
        into[k].wait()
        out[k].start()
    for copy in out:
        copy.wait()


def local(volume, early_w, deep_w, d_out):
    operands = [
        volume.reshape(256, 256),
        early_w.transpose(2, 3, 4, 1, 0).reshape(27, 4, 16),
        deep_w.transpose(2, 3, 4, 0, 1).reshape(432, 32),
        d_out.reshape(256, 128),
        *[jnp.asarray(t) for t in tables()],
    ]
    results = pl.pallas_call(
        kernel,
        out_shape=(
            jax.ShapeDtypeStruct((256, 128), BF16),
            jax.ShapeDtypeStruct((432, 32), F32),
            jax.ShapeDtypeStruct((27, 4, 16), F32),
        ),
        in_specs=[pl.BlockSpec(memory_space=pltpu.HBM)] * len(operands),
        out_specs=[pl.BlockSpec(memory_space=pltpu.VMEM)] * 3,
        scratch_shapes=[pltpu.VMEM(shape, BF16) for shape in OPERANDS]
        + [pltpu.VMEM(shape, dtype) for shape, dtype in SCRATCH]
        + [pltpu.SemaphoreType.DMA((count,)) for count in SEMAPHORES],
        compiler_params=pltpu.CompilerParams(
            collective_id=0, has_side_effects=True, vmem_limit_bytes=60 << 20
        ),
        name="cosmo",
    )(*operands)
    deep_out, grad_deep, grad_early = pl.pallas_call(
        hand_on,
        out_shape=[jax.ShapeDtypeStruct(x.shape, x.dtype) for x in results],
        in_specs=[pl.BlockSpec(memory_space=pl.ANY)] * 3,
        out_specs=[pl.BlockSpec(memory_space=pl.ANY)] * 3,
        scratch_shapes=[pltpu.VMEM(x.shape, x.dtype) for x in results]
        + [pltpu.SemaphoreType.DMA((6,))],
        name="results",
    )(*results)
    return (
        deep_out.reshape(16, 1, 16, 128),
        grad_deep.reshape(3, 3, 3, 16, 32).transpose(3, 4, 0, 1, 2),
        grad_early.reshape(3, 3, 3, 4, 16).transpose(4, 3, 0, 1, 2),
    )


def solution(mesh):
    in_specs = (
        P(None, "cin", "flt", None),
        P(),
        P("flt", "cin", None, None, None),
        P("flt", "cin", None, None),
    )
    out_specs = (P("flt", "cin", None, None), P("flt", "cin", None, None, None), P())
    return jax.shard_map(local, mesh=mesh, in_specs=in_specs, out_specs=out_specs, check_vma=False)
```

```python
import jax
import jax.numpy as jnp
import ml_dtypes
import numpy as np
from jax import lax
from jax.experimental import pallas as pl
from jax.experimental.pallas import tpu as pltpu
from jax.sharding import PartitionSpec as P

MESH = pl.DeviceIdType.MESH
F32, BF16 = jnp.float32, jnp.bfloat16
slope = 0.3
NC, NF = 8, 16

PIECES = (
    (0, 32, 1, 0), (32, 32, -1, 0), (64, 32, 0, 1), (96, 32, 0, -1),
    (128, 16, 1, 1), (144, 16, 1, -1), (160, 16, -1, 1), (176, 16, -1, -1),
)
Q0, PERM0, UP0, SWAP0, EYE0, PAIR0, END0 = 0, 192, 448, 960, 1216, 1472, 1600


def tables():
    sel = np.zeros((END0, 256), np.float32)
    for i in range(4):
        for y in range(8):
            sel[Q0 + i * 8 + y, i * 64 + 56 + y] = 1
            sel[Q0 + 32 + i * 8 + y, i * 64 + y] = 1
        for x in range(8):
            sel[Q0 + 64 + x * 4 + i, i * 64 + x * 8 + 7] = 1
            sel[Q0 + 96 + x * 4 + i, i * 64 + x * 8] = 1
        sel[Q0 + 128 + i, i * 64 + 63] = 1
        sel[Q0 + 144 + i, i * 64 + 56] = 1
        sel[Q0 + 160 + i, i * 64 + 7] = 1
        sel[Q0 + 176 + i, i * 64] = 1
    for a in range(4):
        for e in range(16):
            for b in range(4):
                sel[PERM0 + 16 * e + 4 * a + b, a * 64 + b * 16 + e] = 1
            for y in range(8):
                sel[UP0 + a * 128 + y * 16 + e, 16 * e + 4 * a + y // 2] = 1
    for v in range(16):
        for o in range(16):
            sel[SWAP0 + v * 16 + o, o * 16 + v] = 1
    sel[EYE0 : EYE0 + 256] = np.eye(256)
    for z in range(256):
        sel[PAIR0 + z // 2, z] = 1

    slab = np.zeros((480, 512), np.float32)
    for xs in range(10):
        x = xs - 1
        for i in range(4):
            for y in range(8):
                column = i * 64 + x * 8 + y if 0 <= x < 8 else 256 + (32 if x == 8 else 0) + i * 8 + y
                slab[xs * 48 + i * 8 + y, column] = 1
            low, high = (320 + x * 4, 352 + x * 4) if 0 <= x < 8 else ((384, 400) if x < 0 else (416, 432))
            slab[xs * 48 + 32 + i, low + i] = 1
            slab[xs * 48 + 36 + i, high + i] = 1

    taps = np.zeros((128, 8 * 512), np.float32)
    for y in range(8):
        for a in range(3):
            for b in range(3):
                for c in range(3):
                    for i in range(4):
                        row = y + b - 1
                        k = 32 + i if row < 0 else 36 + i if row > 7 else i * 8 + row
                        taps[(a * 9 + b * 3 + c) * 4 + i, y * 512 + a * 144 + c * 48 + k] = 1

    band = np.zeros((96, 8 * 256), np.float32)
    for u in range(8):
        for a in range(3):
            if 0 <= u + a - 1 < 8:
                for i in range(32):
                    band[a * 32 + i, u * 256 + (u + a - 1) * 32 + i] = 1
    return [t.astype(ml_dtypes.bfloat16) for t in (sel, slab, taps, taps.T, band)]


def dot(a, b):
    return jnp.dot(a, b, preferred_element_type=F32)


def dot_t(a, b):
    return lax.dot_general(a, b, (((1,), (1,)), ((), ())), preferred_element_type=F32)


def moved(value, step):
    width = value.shape[1]
    lane = lax.broadcasted_iota(jnp.int32, value.shape, 1)
    edge = 0 if step > 0 else width - 1
    return jnp.where(lane == edge, 0.0, pltpu.roll(value, step % width, 1))


def kernel(*refs):
    count = len(OPERANDS)
    given, refs = refs[:count], refs[count:]
    deep_out, grad_deep, grad_early = refs[:3]
    here, refs = refs[3 : 3 + count], refs[3 + count :]
    vol, wet, wdt, dout, sel, slab, taps, back, band = here
    (sb, halo, vs, te, fac, pooled, dl, xx, down, g, gs, gh, wl, wall, tw, own, r, pr, q, rr, po, ro, up, ae, acc,
     ar1, ar2, xsum, xgot) = refs[: len(SCRATCH)]
    (got, halo_s, halo_r, g_s, g_r, dl_s, dl_r, xx_s, xx_r, far_s, far_r, fw_s, pr_s, pr_r, rr_s, rr_r, ro_s, ro_r, w_s, w_r,
     a1_s, a1_r, a2_s, a2_r) = refs[len(SCRATCH) :]

    fetches = [pltpu.make_async_copy(given[k], here[k], got.at[k]) for k in range(count)]
    for k in (0, 3, 4, 2, 1, 6, 5, 8, 7):
        fetches[k].start()

    def fetched(*which):
        for k in which:
            fetches[k].wait()

    c, f = lax.axis_index("cin"), lax.axis_index("flt")
    chip, core = f // 2, lax.rem(f, 2)
    mate = f + 1 - 2 * core
    z, xh = chip // 2, lax.rem(chip, 2)
    across = f + 2 - 4 * xh

    def remote(src, dst, send, recv, to_c, to_f):
        return pltpu.make_async_remote_copy(
            src_ref=src, dst_ref=dst, send_sem=send, recv_sem=recv,
            device_id=(to_c, to_f), device_id_type=MESH,
        )

    def exists(piece, sign):
        to_c, to_f = c + sign * piece[2], f + sign * piece[3]
        return (to_c >= 0) & (to_c < NC) & (to_f >= 0) & (to_f < NF)

    def is_cin(k):
        return (k >= 0) & (k < NC)

    def halo_copy(j):
        first, rows, dc, df = PIECES[j]
        at = pl.ds(first, rows)
        return remote(sb.at[at], halo.at[at], halo_s.at[j], halo_r.at[j], c + dc, f + df)

    def g_copy(to, of):
        return remote(down, g.at[:, of], g_s.at[to], g_r.at[of], to, f)

    def dl_copy(to, of):
        return remote(dl.at[to], xx.at[1 + f, of], dl_s.at[to], dl_r.at[of], to, f)

    def at_z(to):
        return 4 * to + 2 * xh + core

    def across_copy(block):
        return remote(xx.at[1 + block], xx.at[1 + block], far_s.at[0], xx_r.at[block], c, across)

    def z_copy(to, block, k):
        return remote(xx.at[1 + block], xx.at[1 + block], xx_s.at[4 * k + to], xx_r.at[block], c, at_z(to))

    def mate_copy(block):
        return remote(xx.at[1 + block], xx.at[1 + block], fw_s.at[block], xx_r.at[block], c, mate)

    def pr_copy(k):
        return remote(r.at[k], pr.at[k], pr_s.at[k], pr_r.at[k], c, mate)

    def rr_copy(to):
        to_z, to_x = to // 2, lax.rem(to, 2)
        return remote(q.at[to], rr.at[to_x, z], rr_s.at[to], rr_r.at[4 * to_x + z], c, at_z(to_z))

    def rr_wait(x, of):
        remote(q.at[0], rr.at[x, of], rr_s.at[0], rr_r.at[4 * x + of], c, mate).wait_recv()

    def sum_copy():
        return remote(xsum, xgot, far_s.at[1], far_r.at[0], c, across)

    def ro_half(h):
        at = pl.ds(8 * h, 8)

        def ro_copy(to, of):
            return remote(po.at[to, at], ro.at[of, at], ro_s.at[8 * h + to], ro_r.at[8 * h + of], to, f)

        return ro_copy

    def w_copy(to, of):
        return remote(wl, wall.at[of], w_s.at[to], w_r.at[of], to, f)

    def a1_copy(to, of):
        return remote(ar1.at[of], ar1.at[of], a1_s.at[to], a1_r.at[of], to, f)

    def a2_copy(to, of):
        return remote(ar2.at[of], ar2.at[of], a2_s.at[to], a2_r.at[of], c, to)

    def each(count, me, act):
        @pl.loop(1, count)
        def _(k):
            act(lax.rem(me + k, count))

    def send(count, me, copy):
        each(count, me, lambda to: copy(to, me).start())

    def receive(count, me, copy):
        each(count, me, lambda of: copy(of, of).wait_recv())

    def sent(count, me, copy):
        each(count, me, lambda to: copy(to, me).wait_send())

    halo[...] = jnp.zeros_like(halo)

    barrier = pltpu.get_barrier_semaphore()

    def greet(to_c, to_f):
        pl.semaphore_signal(barrier, inc=1, device_id=(to_c, to_f), device_id_type=MESH)

    each(NC, c, lambda to: greet(to, f))
    each(NF, f, lambda to: greet(c, to))
    expected = NC + NF - 2
    for piece in PIECES[4:]:
        there = exists(piece, 1)

        @pl.when(there)
        def _(piece=piece):
            greet(c + piece[2], f + piece[3])

        expected = expected + there.astype(jnp.int32)

    fetched(0, 3, 4)
    sb[...] = dot(sel[Q0:PERM0], vol[...]).astype(BF16)
    swapped = dot(sel[SWAP0:EYE0], dout[...]).astype(BF16).reshape(16, 16, 128)
    down[...] = swapped
    g[:, pl.ds(c, 1)] = swapped[:, None]
    xx[0] = jnp.zeros(xx.shape[1:], BF16)
    xx[17] = jnp.zeros(xx.shape[1:], BF16)
    for k in range(3):
        gs[k, 0] = jnp.zeros(gs.shape[2:], BF16)
        gs[k, 17] = jnp.zeros(gs.shape[2:], BF16)

    fetched(2)
    turned = dot_t(sel[EYE0 : EYE0 + 32, :32], wdt[...]).astype(BF16)
    wl[:, :432] = turned
    wl[:, 432:] = jnp.zeros((32, 80), BF16)

    pl.semaphore_wait(barrier, expected)
    for j, piece in enumerate(PIECES):

        @pl.when(exists(piece, 1))
        def _(j=j):
            halo_copy(j).start()

    for step in (1, -1):

        @pl.when(is_cin(c + step))
        def _(step=step):
            g_copy(c + step, c).start()

    send(NC, c, w_copy)
    wall[c] = wl[...]

    fetched(1, 6)
    rows = jnp.concatenate([wet[...].astype(F32).reshape(108, 16), jnp.zeros((20, 16), F32)], 0)
    early = dot_t(sel[EYE0 : EYE0 + 16, :16], rows.astype(BF16)).astype(BF16)
    for y in range(8):
        te[y * 16 : (y + 1) * 16, :] = dot(early, taps[:, y * 512 : (y + 1) * 512]).astype(BF16)

    for j, piece in enumerate(PIECES):

        @pl.when(exists(piece, -1))
        def _(j=j):
            halo_copy(j).wait_recv()

    fetched(5)
    cells = dot(slab[:, :256], vol[...]) + dot(slab[:, 256:448], halo[...])
    for k, shifted in enumerate((moved(cells, 1), cells, moved(cells, -1))):
        shifted = shifted.astype(BF16)
        for xs in range(10):
            vs[xs * 144 + k * 48 : xs * 144 + k * 48 + 48, :] = shifted[xs * 48 : xs * 48 + 48]
    vs[1440:1584, :] = jnp.zeros((144, 256), BF16)

    @pl.loop(0, 4)
    def _(a):
        total = jnp.zeros((128, 256), F32)
        for x in range(2):
            at = pl.multiple_of((2 * a + x) * 144, 16)
            pre = dot(te[...], vs[pl.ds(at, 512), :])
            factor = jnp.where(pre > 0, 1.0, slope)
            fac[2 * a + x] = factor
            total += pre * factor
        for b in range(4):
            pooled[a, b * 16 : b * 16 + 16] = (
                total[b * 32 : b * 32 + 16] + total[b * 32 + 16 : b * 32 + 32]
            )

    pair = sel[PAIR0:END0]
    field = pooled[...].reshape(256, 256)
    high = field.astype(BF16)
    low = (field - high.astype(F32)).astype(BF16)
    means = ((dot_t(high, pair) + dot_t(low, pair)) * 0.125).astype(BF16)
    local = dot(sel[PERM0:UP0], means).astype(BF16).reshape(8, 32, 128)
    dl[...] = local
    send(NC, c, dl_copy)
    xx[1 + f, c] = dl[c]

    def far(k):
        return (k < c - 1) | (k > c + 1)

    @pl.loop(0, NC)
    def _(to):
        @pl.when(far(to))
        def _():
            g_copy(to, c).start()

    receive(NC, c, w_copy)
    for a in range(3):
        of = c + 1 - a
        if a != 1:

            @pl.when(is_cin(of))
            def _(of=of):
                g_copy(of, of).wait_recv()

            @pl.when(jnp.logical_not(is_cin(of)))
            def _(a=a):
                gh[a] = jnp.zeros(gh.shape[1:], BF16)

        @pl.when(is_cin(of))
        def _(a=a, of=of):
            plain = g[:, pl.ds(of, 1)].reshape(256, 128)
            wide = plain.astype(F32)
            parts = (moved(wide, -1).astype(BF16), plain, moved(wide, 1).astype(BF16))
            for v in range(16):
                for k in range(3):
                    gh[a, 16 - v, k * 16 : k * 16 + 16] = parts[k][v * 16 : v * 16 + 16]

            for edge in (0, 17):
                gh[a, edge] = jnp.zeros((48, 128), BF16)

    def chip_at(k):
        return 2 * lax.rem(z + 1 + k, 4) + lax.rem(xh + 1 + k // 4, 2)

    def combine(k):
        to = chip_at(k)
        pr_copy(to).wait_recv()
        total = (own[to] + pr[to].astype(F32)).astype(BF16)

        @pl.when(to // 2 != z)
        def _():
            q[to] = total
            rr_copy(to).start()

        @pl.when(to // 2 == z)
        def _():
            rr[lax.rem(to, 2), z] = total

    def dgrad(k):
        to = chip_at(k)
        v = 2 * to
        low = [gh[a, pl.ds(15 - v, 3)].reshape(144, 128) for a in range(3)]
        high = [gh[a, pl.ds(14 - v, 3)].reshape(144, 128) for a in range(3)]
        both = jnp.concatenate([jnp.concatenate(low, 0), jnp.concatenate(high, 0)], 1)
        out = dot(wall[...].reshape(256, 512)[:, :432], both)
        first, second = out[:, :128], out[:, 128:]
        r[to] = jnp.where(core == 0, second, first).astype(BF16)
        pr_copy(to).start()
        own[to] = jnp.where(core == 0, first, second)

        @pl.when(k >= 2)
        def _():
            combine(k - 2)

    pl.loop(0, 6)(dgrad)
    receive(NC, c, dl_copy)
    across_copy(f).start()
    each(4, z, lambda to: z_copy(to, f, 0).start())
    mate_copy(f).start()
    pl.loop(6, 8)(dgrad)
    combine(6)
    combine(7)
    across_copy(across).wait_recv()
    each(4, z, lambda to: z_copy(to, across, 1).start())
    mate_copy(across).start()

    fetched(8)
    for u in range(8):
        columns = slice(u * 256, (u + 1) * 256)
        wide = dot(wdt[0:144], band[0:32, columns])
        wide += dot(wdt[144:288], band[32:64, columns])
        wide += dot(wdt[288:432], band[64:96, columns])
        wide = wide.astype(BF16)
        for b in range(3):
            for k in range(3):
                block = wide[(b * 3 + k) * 16 : (b * 3 + k) * 16 + 16]
                tw[k, u * 16 : u * 16 + 16, b * 256 : (b + 1) * 256] = block

    @pl.loop(0, NC)
    def _(of):
        @pl.when(far(of))
        def _():
            g_copy(of, of).wait_recv()

    @pl.loop(0, 16)
    def _(v):
        plain = g[v].reshape(128, 128)
        wide = plain.astype(F32)
        gs[0, v + 1] = moved(wide, -1).astype(BF16)
        gs[1, v + 1] = plain
        gs[2, v + 1] = moved(wide, 1).astype(BF16)

    def summed(x):
        each(4, z, lambda of: rr_wait(x, of))
        total = rr[x, 0].astype(F32)
        for k in range(1, 4):
            total += rr[x, k].astype(F32)
        return total

    xsum[...] = summed(1 - xh).astype(BF16)
    sum_copy().start()
    total = summed(xh)
    sum_copy().wait_recv()
    total += xgot[...].astype(F32)
    spread = dot(sel[UP0:SWAP0], total.astype(BF16)).astype(BF16)
    up[...] = (dot(spread, pair) * 0.125).reshape(4, 128, 256)
    ae[...] = jnp.zeros_like(ae)

    @pl.loop(0, 4)
    def _(a):
        for x in range(2):
            at = pl.multiple_of((2 * a + x) * 144, 16)
            grad = (up[a] * fac[2 * a + x]).astype(BF16)
            ae[...] += dot_t(grad, vs[pl.ds(at, 512), :])

    rest = jnp.concatenate([ae[y * 16 : (y + 1) * 16] for y in range(8)], 1)
    pieces = []
    for _ in range(3):
        pieces.append(rest.astype(BF16))
        rest = rest - pieces[-1].astype(F32)
    fetched(7)
    mine = dot(jnp.concatenate(pieces, 0), back[...])
    mine = mine[:16] + mine[16:32] + mine[32:]
    ar1[c] = mine
    send(NC, c, a1_copy)

    for x in range(2):
        side = f if x else across

        def pass_on(of, side=side):
            block = 4 * of + lax.rem(side, 4)
            z_copy(of, block, 0).wait_recv()
            mate_copy(block).start()

        each(4, z, pass_on)

    @pl.loop(0, 8)
    def _(k):
        mate_copy(2 * k + 1 - core).wait_recv()

    def pair_of_rows(v):
        return jnp.concatenate(
            [xx[pl.ds(v, 3)].reshape(768, 128), xx[pl.ds(v + 1, 3)].reshape(768, 128)], 1
        )

    def forward(k):
        v = 2 * k
        out = dot(tw[...].reshape(384, 768), pair_of_rows(v))
        for h in range(2):
            half = out[:, h * 128 : (h + 1) * 128]
            total = moved(half[:128], 1) + half[128:256] + moved(half[256:], -1)
            po[:, v + h] = total.astype(BF16).reshape(8, 16, 128)

    pl.loop(0, 4)(forward)
    send(NC, c, ro_half(0))
    pl.loop(4, 8)(forward)
    send(NC, c, ro_half(1))
    ro[c] = po[c]

    receive(NC, c, a1_copy)
    total = ar1[0]
    for k in range(1, NC):
        total += ar1[k]
    ar2[f] = total
    send(NF, f, a2_copy)

    acc[...] = jnp.zeros_like(acc)

    @pl.loop(0, 8)
    def _(k):
        v = 2 * k
        both = jnp.concatenate(
            [gs[:, v + 1].reshape(384, 128), gs[:, v + 2].reshape(384, 128)], 1
        )
        acc[...] += dot_t(both, pair_of_rows(v))

    receive(NC, c, ro_half(0))
    receive(NC, c, ro_half(1))
    total = ro[0].astype(F32)
    for k in range(1, NC):
        total += ro[k].astype(F32)
    rounded = total.astype(BF16).reshape(256, 128)
    deep_out[...] = dot(sel[SWAP0:EYE0], rounded).astype(BF16)

    lane = lax.broadcasted_iota(jnp.int32, (16, 256), 1)
    for k in range(3):
        for b in range(3):
            total = jnp.zeros((16, 256), F32)
            for u in range(8):
                rows = acc[k * 128 + u * 16 : k * 128 + u * 16 + 16, b * 256 : (b + 1) * 256]
                rows = pltpu.roll(rows, (-(u - 1) * 32) % 256, 1) if u != 1 else rows
                if u == 0:
                    rows = jnp.where(lane < 32, 0.0, rows)
                if u == 7:
                    rows = jnp.where(lane >= 64, 0.0, rows)
                total += rows
            for a in range(3):
                at = ((a * 3 + b) * 3 + k) * 16
                grad_deep[at : at + 16, :] = total[:, a * 32 : (a + 1) * 32]

    receive(NF, f, a2_copy)
    total = ar2[0]
    for k in range(1, NF):
        total += ar2[k]
    square = jnp.concatenate([total, jnp.zeros((112, 128), F32)], 0)
    grad_early[...] = square.T[:108, :16].reshape(27, 4, 16)

    for j, piece in enumerate(PIECES):

        @pl.when(exists(piece, 1))
        def _(j=j):
            halo_copy(j).wait_send()

    sent(NC, c, g_copy)
    sent(NC, c, dl_copy)
    across_copy(f).wait_send()
    sum_copy().wait_send()
    for k in range(2):
        each(4, z, lambda to, k=k: z_copy(to, f, k).wait_send())
        each(4, z, lambda to, k=k: rr_copy(2 * to + k).wait_send())

    @pl.loop(0, 8)
    def _(k):
        mate_copy(2 * k + core).wait_send()
        pr_copy(k).wait_send()

    sent(NC, c, ro_half(0))
    sent(NC, c, ro_half(1))
    sent(NC, c, w_copy)
    sent(NC, c, a1_copy)
    sent(NF, f, a2_copy)


SCRATCH = (
    ((192, 256), BF16), ((192, 256), BF16), ((1584, 256), BF16), ((128, 512), BF16),
    ((8, 128, 256), F32), ((4, 64, 256), F32), ((8, 32, 128), BF16), ((18, 8, 32, 128), BF16),
    ((16, 16, 128), BF16), ((16, 8, 16, 128), BF16), ((3, 18, 128, 128), BF16), ((3, 18, 48, 128), BF16),
    ((32, 512), BF16), ((8, 32, 512), BF16), ((3, 128, 768), BF16), ((8, 256, 128), F32), ((8, 256, 128), BF16),
    ((8, 256, 128), BF16), ((8, 256, 128), BF16), ((2, 4, 256, 128), BF16),
    ((8, 16, 16, 128), BF16), ((8, 16, 16, 128), BF16),
    ((4, 128, 256), F32), ((128, 512), F32), ((384, 768), F32), ((8, 16, 128), F32), ((16, 16, 128), F32),
    ((256, 128), BF16), ((256, 128), BF16),
)
SEMAPHORES = (9, 8, 8, 8, 8, 8, 8, 8, 16, 2, 1, 16, 8, 8, 8, 8, 16, 16, 8, 8, 8, 8, 16, 16)
OPERANDS = (
    (256, 256), (27, 4, 16), (432, 32), (256, 128), (END0, 256), (480, 512), (128, 4096), (4096, 128), (96, 2048),
)


def hand_on(*refs):
    given, results, held, sems = refs[:3], refs[3:6], refs[6:9], refs[9]
    into = [pltpu.make_async_copy(given[k], held[k], sems.at[k]) for k in range(3)]
    out = [pltpu.make_async_copy(held[k], results[k], sems.at[3 + k]) for k in range(3)]
    for copy in into:
        copy.start()
    for k in range(3):
        into[k].wait()
        out[k].start()
    for copy in out:
        copy.wait()


def local(volume, early_w, deep_w, d_out):
    operands = [
        volume.reshape(256, 256),
        early_w.transpose(2, 3, 4, 1, 0).reshape(27, 4, 16),
        deep_w.transpose(2, 3, 4, 0, 1).reshape(432, 32),
        d_out.reshape(256, 128),
        *[jnp.asarray(t) for t in tables()],
    ]
    results = pl.pallas_call(
        kernel,
        out_shape=(
            jax.ShapeDtypeStruct((256, 128), BF16),
            jax.ShapeDtypeStruct((432, 32), F32),
            jax.ShapeDtypeStruct((27, 4, 16), F32),
        ),
        in_specs=[pl.BlockSpec(memory_space=pltpu.HBM)] * len(operands),
        out_specs=[pl.BlockSpec(memory_space=pltpu.VMEM)] * 3,
        scratch_shapes=[pltpu.VMEM(shape, BF16) for shape in OPERANDS]
        + [pltpu.VMEM(shape, dtype) for shape, dtype in SCRATCH]
        + [pltpu.SemaphoreType.DMA((count,)) for count in SEMAPHORES],
        compiler_params=pltpu.CompilerParams(
            collective_id=0, has_side_effects=True, vmem_limit_bytes=60 << 20
        ),
        name="cosmo",
    )(*operands)
    deep_out, grad_deep, grad_early = pl.pallas_call(
        hand_on,
        out_shape=[jax.ShapeDtypeStruct(x.shape, x.dtype) for x in results],
        in_specs=[pl.BlockSpec(memory_space=pl.ANY)] * 3,
        out_specs=[pl.BlockSpec(memory_space=pl.ANY)] * 3,
        scratch_shapes=[pltpu.VMEM(x.shape, x.dtype) for x in results]
        + [pltpu.SemaphoreType.DMA((6,))],
        name="results",
    )(*results)
    return (
        deep_out.reshape(16, 1, 16, 128),
        grad_deep.reshape(3, 3, 3, 16, 32).transpose(3, 4, 0, 1, 2),
        grad_early.reshape(3, 3, 3, 4, 16).transpose(4, 3, 0, 1, 2),
    )


def solution(mesh):
    in_specs = (
        P(None, "cin", "flt", None),
        P(),
        P("flt", "cin", None, None, None),
        P("flt", "cin", None, None),
    )
    out_specs = (P("flt", "cin", None, None), P("flt", "cin", None, None, None), P())
    return jax.shard_map(local, mesh=mesh, in_specs=in_specs, out_specs=out_specs, check_vma=False)
```

```python
import jax
import jax.numpy as jnp
import ml_dtypes
import numpy as np
from jax import lax
from jax.experimental import pallas as pl
from jax.experimental.pallas import tpu as pltpu
from jax.sharding import PartitionSpec as P

MESH = pl.DeviceIdType.MESH
F32, BF16 = jnp.float32, jnp.bfloat16
slope = 0.3
NC, NF = 8, 16

PIECES = (
    (0, 32, 1, 0), (32, 32, -1, 0), (64, 32, 0, 1), (96, 32, 0, -1),
    (128, 16, 1, 1), (144, 16, 1, -1), (160, 16, -1, 1), (176, 16, -1, -1),
)
Q0, PERM0, UP0, SWAP0, EYE0, PAIR0, END0 = 0, 192, 448, 960, 1216, 1472, 1600


def tables():
    sel = np.zeros((END0, 256), np.float32)
    for i in range(4):
        for y in range(8):
            sel[Q0 + i * 8 + y, i * 64 + 56 + y] = 1
            sel[Q0 + 32 + i * 8 + y, i * 64 + y] = 1
        for x in range(8):
            sel[Q0 + 64 + x * 4 + i, i * 64 + x * 8 + 7] = 1
            sel[Q0 + 96 + x * 4 + i, i * 64 + x * 8] = 1
        sel[Q0 + 128 + i, i * 64 + 63] = 1
        sel[Q0 + 144 + i, i * 64 + 56] = 1
        sel[Q0 + 160 + i, i * 64 + 7] = 1
        sel[Q0 + 176 + i, i * 64] = 1
    for a in range(4):
        for e in range(16):
            for b in range(4):
                sel[PERM0 + 16 * e + 4 * a + b, a * 64 + b * 16 + e] = 1
            for y in range(8):
                sel[UP0 + a * 128 + y * 16 + e, 16 * e + 4 * a + y // 2] = 1
    for v in range(16):
        for o in range(16):
            sel[SWAP0 + v * 16 + o, o * 16 + v] = 1
    sel[EYE0 : EYE0 + 256] = np.eye(256)
    for z in range(256):
        sel[PAIR0 + z // 2, z] = 1

    slab = np.zeros((480, 512), np.float32)
    for xs in range(10):
        x = xs - 1
        for i in range(4):
            for y in range(8):
                column = i * 64 + x * 8 + y if 0 <= x < 8 else 256 + (32 if x == 8 else 0) + i * 8 + y
                slab[xs * 48 + i * 8 + y, column] = 1
            low, high = (320 + x * 4, 352 + x * 4) if 0 <= x < 8 else ((384, 400) if x < 0 else (416, 432))
            slab[xs * 48 + 32 + i, low + i] = 1
            slab[xs * 48 + 36 + i, high + i] = 1

    taps = np.zeros((128, 8 * 512), np.float32)
    for y in range(8):
        for a in range(3):
            for b in range(3):
                for c in range(3):
                    for i in range(4):
                        row = y + b - 1
                        k = 32 + i if row < 0 else 36 + i if row > 7 else i * 8 + row
                        taps[(a * 9 + b * 3 + c) * 4 + i, y * 512 + a * 144 + c * 48 + k] = 1

    band = np.zeros((96, 8 * 256), np.float32)
    for u in range(8):
        for a in range(3):
            if 0 <= u + a - 1 < 8:
                for i in range(32):
                    band[a * 32 + i, u * 256 + (u + a - 1) * 32 + i] = 1
    return [t.astype(ml_dtypes.bfloat16) for t in (sel, slab, taps, taps.T, band)]


def dot(a, b):
    return jnp.dot(a, b, preferred_element_type=F32)


def dot_t(a, b):
    return lax.dot_general(a, b, (((1,), (1,)), ((), ())), preferred_element_type=F32)


def moved(value, step):
    width = value.shape[1]
    lane = lax.broadcasted_iota(jnp.int32, value.shape, 1)
    edge = 0 if step > 0 else width - 1
    return jnp.where(lane == edge, 0.0, pltpu.roll(value, step % width, 1))


def kernel(*refs):
    count = len(OPERANDS)
    given, refs = refs[:count], refs[count:]
    deep_out, grad_deep, grad_early = refs[:3]
    here, refs = refs[3 : 3 + count], refs[3 + count :]
    vol, wet, wdt, dout, sel, slab, taps, back, band = here
    (sb, halo, vs, te, fac, pooled, dl, xx, down, g, gs, gh, wl, wall, tw, own, r, pr, q, rr, po, ro, up, ae, acc,
     ar1, ar2, xsum, xgot) = refs[: len(SCRATCH)]
    (got, halo_s, halo_r, g_s, g_r, dl_s, dl_r, xx_s, xx_r, far_s, far_r, fw_s, pr_s, pr_r, rr_s, rr_r, ro_s, ro_r, w_s, w_r,
     a1_s, a1_r, a2_s, a2_r) = refs[len(SCRATCH) :]

    fetches = [pltpu.make_async_copy(given[k], here[k], got.at[k]) for k in range(count)]
    for k in (0, 3, 4, 2, 1, 6, 5, 8, 7):
        fetches[k].start()

    def fetched(*which):
        for k in which:
            fetches[k].wait()

    c, f = lax.axis_index("cin"), lax.axis_index("flt")
    chip, core = f // 2, lax.rem(f, 2)
    mate = f + 1 - 2 * core
    z, xh = chip // 2, lax.rem(chip, 2)
    across = f + 2 - 4 * xh

    def remote(src, dst, send, recv, to_c, to_f):
        return pltpu.make_async_remote_copy(
            src_ref=src, dst_ref=dst, send_sem=send, recv_sem=recv,
            device_id=(to_c, to_f), device_id_type=MESH,
        )

    def exists(piece, sign):
        to_c, to_f = c + sign * piece[2], f + sign * piece[3]
        return (to_c >= 0) & (to_c < NC) & (to_f >= 0) & (to_f < NF)

    def is_cin(k):
        return (k >= 0) & (k < NC)

    def halo_copy(j):
        first, rows, dc, df = PIECES[j]
        at = pl.ds(first, rows)
        return remote(sb.at[at], halo.at[at], halo_s.at[j], halo_r.at[j], c + dc, f + df)

    def g_copy(to, of):
        return remote(down, g.at[:, of], g_s.at[to], g_r.at[of], to, f)

    def dl_copy(to, of):
        return remote(dl.at[to], xx.at[1 + f, of], dl_s.at[to], dl_r.at[of], to, f)

    def at_z(to):
        return 4 * to + 2 * xh + core

    def across_copy(block):
        return remote(xx.at[1 + block], xx.at[1 + block], far_s.at[0], xx_r.at[block], c, across)

    def z_copy(to, block, k):
        return remote(xx.at[1 + block], xx.at[1 + block], xx_s.at[4 * k + to], xx_r.at[block], c, at_z(to))

    def mate_copy(block):
        return remote(xx.at[1 + block], xx.at[1 + block], fw_s.at[block], xx_r.at[block], c, mate)

    def pr_copy(k):
        return remote(r.at[k], pr.at[k], pr_s.at[k], pr_r.at[k], c, mate)

    def rr_copy(to):
        to_z, to_x = to // 2, lax.rem(to, 2)
        return remote(q.at[to], rr.at[to_x, z], rr_s.at[to], rr_r.at[4 * to_x + z], c, at_z(to_z))

    def rr_wait(x, of):
        remote(q.at[0], rr.at[x, of], rr_s.at[0], rr_r.at[4 * x + of], c, mate).wait_recv()

    def sum_copy():
        return remote(xsum, xgot, far_s.at[1], far_r.at[0], c, across)

    def ro_half(h):
        at = pl.ds(8 * h, 8)

        def ro_copy(to, of):
            return remote(po.at[to, at], ro.at[of, at], ro_s.at[8 * h + to], ro_r.at[8 * h + of], to, f)

        return ro_copy

    def w_copy(to, of):
        return remote(wl, wall.at[of], w_s.at[to], w_r.at[of], to, f)

    def a1_copy(to, of):
        return remote(ar1.at[of], ar1.at[of], a1_s.at[to], a1_r.at[of], to, f)

    def a2_copy(to, of):
        return remote(ar2.at[of], ar2.at[of], a2_s.at[to], a2_r.at[of], c, to)

    def each(count, me, act):
        @pl.loop(1, count)
        def _(k):
            act(lax.rem(me + k, count))

    def send(count, me, copy):
        each(count, me, lambda to: copy(to, me).start())

    def receive(count, me, copy):
        each(count, me, lambda of: copy(of, of).wait_recv())

    def sent(count, me, copy):
        each(count, me, lambda to: copy(to, me).wait_send())

    halo[...] = jnp.zeros_like(halo)

    barrier = pltpu.get_barrier_semaphore()

    def greet(to_c, to_f):
        pl.semaphore_signal(barrier, inc=1, device_id=(to_c, to_f), device_id_type=MESH)

    each(NC, c, lambda to: greet(to, f))
    each(NF, f, lambda to: greet(c, to))
    expected = NC + NF - 2
    for piece in PIECES[4:]:
        there = exists(piece, 1)

        @pl.when(there)
        def _(piece=piece):
            greet(c + piece[2], f + piece[3])

        expected = expected + there.astype(jnp.int32)

    fetched(0, 3, 4)
    sb[...] = dot(sel[Q0:PERM0], vol[...]).astype(BF16)
    swapped = dot(sel[SWAP0:EYE0], dout[...]).astype(BF16).reshape(16, 16, 128)
    down[...] = swapped
    g[:, pl.ds(c, 1)] = swapped[:, None]
    xx[0] = jnp.zeros(xx.shape[1:], BF16)
    xx[17] = jnp.zeros(xx.shape[1:], BF16)
    for k in range(3):
        gs[k, 0] = jnp.zeros(gs.shape[2:], BF16)
        gs[k, 17] = jnp.zeros(gs.shape[2:], BF16)

    fetched(2)
    turned = dot_t(sel[EYE0 : EYE0 + 32, :32], wdt[...]).astype(BF16)
    wl[:, :432] = turned
    wl[:, 432:] = jnp.zeros((32, 80), BF16)

    pl.semaphore_wait(barrier, expected)
    for j, piece in enumerate(PIECES):

        @pl.when(exists(piece, 1))
        def _(j=j):
            halo_copy(j).start()

    for step in (1, -1):

        @pl.when(is_cin(c + step))
        def _(step=step):
            g_copy(c + step, c).start()

    send(NC, c, w_copy)
    wall[c] = wl[...]

    fetched(1, 6)
    rows = jnp.concatenate([wet[...].astype(F32).reshape(108, 16), jnp.zeros((20, 16), F32)], 0)
    early = dot_t(sel[EYE0 : EYE0 + 16, :16], rows.astype(BF16)).astype(BF16)
    for y in range(8):
        te[y * 16 : (y + 1) * 16, :] = dot(early, taps[:, y * 512 : (y + 1) * 512]).astype(BF16)

    for j, piece in enumerate(PIECES):

        @pl.when(exists(piece, -1))
        def _(j=j):
            halo_copy(j).wait_recv()

    fetched(5)
    cells = dot(slab[:, :256], vol[...]) + dot(slab[:, 256:448], halo[...])
    for k, shifted in enumerate((moved(cells, 1), cells, moved(cells, -1))):
        shifted = shifted.astype(BF16)
        for xs in range(10):
            vs[xs * 144 + k * 48 : xs * 144 + k * 48 + 48, :] = shifted[xs * 48 : xs * 48 + 48]
    vs[1440:1584, :] = jnp.zeros((144, 256), BF16)

    @pl.loop(0, 4)
    def _(a):
        total = jnp.zeros((128, 256), F32)
        for x in range(2):
            at = pl.multiple_of((2 * a + x) * 144, 16)
            pre = dot(te[...], vs[pl.ds(at, 512), :])
            factor = jnp.where(pre > 0, 1.0, slope)
            fac[2 * a + x] = factor
            total += pre * factor
        for b in range(4):
            pooled[a, b * 16 : b * 16 + 16] = (
                total[b * 32 : b * 32 + 16] + total[b * 32 + 16 : b * 32 + 32]
            )

    pair = sel[PAIR0:END0]
    field = pooled[...].reshape(256, 256)
    high = field.astype(BF16)
    low = (field - high.astype(F32)).astype(BF16)
    means = ((dot_t(high, pair) + dot_t(low, pair)) * 0.125).astype(BF16)
    local = dot(sel[PERM0:UP0], means).astype(BF16).reshape(8, 32, 128)
    dl[...] = local
    send(NC, c, dl_copy)
    xx[1 + f, c] = dl[c]

    def far(k):
        return (k < c - 1) | (k > c + 1)

    @pl.loop(0, NC)
    def _(to):
        @pl.when(far(to))
        def _():
            g_copy(to, c).start()

    receive(NC, c, w_copy)
    for a in range(3):
        of = c + 1 - a
        if a != 1:

            @pl.when(is_cin(of))
            def _(of=of):
                g_copy(of, of).wait_recv()

            @pl.when(jnp.logical_not(is_cin(of)))
            def _(a=a):
                gh[a] = jnp.zeros(gh.shape[1:], BF16)

        @pl.when(is_cin(of))
        def _(a=a, of=of):
            plain = g[:, pl.ds(of, 1)].reshape(256, 128)
            wide = plain.astype(F32)
            parts = (moved(wide, -1).astype(BF16), plain, moved(wide, 1).astype(BF16))
            for v in range(16):
                for k in range(3):
                    gh[a, 16 - v, k * 16 : k * 16 + 16] = parts[k][v * 16 : v * 16 + 16]

            for edge in (0, 17):
                gh[a, edge] = jnp.zeros((48, 128), BF16)

    def chip_at(k):
        return 2 * lax.rem(z + 1 + k, 4) + lax.rem(xh + 1 + k // 4, 2)

    def combine(k):
        to = chip_at(k)
        pr_copy(to).wait_recv()
        total = (own[to] + pr[to].astype(F32)).astype(BF16)

        @pl.when(to // 2 != z)
        def _():
            q[to] = total
            rr_copy(to).start()

        @pl.when(to // 2 == z)
        def _():
            rr[lax.rem(to, 2), z] = total

    def dgrad(k):
        to = chip_at(k)
        v = 2 * to
        low = [gh[a, pl.ds(15 - v, 3)].reshape(144, 128) for a in range(3)]
        high = [gh[a, pl.ds(14 - v, 3)].reshape(144, 128) for a in range(3)]
        both = jnp.concatenate([jnp.concatenate(low, 0), jnp.concatenate(high, 0)], 1)
        out = dot(wall[...].reshape(256, 512)[:, :432], both)
        first, second = out[:, :128], out[:, 128:]
        r[to] = jnp.where(core == 0, second, first).astype(BF16)
        pr_copy(to).start()
        own[to] = jnp.where(core == 0, first, second)

        @pl.when(k >= 2)
        def _():
            combine(k - 2)

    pl.loop(0, 3)(dgrad)
    receive(NC, c, dl_copy)
    across_copy(f).start()
    each(4, z, lambda to: z_copy(to, f, 0).start())
    mate_copy(f).start()
    pl.loop(3, 8)(dgrad)
    combine(6)
    combine(7)
    across_copy(across).wait_recv()
    each(4, z, lambda to: z_copy(to, across, 1).start())
    mate_copy(across).start()

    fetched(8)
    for u in range(8):
        columns = slice(u * 256, (u + 1) * 256)
        wide = dot(wdt[0:144], band[0:32, columns])
        wide += dot(wdt[144:288], band[32:64, columns])
        wide += dot(wdt[288:432], band[64:96, columns])
        wide = wide.astype(BF16)
        for b in range(3):
            for k in range(3):
                block = wide[(b * 3 + k) * 16 : (b * 3 + k) * 16 + 16]
                tw[k, u * 16 : u * 16 + 16, b * 256 : (b + 1) * 256] = block

    @pl.loop(0, NC)
    def _(of):
        @pl.when(far(of))
        def _():
            g_copy(of, of).wait_recv()

    @pl.loop(0, 16)
    def _(v):
        plain = g[v].reshape(128, 128)
        wide = plain.astype(F32)
        gs[0, v + 1] = moved(wide, -1).astype(BF16)
        gs[1, v + 1] = plain
        gs[2, v + 1] = moved(wide, 1).astype(BF16)

    def summed(x):
        each(4, z, lambda of: rr_wait(x, of))
        total = rr[x, 0].astype(F32)
        for k in range(1, 4):
            total += rr[x, k].astype(F32)
        return total

    xsum[...] = summed(1 - xh).astype(BF16)
    sum_copy().start()
    for x in range(2):
        side = f if x else across

        def pass_on(of, side=side):
            block = 4 * of + lax.rem(side, 4)
            z_copy(of, block, 0).wait_recv()
            mate_copy(block).start()

        each(4, z, pass_on)

    total = summed(xh)
    sum_copy().wait_recv()
    total += xgot[...].astype(F32)
    spread = dot(sel[UP0:SWAP0], total.astype(BF16)).astype(BF16)
    up[...] = (dot(spread, pair) * 0.125).reshape(4, 128, 256)
    ae[...] = jnp.zeros_like(ae)

    @pl.loop(0, 4)
    def _(a):
        for x in range(2):
            at = pl.multiple_of((2 * a + x) * 144, 16)
            grad = (up[a] * fac[2 * a + x]).astype(BF16)
            ae[...] += dot_t(grad, vs[pl.ds(at, 512), :])

    rest = jnp.concatenate([ae[y * 16 : (y + 1) * 16] for y in range(8)], 1)
    pieces = []
    for _ in range(3):
        pieces.append(rest.astype(BF16))
        rest = rest - pieces[-1].astype(F32)
    fetched(7)
    mine = dot(jnp.concatenate(pieces, 0), back[...])
    mine = mine[:16] + mine[16:32] + mine[32:]
    ar1[c] = mine
    send(NC, c, a1_copy)

    @pl.loop(0, 8)
    def _(k):
        mate_copy(2 * k + 1 - core).wait_recv()

    def pair_of_rows(v):
        return jnp.concatenate(
            [xx[pl.ds(v, 3)].reshape(768, 128), xx[pl.ds(v + 1, 3)].reshape(768, 128)], 1
        )

    def forward(k):
        v = 2 * k
        out = dot(tw[...].reshape(384, 768), pair_of_rows(v))
        for h in range(2):
            half = out[:, h * 128 : (h + 1) * 128]
            total = moved(half[:128], 1) + half[128:256] + moved(half[256:], -1)
            po[:, v + h] = total.astype(BF16).reshape(8, 16, 128)

    pl.loop(0, 4)(forward)
    send(NC, c, ro_half(0))
    receive(NC, c, a1_copy)
    total = ar1[0]
    for k in range(1, NC):
        total += ar1[k]
    ar2[f] = total
    send(NF, f, a2_copy)
    pl.loop(4, 8)(forward)
    send(NC, c, ro_half(1))
    ro[c] = po[c]

    acc[...] = jnp.zeros_like(acc)

    @pl.loop(0, 8)
    def _(k):
        v = 2 * k
        both = jnp.concatenate(
            [gs[:, v + 1].reshape(384, 128), gs[:, v + 2].reshape(384, 128)], 1
        )
        acc[...] += dot_t(both, pair_of_rows(v))

    receive(NC, c, ro_half(0))
    receive(NC, c, ro_half(1))
    total = ro[0].astype(F32)
    for k in range(1, NC):
        total += ro[k].astype(F32)
    rounded = total.astype(BF16).reshape(256, 128)
    deep_out[...] = dot(sel[SWAP0:EYE0], rounded).astype(BF16)

    lane = lax.broadcasted_iota(jnp.int32, (16, 256), 1)
    for k in range(3):
        for b in range(3):
            total = jnp.zeros((16, 256), F32)
            for u in range(8):
                rows = acc[k * 128 + u * 16 : k * 128 + u * 16 + 16, b * 256 : (b + 1) * 256]
                rows = pltpu.roll(rows, (-(u - 1) * 32) % 256, 1) if u != 1 else rows
                if u == 0:
                    rows = jnp.where(lane < 32, 0.0, rows)
                if u == 7:
                    rows = jnp.where(lane >= 64, 0.0, rows)
                total += rows
            for a in range(3):
                at = ((a * 3 + b) * 3 + k) * 16
                grad_deep[at : at + 16, :] = total[:, a * 32 : (a + 1) * 32]

    receive(NF, f, a2_copy)
    total = ar2[0]
    for k in range(1, NF):
        total += ar2[k]
    square = jnp.concatenate([total, jnp.zeros((112, 128), F32)], 0)
    grad_early[...] = square.T[:108, :16].reshape(27, 4, 16)

    for j, piece in enumerate(PIECES):

        @pl.when(exists(piece, 1))
        def _(j=j):
            halo_copy(j).wait_send()

    sent(NC, c, g_copy)
    sent(NC, c, dl_copy)
    across_copy(f).wait_send()
    sum_copy().wait_send()
    for k in range(2):
        each(4, z, lambda to, k=k: z_copy(to, f, k).wait_send())
        each(4, z, lambda to, k=k: rr_copy(2 * to + k).wait_send())

    @pl.loop(0, 8)
    def _(k):
        mate_copy(2 * k + core).wait_send()
        pr_copy(k).wait_send()

    sent(NC, c, ro_half(0))
    sent(NC, c, ro_half(1))
    sent(NC, c, w_copy)
    sent(NC, c, a1_copy)
    sent(NF, f, a2_copy)


SCRATCH = (
    ((192, 256), BF16), ((192, 256), BF16), ((1584, 256), BF16), ((128, 512), BF16),
    ((8, 128, 256), F32), ((4, 64, 256), F32), ((8, 32, 128), BF16), ((18, 8, 32, 128), BF16),
    ((16, 16, 128), BF16), ((16, 8, 16, 128), BF16), ((3, 18, 128, 128), BF16), ((3, 18, 48, 128), BF16),
    ((32, 512), BF16), ((8, 32, 512), BF16), ((3, 128, 768), BF16), ((8, 256, 128), F32), ((8, 256, 128), BF16),
    ((8, 256, 128), BF16), ((8, 256, 128), BF16), ((2, 4, 256, 128), BF16),
    ((8, 16, 16, 128), BF16), ((8, 16, 16, 128), BF16),
    ((4, 128, 256), F32), ((128, 512), F32), ((384, 768), F32), ((8, 16, 128), F32), ((16, 16, 128), F32),
    ((256, 128), BF16), ((256, 128), BF16),
)
SEMAPHORES = (9, 8, 8, 8, 8, 8, 8, 8, 16, 2, 1, 16, 8, 8, 8, 8, 16, 16, 8, 8, 8, 8, 16, 16)
OPERANDS = (
    (256, 256), (27, 4, 16), (432, 32), (256, 128), (END0, 256), (480, 512), (128, 4096), (4096, 128), (96, 2048),
)


def hand_on(*refs):
    given, results, held, sems = refs[:3], refs[3:6], refs[6:9], refs[9]
    into = [pltpu.make_async_copy(given[k], held[k], sems.at[k]) for k in range(3)]
    out = [pltpu.make_async_copy(held[k], results[k], sems.at[3 + k]) for k in range(3)]
    for copy in into:
        copy.start()
    for k in range(3):
        into[k].wait()
        out[k].start()
    for copy in out:
        copy.wait()


def local(volume, early_w, deep_w, d_out):
    operands = [
        volume.reshape(256, 256),
        early_w.transpose(2, 3, 4, 1, 0).reshape(27, 4, 16),
        deep_w.transpose(2, 3, 4, 0, 1).reshape(432, 32),
        d_out.reshape(256, 128),
        *[jnp.asarray(t) for t in tables()],
    ]
    results = pl.pallas_call(
        kernel,
        out_shape=(
            jax.ShapeDtypeStruct((256, 128), BF16),
            jax.ShapeDtypeStruct((432, 32), F32),
            jax.ShapeDtypeStruct((27, 4, 16), F32),
        ),
        in_specs=[pl.BlockSpec(memory_space=pltpu.HBM)] * len(operands),
        out_specs=[pl.BlockSpec(memory_space=pltpu.VMEM)] * 3,
        scratch_shapes=[pltpu.VMEM(shape, BF16) for shape in OPERANDS]
        + [pltpu.VMEM(shape, dtype) for shape, dtype in SCRATCH]
        + [pltpu.SemaphoreType.DMA((count,)) for count in SEMAPHORES],
        compiler_params=pltpu.CompilerParams(
            collective_id=0, has_side_effects=True, vmem_limit_bytes=60 << 20
        ),
        name="cosmo",
    )(*operands)
    deep_out, grad_deep, grad_early = pl.pallas_call(
        hand_on,
        out_shape=[jax.ShapeDtypeStruct(x.shape, x.dtype) for x in results],
        in_specs=[pl.BlockSpec(memory_space=pl.ANY)] * 3,
        out_specs=[pl.BlockSpec(memory_space=pl.ANY)] * 3,
        scratch_shapes=[pltpu.VMEM(x.shape, x.dtype) for x in results]
        + [pltpu.SemaphoreType.DMA((6,))],
        name="results",
    )(*results)
    return (
        deep_out.reshape(16, 1, 16, 128),
        grad_deep.reshape(3, 3, 3, 16, 32).transpose(3, 4, 0, 1, 2),
        grad_early.reshape(3, 3, 3, 4, 16).transpose(4, 3, 0, 1, 2),
    )


def solution(mesh):
    in_specs = (
        P(None, "cin", "flt", None),
        P(),
        P("flt", "cin", None, None, None),
        P("flt", "cin", None, None),
    )
    out_specs = (P("flt", "cin", None, None), P("flt", "cin", None, None, None), P())
    return jax.shard_map(local, mesh=mesh, in_specs=in_specs, out_specs=out_specs, check_vma=False)
```

```python
import jax
import jax.numpy as jnp
import ml_dtypes
import numpy as np
from jax import lax
from jax.experimental import pallas as pl
from jax.experimental.pallas import tpu as pltpu
from jax.sharding import PartitionSpec as P

MESH = pl.DeviceIdType.MESH
F32, BF16 = jnp.float32, jnp.bfloat16
slope = 0.3
NC, NF = 8, 16

PIECES = (
    (0, 32, 1, 0), (32, 32, -1, 0), (64, 32, 0, 1), (96, 32, 0, -1),
    (128, 16, 1, 1), (144, 16, 1, -1), (160, 16, -1, 1), (176, 16, -1, -1),
)
Q0, PERM0, UP0, SWAP0, EYE0, PAIR0, END0 = 0, 192, 448, 960, 1216, 1472, 1600


def tables():
    sel = np.zeros((END0, 256), np.float32)
    for i in range(4):
        for y in range(8):
            sel[Q0 + i * 8 + y, i * 64 + 56 + y] = 1
            sel[Q0 + 32 + i * 8 + y, i * 64 + y] = 1
        for x in range(8):
            sel[Q0 + 64 + x * 4 + i, i * 64 + x * 8 + 7] = 1
            sel[Q0 + 96 + x * 4 + i, i * 64 + x * 8] = 1
        sel[Q0 + 128 + i, i * 64 + 63] = 1
        sel[Q0 + 144 + i, i * 64 + 56] = 1
        sel[Q0 + 160 + i, i * 64 + 7] = 1
        sel[Q0 + 176 + i, i * 64] = 1
    for a in range(4):
        for e in range(16):
            for b in range(4):
                sel[PERM0 + 16 * e + 4 * a + b, a * 64 + b * 16 + e] = 1
            for y in range(8):
                sel[UP0 + a * 128 + y * 16 + e, 16 * e + 4 * a + y // 2] = 1
    for v in range(16):
        for o in range(16):
            sel[SWAP0 + v * 16 + o, o * 16 + v] = 1
    sel[EYE0 : EYE0 + 256] = np.eye(256)
    for z in range(256):
        sel[PAIR0 + z // 2, z] = 1

    slab = np.zeros((480, 512), np.float32)
    for xs in range(10):
        x = xs - 1
        for i in range(4):
            for y in range(8):
                column = i * 64 + x * 8 + y if 0 <= x < 8 else 256 + (32 if x == 8 else 0) + i * 8 + y
                slab[xs * 48 + i * 8 + y, column] = 1
            low, high = (320 + x * 4, 352 + x * 4) if 0 <= x < 8 else ((384, 400) if x < 0 else (416, 432))
            slab[xs * 48 + 32 + i, low + i] = 1
            slab[xs * 48 + 36 + i, high + i] = 1

    taps = np.zeros((128, 8 * 512), np.float32)
    for y in range(8):
        for a in range(3):
            for b in range(3):
                for c in range(3):
                    for i in range(4):
                        row = y + b - 1
                        k = 32 + i if row < 0 else 36 + i if row > 7 else i * 8 + row
                        taps[(a * 9 + b * 3 + c) * 4 + i, y * 512 + a * 144 + c * 48 + k] = 1

    band = np.zeros((96, 8 * 256), np.float32)
    for u in range(8):
        for a in range(3):
            if 0 <= u + a - 1 < 8:
                for i in range(32):
                    band[a * 32 + i, u * 256 + (u + a - 1) * 32 + i] = 1
    return [t.astype(ml_dtypes.bfloat16) for t in (sel, slab, taps, taps.T, band)]


def dot(a, b):
    return jnp.dot(a, b, preferred_element_type=F32)


def dot_t(a, b):
    return lax.dot_general(a, b, (((1,), (1,)), ((), ())), preferred_element_type=F32)


def moved(value, step):
    width = value.shape[1]
    lane = lax.broadcasted_iota(jnp.int32, value.shape, 1)
    edge = 0 if step > 0 else width - 1
    return jnp.where(lane == edge, 0.0, pltpu.roll(value, step % width, 1))


def kernel(*refs):
    count = len(OPERANDS)
    given, refs = refs[:count], refs[count:]
    deep_out, grad_deep, grad_early = refs[:3]
    here, refs = refs[3 : 3 + count], refs[3 + count :]
    vol, wet, wdt, dout, sel, slab, taps, back, band = here
    (sb, halo, vs, te, fac, pooled, dl, xx, down, g, gs, gh, wl, wall, tw, own, r, pr, q, rr, po, ro, up, ae, acc,
     ar1, ar2, xsum, xgot) = refs[: len(SCRATCH)]
    (got, halo_s, halo_r, g_s, g_r, dl_s, dl_r, xx_s, xx_r, far_s, far_r, fw_s, pr_s, pr_r, rr_s, rr_r, ro_s, ro_r, w_s, w_r,
     a1_s, a1_r, a2_s, a2_r) = refs[len(SCRATCH) :]

    fetches = [pltpu.make_async_copy(given[k], here[k], got.at[k]) for k in range(count)]
    for k in (0, 3, 4, 2, 1, 6, 5, 8, 7):
        fetches[k].start()

    def fetched(*which):
        for k in which:
            fetches[k].wait()

    c, f = lax.axis_index("cin"), lax.axis_index("flt")
    chip, core = f // 2, lax.rem(f, 2)
    mate = f + 1 - 2 * core
    z, xh = chip // 2, lax.rem(chip, 2)
    across = f + 2 - 4 * xh

    def remote(src, dst, send, recv, to_c, to_f):
        return pltpu.make_async_remote_copy(
            src_ref=src, dst_ref=dst, send_sem=send, recv_sem=recv,
            device_id=(to_c, to_f), device_id_type=MESH,
        )

    def exists(piece, sign):
        to_c, to_f = c + sign * piece[2], f + sign * piece[3]
        return (to_c >= 0) & (to_c < NC) & (to_f >= 0) & (to_f < NF)

    def is_cin(k):
        return (k >= 0) & (k < NC)

    def halo_copy(j):
        first, rows, dc, df = PIECES[j]
        at = pl.ds(first, rows)
        return remote(sb.at[at], halo.at[at], halo_s.at[j], halo_r.at[j], c + dc, f + df)

    def g_copy(to, of):
        return remote(down, g.at[:, of], g_s.at[to], g_r.at[of], to, f)

    def dl_copy(to, of):
        return remote(dl.at[to], xx.at[1 + f, of], dl_s.at[to], dl_r.at[of], to, f)

    def at_z(to):
        return 4 * to + 2 * xh + core

    def across_copy(block):
        return remote(xx.at[1 + block], xx.at[1 + block], far_s.at[0], xx_r.at[block], c, across)

    def z_copy(to, block, k):
        return remote(xx.at[1 + block], xx.at[1 + block], xx_s.at[4 * k + to], xx_r.at[block], c, at_z(to))

    def mate_copy(block):
        return remote(xx.at[1 + block], xx.at[1 + block], fw_s.at[block], xx_r.at[block], c, mate)

    def pr_copy(k):
        return remote(r.at[k], pr.at[k], pr_s.at[k], pr_r.at[k], c, mate)

    def rr_copy(to):
        to_z, to_x = to // 2, lax.rem(to, 2)
        return remote(q.at[to], rr.at[to_x, z], rr_s.at[to], rr_r.at[4 * to_x + z], c, at_z(to_z))

    def rr_wait(x, of):
        remote(q.at[0], rr.at[x, of], rr_s.at[0], rr_r.at[4 * x + of], c, mate).wait_recv()

    def sum_copy():
        return remote(xsum, xgot, far_s.at[1], far_r.at[0], c, across)

    def ro_half(h):
        at = pl.ds(8 * h, 8)

        def ro_copy(to, of):
            return remote(po.at[to, at], ro.at[of, at], ro_s.at[8 * h + to], ro_r.at[8 * h + of], to, f)

        return ro_copy

    def w_copy(to, of):
        return remote(wl, wall.at[of], w_s.at[to], w_r.at[of], to, f)

    def a1_copy(to, of):
        return remote(ar1.at[of], ar1.at[of], a1_s.at[to], a1_r.at[of], c, to)

    def a2_copy(to, of):
        return remote(ar2.at[of], ar2.at[of], a2_s.at[to], a2_r.at[of], to, f)

    def each(count, me, act):
        @pl.loop(1, count)
        def _(k):
            act(lax.rem(me + k, count))

    def send(count, me, copy):
        each(count, me, lambda to: copy(to, me).start())

    def receive(count, me, copy):
        each(count, me, lambda of: copy(of, of).wait_recv())

    def sent(count, me, copy):
        each(count, me, lambda to: copy(to, me).wait_send())

    halo[...] = jnp.zeros_like(halo)

    barrier = pltpu.get_barrier_semaphore()

    def greet(to_c, to_f):
        pl.semaphore_signal(barrier, inc=1, device_id=(to_c, to_f), device_id_type=MESH)

    each(NC, c, lambda to: greet(to, f))
    each(NF, f, lambda to: greet(c, to))
    expected = NC + NF - 2
    for piece in PIECES[4:]:
        there = exists(piece, 1)

        @pl.when(there)
        def _(piece=piece):
            greet(c + piece[2], f + piece[3])

        expected = expected + there.astype(jnp.int32)

    fetched(0, 3, 4)
    sb[...] = dot(sel[Q0:PERM0], vol[...]).astype(BF16)
    swapped = dot(sel[SWAP0:EYE0], dout[...]).astype(BF16).reshape(16, 16, 128)
    down[...] = swapped
    g[:, pl.ds(c, 1)] = swapped[:, None]
    xx[0] = jnp.zeros(xx.shape[1:], BF16)
    xx[17] = jnp.zeros(xx.shape[1:], BF16)
    for k in range(3):
        gs[k, 0] = jnp.zeros(gs.shape[2:], BF16)
        gs[k, 17] = jnp.zeros(gs.shape[2:], BF16)

    fetched(2)
    turned = dot_t(sel[EYE0 : EYE0 + 32, :32], wdt[...]).astype(BF16)
    wl[:, :432] = turned
    wl[:, 432:] = jnp.zeros((32, 80), BF16)

    pl.semaphore_wait(barrier, expected)
    for j, piece in enumerate(PIECES):

        @pl.when(exists(piece, 1))
        def _(j=j):
            halo_copy(j).start()

    for step in (1, -1):

        @pl.when(is_cin(c + step))
        def _(step=step):
            g_copy(c + step, c).start()

    send(NC, c, w_copy)
    wall[c] = wl[...]

    fetched(1, 6)
    rows = jnp.concatenate([wet[...].astype(F32).reshape(108, 16), jnp.zeros((20, 16), F32)], 0)
    early = dot_t(sel[EYE0 : EYE0 + 16, :16], rows.astype(BF16)).astype(BF16)
    for y in range(8):
        te[y * 16 : (y + 1) * 16, :] = dot(early, taps[:, y * 512 : (y + 1) * 512]).astype(BF16)

    for j, piece in enumerate(PIECES):

        @pl.when(exists(piece, -1))
        def _(j=j):
            halo_copy(j).wait_recv()

    fetched(5)
    cells = dot(slab[:, :256], vol[...]) + dot(slab[:, 256:448], halo[...])
    for k, shifted in enumerate((moved(cells, 1), cells, moved(cells, -1))):
        shifted = shifted.astype(BF16)
        for xs in range(10):
            vs[xs * 144 + k * 48 : xs * 144 + k * 48 + 48, :] = shifted[xs * 48 : xs * 48 + 48]
    vs[1440:1584, :] = jnp.zeros((144, 256), BF16)

    @pl.loop(0, 4)
    def _(a):
        total = jnp.zeros((128, 256), F32)
        for x in range(2):
            at = pl.multiple_of((2 * a + x) * 144, 16)
            pre = dot(te[...], vs[pl.ds(at, 512), :])
            factor = jnp.where(pre > 0, 1.0, slope)
            fac[2 * a + x] = factor
            total += pre * factor
        for b in range(4):
            pooled[a, b * 16 : b * 16 + 16] = (
                total[b * 32 : b * 32 + 16] + total[b * 32 + 16 : b * 32 + 32]
            )

    pair = sel[PAIR0:END0]
    field = pooled[...].reshape(256, 256)
    high = field.astype(BF16)
    low = (field - high.astype(F32)).astype(BF16)
    means = ((dot_t(high, pair) + dot_t(low, pair)) * 0.125).astype(BF16)
    local = dot(sel[PERM0:UP0], means).astype(BF16).reshape(8, 32, 128)
    dl[...] = local
    send(NC, c, dl_copy)
    xx[1 + f, c] = dl[c]

    def far(k):
        return (k < c - 1) | (k > c + 1)

    @pl.loop(0, NC)
    def _(to):
        @pl.when(far(to))
        def _():
            g_copy(to, c).start()

    receive(NC, c, w_copy)
    for a in range(3):
        of = c + 1 - a
        if a != 1:

            @pl.when(is_cin(of))
            def _(of=of):
                g_copy(of, of).wait_recv()

            @pl.when(jnp.logical_not(is_cin(of)))
            def _(a=a):
                gh[a] = jnp.zeros(gh.shape[1:], BF16)

        @pl.when(is_cin(of))
        def _(a=a, of=of):
            plain = g[:, pl.ds(of, 1)].reshape(256, 128)
            wide = plain.astype(F32)
            parts = (moved(wide, -1).astype(BF16), plain, moved(wide, 1).astype(BF16))
            for v in range(16):
                for k in range(3):
                    gh[a, 16 - v, k * 16 : k * 16 + 16] = parts[k][v * 16 : v * 16 + 16]

            for edge in (0, 17):
                gh[a, edge] = jnp.zeros((48, 128), BF16)

    def chip_at(k):
        return 2 * lax.rem(z + 1 + k, 4) + lax.rem(xh + 1 + k // 4, 2)

    def combine(k):
        to = chip_at(k)
        pr_copy(to).wait_recv()
        total = (own[to] + pr[to].astype(F32)).astype(BF16)

        @pl.when(to // 2 != z)
        def _():
            q[to] = total
            rr_copy(to).start()

        @pl.when(to // 2 == z)
        def _():
            rr[lax.rem(to, 2), z] = total

    def dgrad(k):
        to = chip_at(k)
        v = 2 * to
        low = [gh[a, pl.ds(15 - v, 3)].reshape(144, 128) for a in range(3)]
        high = [gh[a, pl.ds(14 - v, 3)].reshape(144, 128) for a in range(3)]
        both = jnp.concatenate([jnp.concatenate(low, 0), jnp.concatenate(high, 0)], 1)
        out = dot(wall[...].reshape(256, 512)[:, :432], both)
        first, second = out[:, :128], out[:, 128:]
        r[to] = jnp.where(core == 0, second, first).astype(BF16)
        pr_copy(to).start()
        own[to] = jnp.where(core == 0, first, second)

        @pl.when(k >= 2)
        def _():
            combine(k - 2)

    pl.loop(0, 3)(dgrad)
    receive(NC, c, dl_copy)
    across_copy(f).start()
    each(4, z, lambda to: z_copy(to, f, 0).start())
    mate_copy(f).start()
    pl.loop(3, 8)(dgrad)
    combine(6)
    combine(7)
    across_copy(across).wait_recv()
    each(4, z, lambda to: z_copy(to, across, 1).start())
    mate_copy(across).start()

    fetched(8)
    for u in range(8):
        columns = slice(u * 256, (u + 1) * 256)
        wide = dot(wdt[0:144], band[0:32, columns])
        wide += dot(wdt[144:288], band[32:64, columns])
        wide += dot(wdt[288:432], band[64:96, columns])
        wide = wide.astype(BF16)
        for b in range(3):
            for k in range(3):
                block = wide[(b * 3 + k) * 16 : (b * 3 + k) * 16 + 16]
                tw[k, u * 16 : u * 16 + 16, b * 256 : (b + 1) * 256] = block

    @pl.loop(0, NC)
    def _(of):
        @pl.when(far(of))
        def _():
            g_copy(of, of).wait_recv()

    @pl.loop(0, 16)
    def _(v):
        plain = g[v].reshape(128, 128)
        wide = plain.astype(F32)
        gs[0, v + 1] = moved(wide, -1).astype(BF16)
        gs[1, v + 1] = plain
        gs[2, v + 1] = moved(wide, 1).astype(BF16)

    def summed(x):
        each(4, z, lambda of: rr_wait(x, of))
        total = rr[x, 0].astype(F32)
        for k in range(1, 4):
            total += rr[x, k].astype(F32)
        return total

    def pass_on(of, side):
        block = 4 * of + lax.rem(side, 4)
        z_copy(of, block, 0).wait_recv()
        mate_copy(block).start()

    each(4, z, lambda of: pass_on(of, f))
    xsum[...] = summed(1 - xh).astype(BF16)
    sum_copy().start()
    each(4, z, lambda of: pass_on(of, across))

    total = summed(xh)
    sum_copy().wait_recv()
    total += xgot[...].astype(F32)
    spread = dot(sel[UP0:SWAP0], total.astype(BF16)).astype(BF16)
    up[...] = (dot(spread, pair) * 0.125).reshape(4, 128, 256)
    ae[...] = jnp.zeros_like(ae)

    @pl.loop(0, 4)
    def _(a):
        for x in range(2):
            at = pl.multiple_of((2 * a + x) * 144, 16)
            grad = (up[a] * fac[2 * a + x]).astype(BF16)
            ae[...] += dot_t(grad, vs[pl.ds(at, 512), :])

    rest = jnp.concatenate([ae[y * 16 : (y + 1) * 16] for y in range(8)], 1)
    pieces = []
    for _ in range(3):
        pieces.append(rest.astype(BF16))
        rest = rest - pieces[-1].astype(F32)
    fetched(7)
    mine = dot(jnp.concatenate(pieces, 0), back[...])
    mine = mine[:16] + mine[16:32] + mine[32:]
    ar1[f] = mine
    send(NF, f, a1_copy)

    @pl.loop(0, 8)
    def _(k):
        mate_copy(2 * k + 1 - core).wait_recv()

    def pair_of_rows(v):
        return jnp.concatenate(
            [xx[pl.ds(v, 3)].reshape(768, 128), xx[pl.ds(v + 1, 3)].reshape(768, 128)], 1
        )

    def forward(k):
        v = 2 * k
        out = dot(tw[...].reshape(384, 768), pair_of_rows(v))
        for h in range(2):
            half = out[:, h * 128 : (h + 1) * 128]
            total = moved(half[:128], 1) + half[128:256] + moved(half[256:], -1)
            po[:, v + h] = total.astype(BF16).reshape(8, 16, 128)

    pl.loop(0, 4)(forward)
    send(NC, c, ro_half(0))
    pl.loop(4, 8)(forward)
    send(NC, c, ro_half(1))
    ro[c] = po[c]

    receive(NF, f, a1_copy)
    total = ar1[0]
    for k in range(1, NF):
        total += ar1[k]
    ar2[c] = total
    send(NC, c, a2_copy)

    acc[...] = jnp.zeros_like(acc)

    @pl.loop(0, 8)
    def _(k):
        v = 2 * k
        both = jnp.concatenate(
            [gs[:, v + 1].reshape(384, 128), gs[:, v + 2].reshape(384, 128)], 1
        )
        acc[...] += dot_t(both, pair_of_rows(v))

    receive(NC, c, ro_half(0))
    receive(NC, c, ro_half(1))
    total = ro[0].astype(F32)
    for k in range(1, NC):
        total += ro[k].astype(F32)
    rounded = total.astype(BF16).reshape(256, 128)
    deep_out[...] = dot(sel[SWAP0:EYE0], rounded).astype(BF16)

    lane = lax.broadcasted_iota(jnp.int32, (16, 256), 1)
    for k in range(3):
        for b in range(3):
            total = jnp.zeros((16, 256), F32)
            for u in range(8):
                rows = acc[k * 128 + u * 16 : k * 128 + u * 16 + 16, b * 256 : (b + 1) * 256]
                rows = pltpu.roll(rows, (-(u - 1) * 32) % 256, 1) if u != 1 else rows
                if u == 0:
                    rows = jnp.where(lane < 32, 0.0, rows)
                if u == 7:
                    rows = jnp.where(lane >= 64, 0.0, rows)
                total += rows
            for a in range(3):
                at = ((a * 3 + b) * 3 + k) * 16
                grad_deep[at : at + 16, :] = total[:, a * 32 : (a + 1) * 32]

    receive(NC, c, a2_copy)
    total = ar2[0]
    for k in range(1, NC):
        total += ar2[k]
    square = jnp.concatenate([total, jnp.zeros((112, 128), F32)], 0)
    grad_early[...] = square.T[:108, :16].reshape(27, 4, 16)

    for j, piece in enumerate(PIECES):

        @pl.when(exists(piece, 1))
        def _(j=j):
            halo_copy(j).wait_send()

    sent(NC, c, g_copy)
    sent(NC, c, dl_copy)
    across_copy(f).wait_send()
    sum_copy().wait_send()
    for k in range(2):
        each(4, z, lambda to, k=k: z_copy(to, f, k).wait_send())
        each(4, z, lambda to, k=k: rr_copy(2 * to + k).wait_send())

    @pl.loop(0, 8)
    def _(k):
        mate_copy(2 * k + core).wait_send()
        pr_copy(k).wait_send()

    sent(NC, c, ro_half(0))
    sent(NC, c, ro_half(1))
    sent(NC, c, w_copy)
    sent(NF, f, a1_copy)
    sent(NC, c, a2_copy)


SCRATCH = (
    ((192, 256), BF16), ((192, 256), BF16), ((1584, 256), BF16), ((128, 512), BF16),
    ((8, 128, 256), F32), ((4, 64, 256), F32), ((8, 32, 128), BF16), ((18, 8, 32, 128), BF16),
    ((16, 16, 128), BF16), ((16, 8, 16, 128), BF16), ((3, 18, 128, 128), BF16), ((3, 18, 48, 128), BF16),
    ((32, 512), BF16), ((8, 32, 512), BF16), ((3, 128, 768), BF16), ((8, 256, 128), F32), ((8, 256, 128), BF16),
    ((8, 256, 128), BF16), ((8, 256, 128), BF16), ((2, 4, 256, 128), BF16),
    ((8, 16, 16, 128), BF16), ((8, 16, 16, 128), BF16),
    ((4, 128, 256), F32), ((128, 512), F32), ((384, 768), F32), ((16, 16, 128), F32), ((8, 16, 128), F32),
    ((256, 128), BF16), ((256, 128), BF16),
)
SEMAPHORES = (9, 8, 8, 8, 8, 8, 8, 8, 16, 2, 1, 16, 8, 8, 8, 8, 16, 16, 8, 8, 16, 16, 8, 8)
OPERANDS = (
    (256, 256), (27, 4, 16), (432, 32), (256, 128), (END0, 256), (480, 512), (128, 4096), (4096, 128), (96, 2048),
)


def hand_on(*refs):
    given, results, held, sems = refs[:3], refs[3:6], refs[6:9], refs[9]
    into = [pltpu.make_async_copy(given[k], held[k], sems.at[k]) for k in range(3)]
    out = [pltpu.make_async_copy(held[k], results[k], sems.at[3 + k]) for k in range(3)]
    for copy in into:
        copy.start()
    for k in range(3):
        into[k].wait()
        out[k].start()
    for copy in out:
        copy.wait()


def local(volume, early_w, deep_w, d_out):
    operands = [
        volume.reshape(256, 256),
        early_w.transpose(2, 3, 4, 1, 0).reshape(27, 4, 16),
        deep_w.transpose(2, 3, 4, 0, 1).reshape(432, 32),
        d_out.reshape(256, 128),
        *[jnp.asarray(t) for t in tables()],
    ]
    results = pl.pallas_call(
        kernel,
        out_shape=(
            jax.ShapeDtypeStruct((256, 128), BF16),
            jax.ShapeDtypeStruct((432, 32), F32),
            jax.ShapeDtypeStruct((27, 4, 16), F32),
        ),
        in_specs=[pl.BlockSpec(memory_space=pltpu.HBM)] * len(operands),
        out_specs=[pl.BlockSpec(memory_space=pltpu.VMEM)] * 3,
        scratch_shapes=[pltpu.VMEM(shape, BF16) for shape in OPERANDS]
        + [pltpu.VMEM(shape, dtype) for shape, dtype in SCRATCH]
        + [pltpu.SemaphoreType.DMA((count,)) for count in SEMAPHORES],
        compiler_params=pltpu.CompilerParams(
            collective_id=0, has_side_effects=True, vmem_limit_bytes=60 << 20
        ),
        name="cosmo",
    )(*operands)
    deep_out, grad_deep, grad_early = pl.pallas_call(
        hand_on,
        out_shape=[jax.ShapeDtypeStruct(x.shape, x.dtype) for x in results],
        in_specs=[pl.BlockSpec(memory_space=pl.ANY)] * 3,
        out_specs=[pl.BlockSpec(memory_space=pl.ANY)] * 3,
        scratch_shapes=[pltpu.VMEM(x.shape, x.dtype) for x in results]
        + [pltpu.SemaphoreType.DMA((6,))],
        name="results",
    )(*results)
    return (
        deep_out.reshape(16, 1, 16, 128),
        grad_deep.reshape(3, 3, 3, 16, 32).transpose(3, 4, 0, 1, 2),
        grad_early.reshape(3, 3, 3, 4, 16).transpose(4, 3, 0, 1, 2),
    )


def solution(mesh):
    in_specs = (
        P(None, "cin", "flt", None),
        P(),
        P("flt", "cin", None, None, None),
        P("flt", "cin", None, None),
    )
    out_specs = (P("flt", "cin", None, None), P("flt", "cin", None, None, None), P())
    return jax.shard_map(local, mesh=mesh, in_specs=in_specs, out_specs=out_specs, check_vma=False)
```

```python
import jax
import jax.numpy as jnp
import ml_dtypes
import numpy as np
from jax import lax
from jax.experimental import pallas as pl
from jax.experimental.pallas import tpu as pltpu
from jax.sharding import PartitionSpec as P

MESH = pl.DeviceIdType.MESH
F32, BF16 = jnp.float32, jnp.bfloat16
slope = 0.3
NC, NF = 8, 16

PIECES = (
    (0, 32, 1, 0), (32, 32, -1, 0), (64, 32, 0, 1), (96, 32, 0, -1),
    (128, 16, 1, 1), (144, 16, 1, -1), (160, 16, -1, 1), (176, 16, -1, -1),
)
Q0, PERM0, UP0, SWAP0, EYE0, PAIR0, END0 = 0, 192, 448, 960, 1216, 1472, 1600


def tables():
    sel = np.zeros((END0, 256), np.float32)
    for i in range(4):
        for y in range(8):
            sel[Q0 + i * 8 + y, i * 64 + 56 + y] = 1
            sel[Q0 + 32 + i * 8 + y, i * 64 + y] = 1
        for x in range(8):
            sel[Q0 + 64 + x * 4 + i, i * 64 + x * 8 + 7] = 1
            sel[Q0 + 96 + x * 4 + i, i * 64 + x * 8] = 1
        sel[Q0 + 128 + i, i * 64 + 63] = 1
        sel[Q0 + 144 + i, i * 64 + 56] = 1
        sel[Q0 + 160 + i, i * 64 + 7] = 1
        sel[Q0 + 176 + i, i * 64] = 1
    for a in range(4):
        for e in range(16):
            for b in range(4):
                sel[PERM0 + 16 * e + 4 * a + b, a * 64 + b * 16 + e] = 1
            for y in range(8):
                sel[UP0 + a * 128 + y * 16 + e, 16 * e + 4 * a + y // 2] = 1
    for v in range(16):
        for o in range(16):
            sel[SWAP0 + v * 16 + o, o * 16 + v] = 1
    sel[EYE0 : EYE0 + 256] = np.eye(256)
    for z in range(256):
        sel[PAIR0 + z // 2, z] = 1

    slab = np.zeros((480, 512), np.float32)
    for xs in range(10):
        x = xs - 1
        for i in range(4):
            for y in range(8):
                column = i * 64 + x * 8 + y if 0 <= x < 8 else 256 + (32 if x == 8 else 0) + i * 8 + y
                slab[xs * 48 + i * 8 + y, column] = 1
            low, high = (320 + x * 4, 352 + x * 4) if 0 <= x < 8 else ((384, 400) if x < 0 else (416, 432))
            slab[xs * 48 + 32 + i, low + i] = 1
            slab[xs * 48 + 36 + i, high + i] = 1

    taps = np.zeros((128, 8 * 512), np.float32)
    for y in range(8):
        for a in range(3):
            for b in range(3):
                for c in range(3):
                    for i in range(4):
                        row = y + b - 1
                        k = 32 + i if row < 0 else 36 + i if row > 7 else i * 8 + row
                        taps[(a * 9 + b * 3 + c) * 4 + i, y * 512 + a * 144 + c * 48 + k] = 1

    band = np.zeros((96, 8 * 256), np.float32)
    for u in range(8):
        for a in range(3):
            if 0 <= u + a - 1 < 8:
                for i in range(32):
                    band[a * 32 + i, u * 256 + (u + a - 1) * 32 + i] = 1
    return [t.astype(ml_dtypes.bfloat16) for t in (sel, slab, taps, taps.T, band)]


def dot(a, b):
    return jnp.dot(a, b, preferred_element_type=F32)


def dot_t(a, b):
    return lax.dot_general(a, b, (((1,), (1,)), ((), ())), preferred_element_type=F32)


def moved(value, step):
    width = value.shape[1]
    lane = lax.broadcasted_iota(jnp.int32, value.shape, 1)
    edge = 0 if step > 0 else width - 1
    return jnp.where(lane == edge, 0.0, pltpu.roll(value, step % width, 1))


def kernel(*refs):
    count = len(OPERANDS)
    given, refs = refs[:count], refs[count:]
    deep_out, grad_deep, grad_early = refs[:3]
    here, refs = refs[3 : 3 + count], refs[3 + count :]
    vol, wet, wdt, dout, sel, slab, taps, back, band = here
    (sb, halo, vs, te, fac, pooled, dl, xx, down, g, gs, gh, wl, wall, tw, own, r, pr, q, rr, po, ro, up, ae, acc,
     ar1, ar2, xsum, xgot) = refs[: len(SCRATCH)]
    (got, halo_s, halo_r, g_s, g_r, dl_s, dl_r, xx_s, xx_r, far_s, far_r, fw_s, pr_s, pr_r, rr_s, rr_r, ro_s, ro_r, w_s, w_r,
     a1_s, a1_r, a2_s, a2_r) = refs[len(SCRATCH) :]

    fetches = [pltpu.make_async_copy(given[k], here[k], got.at[k]) for k in range(count)]
    for k in (0, 3, 4, 2, 1, 6, 5, 8, 7):
        fetches[k].start()

    def fetched(*which):
        for k in which:
            fetches[k].wait()

    c, f = lax.axis_index("cin"), lax.axis_index("flt")
    chip, core = f // 2, lax.rem(f, 2)
    mate = f + 1 - 2 * core
    z, xh = chip // 2, lax.rem(chip, 2)
    across = f + 2 - 4 * xh

    def remote(src, dst, send, recv, to_c, to_f):
        return pltpu.make_async_remote_copy(
            src_ref=src, dst_ref=dst, send_sem=send, recv_sem=recv,
            device_id=(to_c, to_f), device_id_type=MESH,
        )

    def exists(piece, sign):
        to_c, to_f = c + sign * piece[2], f + sign * piece[3]
        return (to_c >= 0) & (to_c < NC) & (to_f >= 0) & (to_f < NF)

    def is_cin(k):
        return (k >= 0) & (k < NC)

    def halo_copy(j):
        first, rows, dc, df = PIECES[j]
        at = pl.ds(first, rows)
        return remote(sb.at[at], halo.at[at], halo_s.at[j], halo_r.at[j], c + dc, f + df)

    def g_copy(to, of):
        return remote(down, g.at[:, of], g_s.at[to], g_r.at[of], to, f)

    def dl_copy(to, of):
        return remote(dl.at[to], xx.at[1 + f, of], dl_s.at[to], dl_r.at[of], to, f)

    def at_z(to):
        return 4 * to + 2 * xh + core

    def across_copy(block):
        return remote(xx.at[1 + block], xx.at[1 + block], far_s.at[0], xx_r.at[block], c, across)

    def z_copy(to, block, k):
        return remote(xx.at[1 + block], xx.at[1 + block], xx_s.at[4 * k + to], xx_r.at[block], c, at_z(to))

    def mate_copy(block):
        return remote(xx.at[1 + block], xx.at[1 + block], fw_s.at[block], xx_r.at[block], c, mate)

    def pr_copy(k):
        return remote(r.at[k], pr.at[k], pr_s.at[k], pr_r.at[k], c, mate)

    def rr_copy(to):
        to_z, to_x = to // 2, lax.rem(to, 2)
        return remote(q.at[to], rr.at[to_x, z], rr_s.at[to], rr_r.at[4 * to_x + z], c, at_z(to_z))

    def rr_wait(x, of):
        remote(q.at[0], rr.at[x, of], rr_s.at[0], rr_r.at[4 * x + of], c, mate).wait_recv()

    def sum_copy():
        return remote(xsum, xgot, far_s.at[1], far_r.at[0], c, across)

    def ro_half(h):
        at = pl.ds(8 * h, 8)

        def ro_copy(to, of):
            return remote(po.at[to, at], ro.at[of, at], ro_s.at[8 * h + to], ro_r.at[8 * h + of], to, f)

        return ro_copy

    def w_copy(to, of):
        return remote(wl, wall.at[of], w_s.at[to], w_r.at[of], to, f)

    def a1_copy(to, of):
        return remote(ar1.at[of], ar1.at[of], a1_s.at[to], a1_r.at[of], c, to)

    def a2_copy(to, of):
        return remote(ar2.at[of], ar2.at[of], a2_s.at[to], a2_r.at[of], to, f)

    def each(count, me, act):
        @pl.loop(1, count)
        def _(k):
            act(lax.rem(me + k, count))

    def send(count, me, copy):
        each(count, me, lambda to: copy(to, me).start())

    def receive(count, me, copy):
        each(count, me, lambda of: copy(of, of).wait_recv())

    def sent(count, me, copy):
        each(count, me, lambda to: copy(to, me).wait_send())

    halo[...] = jnp.zeros_like(halo)

    barrier = pltpu.get_barrier_semaphore()

    def greet(to_c, to_f):
        pl.semaphore_signal(barrier, inc=1, device_id=(to_c, to_f), device_id_type=MESH)

    each(NC, c, lambda to: greet(to, f))
    each(NF, f, lambda to: greet(c, to))
    expected = NC + NF - 2
    for piece in PIECES[4:]:
        there = exists(piece, 1)

        @pl.when(there)
        def _(piece=piece):
            greet(c + piece[2], f + piece[3])

        expected = expected + there.astype(jnp.int32)

    fetched(0, 3, 4)
    sb[...] = dot(sel[Q0:PERM0], vol[...]).astype(BF16)
    swapped = dot(sel[SWAP0:EYE0], dout[...]).astype(BF16).reshape(16, 16, 128)
    down[...] = swapped
    g[:, pl.ds(c, 1)] = swapped[:, None]
    xx[0] = jnp.zeros(xx.shape[1:], BF16)
    xx[17] = jnp.zeros(xx.shape[1:], BF16)
    for k in range(3):
        gs[k, 0] = jnp.zeros(gs.shape[2:], BF16)
        gs[k, 17] = jnp.zeros(gs.shape[2:], BF16)

    fetched(2)
    turned = dot_t(sel[EYE0 : EYE0 + 32, :32], wdt[...]).astype(BF16)
    wl[:, :432] = turned
    wl[:, 432:] = jnp.zeros((32, 80), BF16)

    pl.semaphore_wait(barrier, expected)
    for j, piece in enumerate(PIECES):

        @pl.when(exists(piece, 1))
        def _(j=j):
            halo_copy(j).start()

    for step in (1, -1):

        @pl.when(is_cin(c + step))
        def _(step=step):
            g_copy(c + step, c).start()

    send(NC, c, w_copy)
    wall[c] = wl[...]

    fetched(1, 6)
    rows = jnp.concatenate([wet[...].astype(F32).reshape(108, 16), jnp.zeros((20, 16), F32)], 0)
    early = dot_t(sel[EYE0 : EYE0 + 16, :16], rows.astype(BF16)).astype(BF16)
    for y in range(8):
        te[y * 16 : (y + 1) * 16, :] = dot(early, taps[:, y * 512 : (y + 1) * 512]).astype(BF16)

    for j, piece in enumerate(PIECES):

        @pl.when(exists(piece, -1))
        def _(j=j):
            halo_copy(j).wait_recv()

    fetched(5)
    cells = dot(slab[:, :256], vol[...]) + dot(slab[:, 256:448], halo[...])
    for k, shifted in enumerate((moved(cells, 1), cells, moved(cells, -1))):
        shifted = shifted.astype(BF16)
        for xs in range(10):
            vs[xs * 144 + k * 48 : xs * 144 + k * 48 + 48, :] = shifted[xs * 48 : xs * 48 + 48]
    vs[1440:1584, :] = jnp.zeros((144, 256), BF16)

    @pl.loop(0, 4)
    def _(a):
        total = jnp.zeros((128, 256), F32)
        for x in range(2):
            at = pl.multiple_of((2 * a + x) * 144, 16)
            pre = dot(te[...], vs[pl.ds(at, 512), :])
            factor = jnp.where(pre > 0, 1.0, slope)
            fac[2 * a + x] = factor
            total += pre * factor
        for b in range(4):
            pooled[a, b * 16 : b * 16 + 16] = (
                total[b * 32 : b * 32 + 16] + total[b * 32 + 16 : b * 32 + 32]
            )

    pair = sel[PAIR0:END0]
    field = pooled[...].reshape(256, 256)
    high = field.astype(BF16)
    low = (field - high.astype(F32)).astype(BF16)
    means = ((dot_t(high, pair) + dot_t(low, pair)) * 0.125).astype(BF16)
    local = dot(sel[PERM0:UP0], means).astype(BF16).reshape(8, 32, 128)
    dl[...] = local
    send(NC, c, dl_copy)
    xx[1 + f, c] = dl[c]

    def far(k):
        return (k < c - 1) | (k > c + 1)

    @pl.loop(0, NC)
    def _(to):
        @pl.when(far(to))
        def _():
            g_copy(to, c).start()

    receive(NC, c, w_copy)
    for a in range(3):
        of = c + 1 - a
        if a != 1:

            @pl.when(is_cin(of))
            def _(of=of):
                g_copy(of, of).wait_recv()

            @pl.when(jnp.logical_not(is_cin(of)))
            def _(a=a):
                gh[a] = jnp.zeros(gh.shape[1:], BF16)

        @pl.when(is_cin(of))
        def _(a=a, of=of):
            plain = g[:, pl.ds(of, 1)].reshape(256, 128)
            wide = plain.astype(F32)
            parts = (moved(wide, -1).astype(BF16), plain, moved(wide, 1).astype(BF16))
            for v in range(16):
                for k in range(3):
                    gh[a, 16 - v, k * 16 : k * 16 + 16] = parts[k][v * 16 : v * 16 + 16]

            for edge in (0, 17):
                gh[a, edge] = jnp.zeros((48, 128), BF16)

    def chip_at(k):
        return 2 * lax.rem(z + 1 + k, 4) + lax.rem(xh + 1 + k // 4, 2)

    def combine(k):
        to = chip_at(k)
        pr_copy(to).wait_recv()
        total = (own[to] + pr[to].astype(F32)).astype(BF16)

        @pl.when(to // 2 != z)
        def _():
            q[to] = total
            rr_copy(to).start()

        @pl.when(to // 2 == z)
        def _():
            rr[lax.rem(to, 2), z] = total

    def dgrad(k):
        to = chip_at(k)
        v = 2 * to
        low = [gh[a, pl.ds(15 - v, 3)].reshape(144, 128) for a in range(3)]
        high = [gh[a, pl.ds(14 - v, 3)].reshape(144, 128) for a in range(3)]
        both = jnp.concatenate([jnp.concatenate(low, 0), jnp.concatenate(high, 0)], 1)
        out = dot(wall[...].reshape(256, 512)[:, :432], both)
        first, second = out[:, :128], out[:, 128:]
        r[to] = jnp.where(core == 0, second, first).astype(BF16)
        pr_copy(to).start()
        own[to] = jnp.where(core == 0, first, second)

        @pl.when(k >= 2)
        def _():
            combine(k - 2)

    receive(NC, c, dl_copy)
    across_copy(f).start()
    each(4, z, lambda to: z_copy(to, f, 0).start())
    mate_copy(f).start()
    pl.loop(0, 8)(dgrad)
    combine(6)
    combine(7)
    across_copy(across).wait_recv()
    each(4, z, lambda to: z_copy(to, across, 1).start())
    mate_copy(across).start()

    fetched(8)
    for u in range(8):
        columns = slice(u * 256, (u + 1) * 256)
        wide = dot(wdt[0:144], band[0:32, columns])
        wide += dot(wdt[144:288], band[32:64, columns])
        wide += dot(wdt[288:432], band[64:96, columns])
        wide = wide.astype(BF16)
        for b in range(3):
            for k in range(3):
                block = wide[(b * 3 + k) * 16 : (b * 3 + k) * 16 + 16]
                tw[k, u * 16 : u * 16 + 16, b * 256 : (b + 1) * 256] = block

    @pl.loop(0, NC)
    def _(of):
        @pl.when(far(of))
        def _():
            g_copy(of, of).wait_recv()

    @pl.loop(0, 16)
    def _(v):
        plain = g[v].reshape(128, 128)
        wide = plain.astype(F32)
        gs[0, v + 1] = moved(wide, -1).astype(BF16)
        gs[1, v + 1] = plain
        gs[2, v + 1] = moved(wide, 1).astype(BF16)

    def summed(x):
        each(4, z, lambda of: rr_wait(x, of))
        total = rr[x, 0].astype(F32)
        for k in range(1, 4):
            total += rr[x, k].astype(F32)
        return total

    def pass_on(of, side):
        block = 4 * of + lax.rem(side, 4)
        z_copy(of, block, 0).wait_recv()
        mate_copy(block).start()

    each(4, z, lambda of: pass_on(of, f))
    xsum[...] = summed(1 - xh).astype(BF16)
    sum_copy().start()
    each(4, z, lambda of: pass_on(of, across))

    total = summed(xh)
    sum_copy().wait_recv()
    total += xgot[...].astype(F32)
    spread = dot(sel[UP0:SWAP0], total.astype(BF16)).astype(BF16)
    up[...] = (dot(spread, pair) * 0.125).reshape(4, 128, 256)
    ae[...] = jnp.zeros_like(ae)

    @pl.loop(0, 4)
    def _(a):
        for x in range(2):
            at = pl.multiple_of((2 * a + x) * 144, 16)
            grad = (up[a] * fac[2 * a + x]).astype(BF16)
            ae[...] += dot_t(grad, vs[pl.ds(at, 512), :])

    rest = jnp.concatenate([ae[y * 16 : (y + 1) * 16] for y in range(8)], 1)
    pieces = []
    for _ in range(3):
        pieces.append(rest.astype(BF16))
        rest = rest - pieces[-1].astype(F32)
    fetched(7)
    mine = dot(jnp.concatenate(pieces, 0), back[...])
    mine = mine[:16] + mine[16:32] + mine[32:]
    ar1[f] = mine
    send(NF, f, a1_copy)

    @pl.loop(0, 8)
    def _(k):
        mate_copy(2 * k + 1 - core).wait_recv()

    def pair_of_rows(v):
        return jnp.concatenate(
            [xx[pl.ds(v, 3)].reshape(768, 128), xx[pl.ds(v + 1, 3)].reshape(768, 128)], 1
        )

    def forward(k):
        v = 2 * k
        out = dot(tw[...].reshape(384, 768), pair_of_rows(v))
        for h in range(2):
            half = out[:, h * 128 : (h + 1) * 128]
            total = moved(half[:128], 1) + half[128:256] + moved(half[256:], -1)
            po[:, v + h] = total.astype(BF16).reshape(8, 16, 128)

    pl.loop(0, 4)(forward)
    send(NC, c, ro_half(0))
    pl.loop(4, 8)(forward)
    send(NC, c, ro_half(1))
    ro[c] = po[c]

    receive(NF, f, a1_copy)
    total = ar1[0]
    for k in range(1, NF):
        total += ar1[k]
    ar2[c] = total
    send(NC, c, a2_copy)

    acc[...] = jnp.zeros_like(acc)

    @pl.loop(0, 8)
    def _(k):
        v = 2 * k
        both = jnp.concatenate(
            [gs[:, v + 1].reshape(384, 128), gs[:, v + 2].reshape(384, 128)], 1
        )
        acc[...] += dot_t(both, pair_of_rows(v))

    receive(NC, c, ro_half(0))
    receive(NC, c, ro_half(1))
    total = ro[0].astype(F32)
    for k in range(1, NC):
        total += ro[k].astype(F32)
    rounded = total.astype(BF16).reshape(256, 128)
    deep_out[...] = dot(sel[SWAP0:EYE0], rounded).astype(BF16)

    lane = lax.broadcasted_iota(jnp.int32, (16, 256), 1)
    for k in range(3):
        for b in range(3):
            total = jnp.zeros((16, 256), F32)
            for u in range(8):
                rows = acc[k * 128 + u * 16 : k * 128 + u * 16 + 16, b * 256 : (b + 1) * 256]
                rows = pltpu.roll(rows, (-(u - 1) * 32) % 256, 1) if u != 1 else rows
                if u == 0:
                    rows = jnp.where(lane < 32, 0.0, rows)
                if u == 7:
                    rows = jnp.where(lane >= 64, 0.0, rows)
                total += rows
            for a in range(3):
                at = ((a * 3 + b) * 3 + k) * 16
                grad_deep[at : at + 16, :] = total[:, a * 32 : (a + 1) * 32]

    receive(NC, c, a2_copy)
    total = ar2[0]
    for k in range(1, NC):
        total += ar2[k]
    square = jnp.concatenate([total, jnp.zeros((112, 128), F32)], 0)
    grad_early[...] = square.T[:108, :16].reshape(27, 4, 16)

    for j, piece in enumerate(PIECES):

        @pl.when(exists(piece, 1))
        def _(j=j):
            halo_copy(j).wait_send()

    sent(NC, c, g_copy)
    sent(NC, c, dl_copy)
    across_copy(f).wait_send()
    sum_copy().wait_send()
    for k in range(2):
        each(4, z, lambda to, k=k: z_copy(to, f, k).wait_send())
        each(4, z, lambda to, k=k: rr_copy(2 * to + k).wait_send())

    @pl.loop(0, 8)
    def _(k):
        mate_copy(2 * k + core).wait_send()
        pr_copy(k).wait_send()

    sent(NC, c, ro_half(0))
    sent(NC, c, ro_half(1))
    sent(NC, c, w_copy)
    sent(NF, f, a1_copy)
    sent(NC, c, a2_copy)


SCRATCH = (
    ((192, 256), BF16), ((192, 256), BF16), ((1584, 256), BF16), ((128, 512), BF16),
    ((8, 128, 256), F32), ((4, 64, 256), F32), ((8, 32, 128), BF16), ((18, 8, 32, 128), BF16),
    ((16, 16, 128), BF16), ((16, 8, 16, 128), BF16), ((3, 18, 128, 128), BF16), ((3, 18, 48, 128), BF16),
    ((32, 512), BF16), ((8, 32, 512), BF16), ((3, 128, 768), BF16), ((8, 256, 128), F32), ((8, 256, 128), BF16),
    ((8, 256, 128), BF16), ((8, 256, 128), BF16), ((2, 4, 256, 128), BF16),
    ((8, 16, 16, 128), BF16), ((8, 16, 16, 128), BF16),
    ((4, 128, 256), F32), ((128, 512), F32), ((384, 768), F32), ((16, 16, 128), F32), ((8, 16, 128), F32),
    ((256, 128), BF16), ((256, 128), BF16),
)
SEMAPHORES = (9, 8, 8, 8, 8, 8, 8, 8, 16, 2, 1, 16, 8, 8, 8, 8, 16, 16, 8, 8, 16, 16, 8, 8)
OPERANDS = (
    (256, 256), (27, 4, 16), (432, 32), (256, 128), (END0, 256), (480, 512), (128, 4096), (4096, 128), (96, 2048),
)


def hand_on(*refs):
    given, results, held, sems = refs[:3], refs[3:6], refs[6:9], refs[9]
    into = [pltpu.make_async_copy(given[k], held[k], sems.at[k]) for k in range(3)]
    out = [pltpu.make_async_copy(held[k], results[k], sems.at[3 + k]) for k in range(3)]
    for copy in into:
        copy.start()
    for k in range(3):
        into[k].wait()
        out[k].start()
    for copy in out:
        copy.wait()


def local(volume, early_w, deep_w, d_out):
    operands = [
        volume.reshape(256, 256),
        early_w.transpose(2, 3, 4, 1, 0).reshape(27, 4, 16),
        deep_w.transpose(2, 3, 4, 0, 1).reshape(432, 32),
        d_out.reshape(256, 128),
        *[jnp.asarray(t) for t in tables()],
    ]
    results = pl.pallas_call(
        kernel,
        out_shape=(
            jax.ShapeDtypeStruct((256, 128), BF16),
            jax.ShapeDtypeStruct((432, 32), F32),
            jax.ShapeDtypeStruct((27, 4, 16), F32),
        ),
        in_specs=[pl.BlockSpec(memory_space=pltpu.HBM)] * len(operands),
        out_specs=[pl.BlockSpec(memory_space=pltpu.VMEM)] * 3,
        scratch_shapes=[pltpu.VMEM(shape, BF16) for shape in OPERANDS]
        + [pltpu.VMEM(shape, dtype) for shape, dtype in SCRATCH]
        + [pltpu.SemaphoreType.DMA((count,)) for count in SEMAPHORES],
        compiler_params=pltpu.CompilerParams(
            collective_id=0, has_side_effects=True, vmem_limit_bytes=60 << 20
        ),
        name="cosmo",
    )(*operands)
    deep_out, grad_deep, grad_early = pl.pallas_call(
        hand_on,
        out_shape=[jax.ShapeDtypeStruct(x.shape, x.dtype) for x in results],
        in_specs=[pl.BlockSpec(memory_space=pl.ANY)] * 3,
        out_specs=[pl.BlockSpec(memory_space=pl.ANY)] * 3,
        scratch_shapes=[pltpu.VMEM(x.shape, x.dtype) for x in results]
        + [pltpu.SemaphoreType.DMA((6,))],
        name="results",
    )(*results)
    return (
        deep_out.reshape(16, 1, 16, 128),
        grad_deep.reshape(3, 3, 3, 16, 32).transpose(3, 4, 0, 1, 2),
        grad_early.reshape(3, 3, 3, 4, 16).transpose(4, 3, 0, 1, 2),
    )


def solution(mesh):
    in_specs = (
        P(None, "cin", "flt", None),
        P(),
        P("flt", "cin", None, None, None),
        P("flt", "cin", None, None),
    )
    out_specs = (P("flt", "cin", None, None), P("flt", "cin", None, None, None), P())
    return jax.shard_map(local, mesh=mesh, in_specs=in_specs, out_specs=out_specs, check_vma=False)
```

```python
import jax
import jax.numpy as jnp
import ml_dtypes
import numpy as np
from jax import lax
from jax.experimental import pallas as pl
from jax.experimental.pallas import tpu as pltpu
from jax.sharding import PartitionSpec as P

MESH = pl.DeviceIdType.MESH
F32, BF16 = jnp.float32, jnp.bfloat16
slope = 0.3
NC, NF = 8, 16

PIECES = (
    (0, 32, 1, 0), (32, 32, -1, 0), (64, 32, 0, 1), (96, 32, 0, -1),
    (128, 16, 1, 1), (144, 16, 1, -1), (160, 16, -1, 1), (176, 16, -1, -1),
)
Q0, PERM0, UP0, SWAP0, EYE0, PAIR0, END0 = 0, 192, 448, 960, 1216, 1472, 1600


def tables():
    sel = np.zeros((END0, 256), np.float32)
    for i in range(4):
        for y in range(8):
            sel[Q0 + i * 8 + y, i * 64 + 56 + y] = 1
            sel[Q0 + 32 + i * 8 + y, i * 64 + y] = 1
        for x in range(8):
            sel[Q0 + 64 + x * 4 + i, i * 64 + x * 8 + 7] = 1
            sel[Q0 + 96 + x * 4 + i, i * 64 + x * 8] = 1
        sel[Q0 + 128 + i, i * 64 + 63] = 1
        sel[Q0 + 144 + i, i * 64 + 56] = 1
        sel[Q0 + 160 + i, i * 64 + 7] = 1
        sel[Q0 + 176 + i, i * 64] = 1
    for a in range(4):
        for e in range(16):
            for b in range(4):
                sel[PERM0 + 16 * e + 4 * a + b, a * 64 + b * 16 + e] = 1
            for y in range(8):
                sel[UP0 + a * 128 + y * 16 + e, 16 * e + 4 * a + y // 2] = 1
    for v in range(16):
        for o in range(16):
            sel[SWAP0 + v * 16 + o, o * 16 + v] = 1
    sel[EYE0 : EYE0 + 256] = np.eye(256)
    for z in range(256):
        sel[PAIR0 + z // 2, z] = 1

    slab = np.zeros((480, 512), np.float32)
    for xs in range(10):
        x = xs - 1
        for i in range(4):
            for y in range(8):
                column = i * 64 + x * 8 + y if 0 <= x < 8 else 256 + (32 if x == 8 else 0) + i * 8 + y
                slab[xs * 48 + i * 8 + y, column] = 1
            low, high = (320 + x * 4, 352 + x * 4) if 0 <= x < 8 else ((384, 400) if x < 0 else (416, 432))
            slab[xs * 48 + 32 + i, low + i] = 1
            slab[xs * 48 + 36 + i, high + i] = 1

    taps = np.zeros((128, 8 * 512), np.float32)
    for y in range(8):
        for a in range(3):
            for b in range(3):
                for c in range(3):
                    for i in range(4):
                        row = y + b - 1
                        k = 32 + i if row < 0 else 36 + i if row > 7 else i * 8 + row
                        taps[(a * 9 + b * 3 + c) * 4 + i, y * 512 + a * 144 + c * 48 + k] = 1

    band = np.zeros((96, 8 * 256), np.float32)
    for u in range(8):
        for a in range(3):
            if 0 <= u + a - 1 < 8:
                for i in range(32):
                    band[a * 32 + i, u * 256 + (u + a - 1) * 32 + i] = 1
    return [t.astype(ml_dtypes.bfloat16) for t in (sel, slab, taps, taps.T, band)]


def dot(a, b):
    return jnp.dot(a, b, preferred_element_type=F32)


def dot_t(a, b):
    return lax.dot_general(a, b, (((1,), (1,)), ((), ())), preferred_element_type=F32)


def moved(value, step):
    width = value.shape[1]
    lane = lax.broadcasted_iota(jnp.int32, value.shape, 1)
    edge = 0 if step > 0 else width - 1
    return jnp.where(lane == edge, 0.0, pltpu.roll(value, step % width, 1))


def kernel(*refs):
    count = len(OPERANDS)
    given, refs = refs[:count], refs[count:]
    deep_out, grad_deep, grad_early = refs[:3]
    here, refs = refs[3 : 3 + count], refs[3 + count :]
    vol, wet, wdt, dout, sel, slab, taps, back, band = here
    (sb, halo, vs, te, fac, pooled, dl, xx, down, g, gs, gh, wl, wall, tw, own, r, pr, q, rr, po, ro, up, ae, acc,
     ar1, ar2, xsum, xgot) = refs[: len(SCRATCH)]
    (got, halo_s, halo_r, g_s, g_r, dl_s, dl_r, xx_s, xx_r, far_s, far_r, fw_s, pr_s, pr_r, rr_s, rr_r, ro_s, ro_r, w_s, w_r,
     a1_s, a1_r, a2_s, a2_r) = refs[len(SCRATCH) :]

    fetches = [pltpu.make_async_copy(given[k], here[k], got.at[k]) for k in range(count)]
    for k in (0, 3, 4, 2, 1, 6, 5, 8, 7):
        fetches[k].start()

    def fetched(*which):
        for k in which:
            fetches[k].wait()

    c, f = lax.axis_index("cin"), lax.axis_index("flt")
    chip, core = f // 2, lax.rem(f, 2)
    mate = f + 1 - 2 * core
    z, xh = chip // 2, lax.rem(chip, 2)
    across = f + 2 - 4 * xh

    def remote(src, dst, send, recv, to_c, to_f):
        return pltpu.make_async_remote_copy(
            src_ref=src, dst_ref=dst, send_sem=send, recv_sem=recv,
            device_id=(to_c, to_f), device_id_type=MESH,
        )

    def exists(piece, sign):
        to_c, to_f = c + sign * piece[2], f + sign * piece[3]
        return (to_c >= 0) & (to_c < NC) & (to_f >= 0) & (to_f < NF)

    def is_cin(k):
        return (k >= 0) & (k < NC)

    def halo_copy(j):
        first, rows, dc, df = PIECES[j]
        at = pl.ds(first, rows)
        return remote(sb.at[at], halo.at[at], halo_s.at[j], halo_r.at[j], c + dc, f + df)

    def g_copy(to, of):
        return remote(down, g.at[:, of], g_s.at[to], g_r.at[of], to, f)

    def dl_copy(to, of):
        return remote(dl.at[to], xx.at[1 + f, of], dl_s.at[to], dl_r.at[of], to, f)

    def at_z(to):
        return 4 * to + 2 * xh + core

    def across_copy(block):
        return remote(xx.at[1 + block], xx.at[1 + block], far_s.at[0], xx_r.at[block], c, across)

    def z_copy(to, block, k):
        return remote(xx.at[1 + block], xx.at[1 + block], xx_s.at[4 * k + to], xx_r.at[block], c, at_z(to))

    def mate_copy(block):
        return remote(xx.at[1 + block], xx.at[1 + block], fw_s.at[block], xx_r.at[block], c, mate)

    def pr_copy(k):
        return remote(r.at[k], pr.at[k], pr_s.at[k], pr_r.at[k], c, mate)

    def rr_copy(to):
        to_z, to_x = to // 2, lax.rem(to, 2)
        return remote(q.at[to], rr.at[to_x, z], rr_s.at[to], rr_r.at[4 * to_x + z], c, at_z(to_z))

    def rr_wait(x, of):
        remote(q.at[0], rr.at[x, of], rr_s.at[0], rr_r.at[4 * x + of], c, mate).wait_recv()

    def sum_copy():
        return remote(xsum, xgot, far_s.at[1], far_r.at[0], c, across)

    def ro_half(h):
        at = pl.ds(8 * h, 8)

        def ro_copy(to, of):
            return remote(po.at[to, at], ro.at[of, at], ro_s.at[8 * h + to], ro_r.at[8 * h + of], to, f)

        return ro_copy

    def w_copy(to, of):
        return remote(wl, wall.at[of], w_s.at[to], w_r.at[of], to, f)

    def a1_copy(to, of):
        return remote(ar1.at[of], ar1.at[of], a1_s.at[to], a1_r.at[of], c, to)

    def a2_copy(to, of):
        return remote(ar2.at[of], ar2.at[of], a2_s.at[to], a2_r.at[of], to, f)

    def each(count, me, act):
        @pl.loop(1, count)
        def _(k):
            act(lax.rem(me + k, count))

    def send(count, me, copy):
        each(count, me, lambda to: copy(to, me).start())

    def receive(count, me, copy):
        each(count, me, lambda of: copy(of, of).wait_recv())

    def sent(count, me, copy):
        each(count, me, lambda to: copy(to, me).wait_send())

    halo[...] = jnp.zeros_like(halo)

    barrier = pltpu.get_barrier_semaphore()

    def greet(to_c, to_f):
        pl.semaphore_signal(barrier, inc=1, device_id=(to_c, to_f), device_id_type=MESH)

    each(NC, c, lambda to: greet(to, f))
    each(NF, f, lambda to: greet(c, to))
    expected = NC + NF - 2
    for piece in PIECES[4:]:
        there = exists(piece, 1)

        @pl.when(there)
        def _(piece=piece):
            greet(c + piece[2], f + piece[3])

        expected = expected + there.astype(jnp.int32)

    fetched(0, 3, 4)
    sb[...] = dot(sel[Q0:PERM0], vol[...]).astype(BF16)
    swapped = dot(sel[SWAP0:EYE0], dout[...]).astype(BF16).reshape(16, 16, 128)
    down[...] = swapped
    g[:, pl.ds(c, 1)] = swapped[:, None]
    xx[0] = jnp.zeros(xx.shape[1:], BF16)
    xx[17] = jnp.zeros(xx.shape[1:], BF16)
    for k in range(3):
        gs[k, 0] = jnp.zeros(gs.shape[2:], BF16)
        gs[k, 17] = jnp.zeros(gs.shape[2:], BF16)

    fetched(2)
    turned = dot_t(sel[EYE0 : EYE0 + 32, :32], wdt[...]).astype(BF16)
    wl[:, :432] = turned
    wl[:, 432:] = jnp.zeros((32, 80), BF16)

    pl.semaphore_wait(barrier, expected)
    for j, piece in enumerate(PIECES):

        @pl.when(exists(piece, 1))
        def _(j=j):
            halo_copy(j).start()

    for step in (1, -1):

        @pl.when(is_cin(c + step))
        def _(step=step):
            g_copy(c + step, c).start()

    send(NC, c, w_copy)
    wall[c] = wl[...]

    fetched(1, 6)
    rows = jnp.concatenate([wet[...].astype(F32).reshape(108, 16), jnp.zeros((20, 16), F32)], 0)
    early = dot_t(sel[EYE0 : EYE0 + 16, :16], rows.astype(BF16)).astype(BF16)
    for y in range(8):
        te[y * 16 : (y + 1) * 16, :] = dot(early, taps[:, y * 512 : (y + 1) * 512]).astype(BF16)

    for j, piece in enumerate(PIECES):

        @pl.when(exists(piece, -1))
        def _(j=j):
            halo_copy(j).wait_recv()

    fetched(5)
    cells = dot(slab[:, :256], vol[...]) + dot(slab[:, 256:448], halo[...])
    for k, shifted in enumerate((moved(cells, 1), cells, moved(cells, -1))):
        shifted = shifted.astype(BF16)
        for xs in range(10):
            vs[xs * 144 + k * 48 : xs * 144 + k * 48 + 48, :] = shifted[xs * 48 : xs * 48 + 48]
    vs[1440:1584, :] = jnp.zeros((144, 256), BF16)

    @pl.loop(0, 4)
    def _(a):
        total = jnp.zeros((128, 256), F32)
        for x in range(2):
            at = pl.multiple_of((2 * a + x) * 144, 16)
            pre = dot(te[...], vs[pl.ds(at, 512), :])
            factor = jnp.where(pre > 0, 1.0, slope)
            fac[2 * a + x] = factor
            total += pre * factor
        for b in range(4):
            pooled[a, b * 16 : b * 16 + 16] = (
                total[b * 32 : b * 32 + 16] + total[b * 32 + 16 : b * 32 + 32]
            )

    pair = sel[PAIR0:END0]
    field = pooled[...].reshape(256, 256)
    high = field.astype(BF16)
    low = (field - high.astype(F32)).astype(BF16)
    means = ((dot_t(high, pair) + dot_t(low, pair)) * 0.125).astype(BF16)
    local = dot(sel[PERM0:UP0], means).astype(BF16).reshape(8, 32, 128)
    dl[...] = local
    send(NC, c, dl_copy)
    xx[1 + f, c] = dl[c]

    def far(k):
        return (k < c - 1) | (k > c + 1)

    @pl.loop(0, NC)
    def _(to):
        @pl.when(far(to))
        def _():
            g_copy(to, c).start()

    receive(NC, c, w_copy)
    for a in range(3):
        of = c + 1 - a
        if a != 1:

            @pl.when(is_cin(of))
            def _(of=of):
                g_copy(of, of).wait_recv()

            @pl.when(jnp.logical_not(is_cin(of)))
            def _(a=a):
                gh[a] = jnp.zeros(gh.shape[1:], BF16)

        @pl.when(is_cin(of))
        def _(a=a, of=of):
            plain = g[:, pl.ds(of, 1)].reshape(256, 128)
            wide = plain.astype(F32)
            parts = (moved(wide, -1).astype(BF16), plain, moved(wide, 1).astype(BF16))
            for v in range(16):
                for k in range(3):
                    gh[a, 16 - v, k * 16 : k * 16 + 16] = parts[k][v * 16 : v * 16 + 16]

            for edge in (0, 17):
                gh[a, edge] = jnp.zeros((48, 128), BF16)

    def chip_at(k):
        return 2 * lax.rem(z + 1 + k, 4) + lax.rem(xh + 1 + k // 4, 2)

    def combine(k):
        to = chip_at(k)
        pr_copy(to).wait_recv()
        total = (own[to] + pr[to].astype(F32)).astype(BF16)

        @pl.when(to // 2 != z)
        def _():
            q[to] = total
            rr_copy(to).start()

        @pl.when(to // 2 == z)
        def _():
            rr[lax.rem(to, 2), z] = total

    def dgrad(k):
        to = chip_at(k)
        v = 2 * to
        low = [gh[a, pl.ds(15 - v, 3)].reshape(144, 128) for a in range(3)]
        high = [gh[a, pl.ds(14 - v, 3)].reshape(144, 128) for a in range(3)]
        both = jnp.concatenate([jnp.concatenate(low, 0), jnp.concatenate(high, 0)], 1)
        out = dot(wall[...].reshape(256, 512)[:, :432], both)
        first, second = out[:, :128], out[:, 128:]
        r[to] = jnp.where(core == 0, second, first).astype(BF16)
        pr_copy(to).start()
        own[to] = jnp.where(core == 0, first, second)

        @pl.when(k >= 2)
        def _():
            combine(k - 2)

    pl.loop(0, 3)(dgrad)
    receive(NC, c, dl_copy)
    across_copy(f).start()
    each(4, z, lambda to: z_copy(to, f, 0).start())
    mate_copy(f).start()
    pl.loop(3, 8)(dgrad)
    combine(6)
    combine(7)
    across_copy(across).wait_recv()
    each(4, z, lambda to: z_copy(to, across, 1).start())
    mate_copy(across).start()

    fetched(8)
    for u in range(8):
        columns = slice(u * 256, (u + 1) * 256)
        wide = dot(wdt[0:144], band[0:32, columns])
        wide += dot(wdt[144:288], band[32:64, columns])
        wide += dot(wdt[288:432], band[64:96, columns])
        wide = wide.astype(BF16)
        for b in range(3):
            for k in range(3):
                block = wide[(b * 3 + k) * 16 : (b * 3 + k) * 16 + 16]
                tw[k, u * 16 : u * 16 + 16, b * 256 : (b + 1) * 256] = block

    @pl.loop(0, NC)
    def _(of):
        @pl.when(far(of))
        def _():
            g_copy(of, of).wait_recv()

    @pl.loop(0, 16)
    def _(v):
        plain = g[v].reshape(128, 128)
        wide = plain.astype(F32)
        gs[0, v + 1] = moved(wide, -1).astype(BF16)
        gs[1, v + 1] = plain
        gs[2, v + 1] = moved(wide, 1).astype(BF16)

    def summed(x):
        each(4, z, lambda of: rr_wait(x, of))
        total = rr[x, 0].astype(F32)
        for k in range(1, 4):
            total += rr[x, k].astype(F32)
        return total

    xsum[...] = summed(1 - xh).astype(BF16)
    sum_copy().start()
    for x in range(2):
        side = f if x else across

        def pass_on(of, side=side):
            block = 4 * of + lax.rem(side, 4)
            z_copy(of, block, 0).wait_recv()
            mate_copy(block).start()

        each(4, z, pass_on)

    total = summed(xh)
    sum_copy().wait_recv()
    total += xgot[...].astype(F32)
    spread = dot(sel[UP0:SWAP0], total.astype(BF16)).astype(BF16)
    up[...] = (dot(spread, pair) * 0.125).reshape(4, 128, 256)
    ae[...] = jnp.zeros_like(ae)

    @pl.loop(0, 4)
    def _(a):
        for x in range(2):
            at = pl.multiple_of((2 * a + x) * 144, 16)
            grad = (up[a] * fac[2 * a + x]).astype(BF16)
            ae[...] += dot_t(grad, vs[pl.ds(at, 512), :])

    rest = jnp.concatenate([ae[y * 16 : (y + 1) * 16] for y in range(8)], 1)
    pieces = []
    for _ in range(3):
        pieces.append(rest.astype(BF16))
        rest = rest - pieces[-1].astype(F32)
    fetched(7)
    mine = dot(jnp.concatenate(pieces, 0), back[...])
    mine = mine[:16] + mine[16:32] + mine[32:]
    ar1[f] = mine
    send(NF, f, a1_copy)

    @pl.loop(0, 8)
    def _(k):
        mate_copy(2 * k + 1 - core).wait_recv()

    def pair_of_rows(v):
        return jnp.concatenate(
            [xx[pl.ds(v, 3)].reshape(768, 128), xx[pl.ds(v + 1, 3)].reshape(768, 128)], 1
        )

    def forward(k):
        v = 2 * k
        out = dot(tw[...].reshape(384, 768), pair_of_rows(v))
        for h in range(2):
            half = out[:, h * 128 : (h + 1) * 128]
            total = moved(half[:128], 1) + half[128:256] + moved(half[256:], -1)
            po[:, v + h] = total.astype(BF16).reshape(8, 16, 128)

    pl.loop(0, 4)(forward)
    send(NC, c, ro_half(0))
    pl.loop(4, 8)(forward)
    send(NC, c, ro_half(1))
    ro[c] = po[c]

    receive(NF, f, a1_copy)
    total = ar1[0]
    for k in range(1, NF):
        total += ar1[k]
    ar2[c] = total
    send(NC, c, a2_copy)

    acc[...] = jnp.zeros_like(acc)

    @pl.loop(0, 8)
    def _(k):
        v = 2 * k
        both = jnp.concatenate(
            [gs[:, v + 1].reshape(384, 128), gs[:, v + 2].reshape(384, 128)], 1
        )
        acc[...] += dot_t(both, pair_of_rows(v))

    lane = lax.broadcasted_iota(jnp.int32, (16, 256), 1)
    for k in range(3):
        for b in range(3):
            total = jnp.zeros((16, 256), F32)
            for u in range(8):
                rows = acc[k * 128 + u * 16 : k * 128 + u * 16 + 16, b * 256 : (b + 1) * 256]
                rows = pltpu.roll(rows, (-(u - 1) * 32) % 256, 1) if u != 1 else rows
                if u == 0:
                    rows = jnp.where(lane < 32, 0.0, rows)
                if u == 7:
                    rows = jnp.where(lane >= 64, 0.0, rows)
                total += rows
            for a in range(3):
                at = ((a * 3 + b) * 3 + k) * 16
                grad_deep[at : at + 16, :] = total[:, a * 32 : (a + 1) * 32]

    receive(NC, c, ro_half(0))
    receive(NC, c, ro_half(1))
    total = ro[0].astype(F32)
    for k in range(1, NC):
        total += ro[k].astype(F32)
    rounded = total.astype(BF16).reshape(256, 128)
    deep_out[...] = dot(sel[SWAP0:EYE0], rounded).astype(BF16)

    receive(NC, c, a2_copy)
    total = ar2[0]
    for k in range(1, NC):
        total += ar2[k]
    square = jnp.concatenate([total, jnp.zeros((112, 128), F32)], 0)
    grad_early[...] = square.T[:108, :16].reshape(27, 4, 16)

    for j, piece in enumerate(PIECES):

        @pl.when(exists(piece, 1))
        def _(j=j):
            halo_copy(j).wait_send()

    sent(NC, c, g_copy)
    sent(NC, c, dl_copy)
    across_copy(f).wait_send()
    sum_copy().wait_send()
    for k in range(2):
        each(4, z, lambda to, k=k: z_copy(to, f, k).wait_send())
        each(4, z, lambda to, k=k: rr_copy(2 * to + k).wait_send())

    @pl.loop(0, 8)
    def _(k):
        mate_copy(2 * k + core).wait_send()
        pr_copy(k).wait_send()

    sent(NC, c, ro_half(0))
    sent(NC, c, ro_half(1))
    sent(NC, c, w_copy)
    sent(NF, f, a1_copy)
    sent(NC, c, a2_copy)


SCRATCH = (
    ((192, 256), BF16), ((192, 256), BF16), ((1584, 256), BF16), ((128, 512), BF16),
    ((8, 128, 256), F32), ((4, 64, 256), F32), ((8, 32, 128), BF16), ((18, 8, 32, 128), BF16),
    ((16, 16, 128), BF16), ((16, 8, 16, 128), BF16), ((3, 18, 128, 128), BF16), ((3, 18, 48, 128), BF16),
    ((32, 512), BF16), ((8, 32, 512), BF16), ((3, 128, 768), BF16), ((8, 256, 128), F32), ((8, 256, 128), BF16),
    ((8, 256, 128), BF16), ((8, 256, 128), BF16), ((2, 4, 256, 128), BF16),
    ((8, 16, 16, 128), BF16), ((8, 16, 16, 128), BF16),
    ((4, 128, 256), F32), ((128, 512), F32), ((384, 768), F32), ((16, 16, 128), F32), ((8, 16, 128), F32),
    ((256, 128), BF16), ((256, 128), BF16),
)
SEMAPHORES = (9, 8, 8, 8, 8, 8, 8, 8, 16, 2, 1, 16, 8, 8, 8, 8, 16, 16, 8, 8, 16, 16, 8, 8)
OPERANDS = (
    (256, 256), (27, 4, 16), (432, 32), (256, 128), (END0, 256), (480, 512), (128, 4096), (4096, 128), (96, 2048),
)


def hand_on(*refs):
    given, results, held, sems = refs[:3], refs[3:6], refs[6:9], refs[9]
    into = [pltpu.make_async_copy(given[k], held[k], sems.at[k]) for k in range(3)]
    out = [pltpu.make_async_copy(held[k], results[k], sems.at[3 + k]) for k in range(3)]
    for copy in into:
        copy.start()
    for k in range(3):
        into[k].wait()
        out[k].start()
    for copy in out:
        copy.wait()


def local(volume, early_w, deep_w, d_out):
    operands = [
        volume.reshape(256, 256),
        early_w.transpose(2, 3, 4, 1, 0).reshape(27, 4, 16),
        deep_w.transpose(2, 3, 4, 0, 1).reshape(432, 32),
        d_out.reshape(256, 128),
        *[jnp.asarray(t) for t in tables()],
    ]
    results = pl.pallas_call(
        kernel,
        out_shape=(
            jax.ShapeDtypeStruct((256, 128), BF16),
            jax.ShapeDtypeStruct((432, 32), F32),
            jax.ShapeDtypeStruct((27, 4, 16), F32),
        ),
        in_specs=[pl.BlockSpec(memory_space=pltpu.HBM)] * len(operands),
        out_specs=[pl.BlockSpec(memory_space=pltpu.VMEM)] * 3,
        scratch_shapes=[pltpu.VMEM(shape, BF16) for shape in OPERANDS]
        + [pltpu.VMEM(shape, dtype) for shape, dtype in SCRATCH]
        + [pltpu.SemaphoreType.DMA((count,)) for count in SEMAPHORES],
        compiler_params=pltpu.CompilerParams(
            collective_id=0, has_side_effects=True, vmem_limit_bytes=60 << 20
        ),
        name="cosmo",
    )(*operands)
    deep_out, grad_deep, grad_early = pl.pallas_call(
        hand_on,
        out_shape=[jax.ShapeDtypeStruct(x.shape, x.dtype) for x in results],
        in_specs=[pl.BlockSpec(memory_space=pl.ANY)] * 3,
        out_specs=[pl.BlockSpec(memory_space=pl.ANY)] * 3,
        scratch_shapes=[pltpu.VMEM(x.shape, x.dtype) for x in results]
        + [pltpu.SemaphoreType.DMA((6,))],
        name="results",
    )(*results)
    return (
        deep_out.reshape(16, 1, 16, 128),
        grad_deep.reshape(3, 3, 3, 16, 32).transpose(3, 4, 0, 1, 2),
        grad_early.reshape(3, 3, 3, 4, 16).transpose(4, 3, 0, 1, 2),
    )


def solution(mesh):
    in_specs = (
        P(None, "cin", "flt", None),
        P(),
        P("flt", "cin", None, None, None),
        P("flt", "cin", None, None),
    )
    out_specs = (P("flt", "cin", None, None), P("flt", "cin", None, None, None), P())
    return jax.shard_map(local, mesh=mesh, in_specs=in_specs, out_specs=out_specs, check_vma=False)
```
